128 devices in a mesh: ctx: 4 (over z), ep: 32 (over y, x, core).
Axes of the slice: x: 4, y: 4, z: 4, core: 2. Of those that a mesh axis runs over, the one named last changes fastest.
Arguments:
- prefill_pages: bfloat16 [4, 32, 4, 20, 36864], P('ctx', 'ep'), may hold values from -4.5 to 4.5
- page_map: int32 [4, 32, 4, 20], P('ctx', 'ep'), may hold values from 0 to 79, as said below
- prompt_len: int32 [512], P(('ctx', 'ep')), may hold values from 1 to 1280, 393216 in all
- queries: bfloat16 [2, 512, 73728], P(None, ('ctx', 'ep')), may hold values from -24 to 24
- new_latent: bfloat16 [2, 512, 576], P(None, ('ctx', 'ep')), may hold values from -4 to 4
- resid: bfloat16 [2, 512, 7168], P(None, ('ctx', 'ep')), may hold values from -3 to 3
- w_uv: bfloat16 [128, 512, 128], P('ep'), may hold values from -1 to 1
- w_out: bfloat16 [16384, 7168], P('ep'), may hold values from -0.046875 to 0.046875
- norm_gain: bfloat16 [7168], replicated, may hold values from 0.099609375 to 1.8984375
- router_w: bfloat16 [7168, 32], replicated, may hold values from -0.0625 to 0.0625
- routes: int32 [2, 512, 8], P(None, ('ctx', 'ep')), may hold values from 0 to 31, all different within a row; in each aligned block of 4 rows (0 to 3, 4 to 7, ..., all dimensions but the last counted through in order) at most 2 rows name the same one
- w_gate: bfloat16 [32, 7168, 1024], P('ep', None, 'ctx'), may hold values from -0.0625 to 0.0625
- w_up: bfloat16 [32, 7168, 1024], P('ep', None, 'ctx'), may hold values from -0.0625 to 0.0625
- w_down: bfloat16 [32, 1024, 7168], P('ep', 'ctx'), may hold values from -0.1875 to 0.1875
Outputs:
- layer_out: bfloat16 [2, 512, 7168], P(None, ('ctx', 'ep'))
The draws below stay inside these ranges and needn't reach their ends.
Inputs may be any that keep to these rules, and one draw needn't show every extreme that they name: For each owner ctx index c2 and column e, the values page_map[c2, e, c, s] over all c and s are the numbers 0 to 79, each once, and a value q * 20 + k at producer index c has k % 4 == c. `routes`: the 8 experts of a token differ. In each step the 4 tokens of one device name one expert at most 2 times.
All inputs are finite; a program needn't handle non-finite values. No bound on the sum of `prompt_len` on one device may be relied on, other than what follows from the above.
Results may differ from the reference program's by a relative error of at most 0.023.
Values may be sent and summed in bfloat16 or wider, within the bound.
A program may use at most 128 MiB of HBM per device.

```python
import math
import jax
import jax.numpy as jnp
import numpy as np
from jax import lax

D = 7168
H = 128
LAT = 512
ROPE = 64
NOPE = 128
VH = 128
TOPK = 8
FFE = 1024
PAGE = 64
STEPS = 2
REQ_DEV = 4
MAXP = 20
LATW = 576
EXPERTS = 32
TOKENS = 512
SLOTS = 20
MOST = 2
N_CTX = 4
N_EP = 32


def latent_rows(key):
    return jnp.clip(jax.random.normal(key, (STEPS, TOKENS, LATW), jnp.float32), -3.0, 3.0)


def draw_new_latent(key, part):
    rows = latent_rows(key)
    return rows.astype(jnp.bfloat16)


def draw_queries(key, part):
    key = jax.random.fold_in(key, 37)
    value_key = jax.random.fold_in(key, 2)
    full_shape = (STEPS, TOKENS, H, LATW)
    values = jnp.clip(jax.random.normal(value_key, full_shape, jnp.float32), -4.5, 4.5)
    return values.reshape(STEPS, TOKENS, H * LATW).astype(jnp.bfloat16)


def draw_page_map(key, part):
    key = jax.random.fold_in(key, 11)
    per_source = MAXP // N_CTX
    slot_ids = jnp.arange(SLOTS, dtype=jnp.int32)
    request = slot_ids // per_source
    page_number = slot_ids % per_source
    source = jnp.arange(N_CTX, dtype=jnp.int32)
    targets = request[None, :] * MAXP + page_number[None, :] * N_CTX + source[:, None]
    subkeys = jax.random.split(key, N_CTX * N_EP * N_CTX)
    orders = jax.vmap(lambda one_key: jax.random.permutation(one_key, SLOTS))(subkeys)
    orders = orders.reshape(N_CTX, N_EP, N_CTX, SLOTS)
    spread = jnp.broadcast_to(targets[None, None], (N_CTX, N_EP, N_CTX, SLOTS))
    return jnp.take_along_axis(spread, orders, axis=3).astype(jnp.int32)


def block_levels(stream_key, shape, cuts, low, top_value):
    def one(dim, parts):
        draws = jax.random.uniform(jax.random.fold_in(jax.random.fold_in(stream_key, 6), dim), (parts,), jnp.float32, low / len(cuts), top_value / len(cuts))
        return jnp.repeat(jnp.exp(draws), shape[dim] // parts).reshape((-1,) + (1,) * (len(shape) - dim - 1))

    level = one(*cuts[0])
    for cut in cuts[1:]:
        level = level * one(*cut)
    return level


def length_profile(count, total, most, slope):
    weights = [(1 << 20) // math.isqrt(rank ** slope) + 1 for rank in range(2, count + 1)]
    spare, given = total - most - (count - 1), [1] * (count - 1)
    while spare > 0:
        candidates = [i for i in range(count - 1) if given[i] < most]
        pool, remaining = sum([weights[i] for i in candidates]), spare
        for i in candidates:
            more = min(most - given[i], max(1, remaining * weights[i] // pool), spare)
            given[i] = given[i] + more
            spare = spare - more
    return np.array([most] + given)


def uneven_parts(stream_key, count, total, reach, lean):
    if count == 2:
        one = jax.random.randint(stream_key, (), max(1, total - reach), min(reach, total - 1) + 1)
        return jnp.stack([one, total - one])
    lengths = jnp.asarray(length_profile(count, total, reach, lean), jnp.int32)
    pairs = (count - 1) // 2
    giver, sink = lengths[1:1 + 2 * pairs:2], lengths[2:2 + 2 * pairs:2]
    margin = jnp.minimum(giver - 1, reach - sink)
    passed = jax.random.randint(jax.random.fold_in(stream_key, 1), (pairs,), 0, 1 << 20) % (margin + 1)
    lengths = lengths.at[1:1 + 2 * pairs:2].set(giver - passed).at[2:2 + 2 * pairs:2].set(sink + passed)
    return lengths[jax.random.permutation(jax.random.fold_in(stream_key, 2), count)]


def deal_out(rng, own, number, rows, count, top, most, lean):
    sequence = jax.random.permutation(rng, count)
    crowded, ordinary = portions_of(count, rows * top, most, lean, True), portions_of(count, rows * top, most, lean, False)
    places = jnp.arange(count)

    def named(lengths, turn):
        used = int((lengths > 0).sum())
        fixed = max(1, used // 4)
        passed = fixed + (places - fixed + turn * (used - fixed)) % max(1, count - fixed)
        return jnp.zeros((count,), jnp.int32).at[sequence[jnp.where(places < fixed, places, passed)]].set(jnp.asarray(lengths, jnp.int32))

    lengths = jnp.where(number % 4 == 0, named(crowded, number // 4), named(ordinary, number - number // 4 - 1))
    mixed = jax.random.permutation(jax.random.fold_in(own, 3), count)
    donor, sink = mixed[0:count // 2 * 2:2], mixed[1:count // 2 * 2:2]
    room = jnp.minimum(lengths[donor] - 1, most - lengths[sink]) // 2
    room = jnp.where((donor == sequence[0]) | (sink == sequence[0]) | (lengths[sink] == 0), 0, jnp.maximum(room, 0))
    passed = jax.random.randint(jax.random.fold_in(own, 4), (count // 2,), 0, 1 << 20) % (room + 1)
    lengths = lengths.at[donor].add(-passed).at[sink].add(passed)
    items = jnp.searchsorted(jnp.cumsum(lengths), jnp.arange(rows * top), side="right").astype(jnp.int32)
    grid = items.reshape(top, rows).T
    grid = grid[jax.random.permutation(jax.random.fold_in(own, 1), rows)]
    turn = jax.random.randint(jax.random.fold_in(own, 2), (rows, 1), 0, top)
    return jnp.take_along_axis(grid, (jnp.arange(top)[None, :] + turn) % top, axis=1)


def portions_of(number_of, total, reach, slope, full):
    loads = [(1 << 20) // math.isqrt(grade ** slope) + 1 for grade in range(1, number_of + 1)]
    largest = reach if full else min(reach, max(-(-total // number_of), total * loads[0] // sum(loads)))
    least = 1 if total - largest >= number_of - 1 else 0
    given, rest = [largest] + [least] * (number_of - 1), total - largest - least * (number_of - 1)
    while rest > 0:
        movable = [i for i in range(1, number_of) if given[i] < largest] or [i for i in range(1, number_of) if given[i] < reach]
        mass, budget = sum([loads[i] for i in movable]), rest
        for i in movable:
            extra = min(reach - given[i], max(1, budget * loads[i] // mass), rest)
            given[i] = given[i] + extra
            rest = rest - extra
    return np.array(given)


def normal_values(stream_key, shape, width, limit, shards=(), kind=jnp.bfloat16):
    drawn = jax.random.normal(stream_key, shape, jnp.float32) * width
    if len(shards) > 0:
        drawn = block_levels(stream_key, shape, shards, -0.22, 0.18) * drawn
    return jnp.clip(drawn, min=-limit, max=limit).astype(kind)


def setup_inputs(seed: int = 0) -> dict:
    key_list = jax.random.split(jax.random.key(seed), 15)
    prefill_pages = normal_values(key_list[0], (N_CTX, N_EP, N_CTX, SLOTS, PAGE * LATW), 1.0, 4.5, ((0, 4), (1, 32)))
    page_map = draw_page_map(jax.random.fold_in(key_list[14], 71), 0)
    prompt_len = uneven_parts(key_list[2], TOKENS, TOKENS * MAXP * PAGE * 3 // 5, MAXP * PAGE, 2).astype(jnp.int32)
    queries = draw_queries(jax.random.fold_in(key_list[14], 71), 0)
    new_latent = draw_new_latent(jax.random.fold_in(key_list[14], 71), 0)
    resid = normal_values(key_list[5], (STEPS, TOKENS, D), 0.5, 3.0, ((1, 128),))
    w_uv = normal_values(key_list[6], (H, LAT, VH), (LAT // 16) ** -0.5, 1.0, ((0, 32),))
    w_out = normal_values(key_list[7], (H * VH, D), (H * VH) ** -0.5, 0.046875, ((0, 32),))
    norm_gain = jnp.clip(1.0 + 0.18 * jax.random.normal(key_list[8], (D,), jnp.float32), 0.099609375, 1.8984375).astype(jnp.bfloat16)
    router_w = normal_values(key_list[9], (D, EXPERTS), D ** -0.5, 0.0625)
    routes_keys = jax.random.split(jax.random.fold_in(key_list[10], 1), STEPS * TOKENS // REQ_DEV)
    routes_turns = jax.random.permutation(jax.random.fold_in(key_list[10], 3), STEPS * TOKENS // REQ_DEV)
    routes = jax.vmap(lambda own, number: deal_out(jax.random.fold_in(key_list[10], 2), own, number, REQ_DEV, EXPERTS, TOPK, MOST, 2))(routes_keys, routes_turns).reshape((STEPS, TOKENS, TOPK))
    w_gate = normal_values(key_list[11], (EXPERTS, D, FFE), D ** -0.5, 0.0625, ((0, 32), (2, 4)))
    w_up = normal_values(key_list[12], (EXPERTS, D, FFE), D ** -0.5, 0.0625, ((0, 32), (2, 4)))
    w_down = normal_values(key_list[13], (EXPERTS, FFE, D), FFE ** -0.5, 0.1875, ((0, 32), (1, 4)))
    return {"prefill_pages": prefill_pages, "page_map": page_map, "prompt_len": prompt_len, "queries": queries, "new_latent": new_latent, "resid": resid, "w_uv": w_uv, "w_out": w_out, "norm_gain": norm_gain, "router_w": router_w, "routes": routes, "w_gate": w_gate, "w_up": w_up, "w_down": w_down}


norm_eps = 1e-06
route_scale = 2.5
masked_score = -1e+30

def build_cache(prefill_pages, page_map):
    moved_pages = jnp.transpose(prefill_pages, (2, 1, 0, 3, 4)).reshape(N_CTX, N_EP, N_CTX * SLOTS, PAGE * LATW)
    target_rows = page_map.reshape(N_CTX, N_EP, N_CTX * SLOTS)

    def place(values, positions):
        return jnp.zeros_like(values).at[positions].set(values)
    placed = jax.vmap(jax.vmap(place))(moved_pages, target_rows)
    return placed.reshape(TOKENS, MAXP * PAGE, LATW)

def attend_one(packed):
    key_rows, length, query_rows, fresh_rows = packed
    query_wide = query_rows.reshape(STEPS, H, LATW).astype(jnp.float32)
    key_wide = key_rows.astype(jnp.float32)
    fresh_wide = fresh_rows.astype(jnp.float32)
    score_scale = (NOPE + ROPE) ** (-0.5)
    old_scores = jnp.einsum('shd,ld->shl', query_wide, key_wide) * score_scale
    new_scores = jnp.einsum('shd,jd->shj', query_wide, fresh_wide) * score_scale
    live_keys = jnp.arange(MAXP * PAGE) < length
    old_scores = jnp.where(live_keys[None, None, :], old_scores, masked_score)
    causal = jnp.arange(STEPS)[None, :] <= jnp.arange(STEPS)[:, None]
    new_scores = jnp.where(causal[:, None, :], new_scores, masked_score)
    row_max = jnp.maximum(old_scores.max(-1), new_scores.max(-1))[..., None]
    old_exp = jnp.exp(old_scores - row_max)
    new_exp = jnp.exp(new_scores - row_max)
    row_total = old_exp.sum(-1, keepdims=True) + new_exp.sum(-1, keepdims=True)
    old_weights = lax.optimization_barrier((old_exp / row_total).astype(jnp.bfloat16)).astype(jnp.float32)
    new_weights = lax.optimization_barrier((new_exp / row_total).astype(jnp.bfloat16)).astype(jnp.float32)
    mixed = jnp.einsum('shl,lc->shc', old_weights, key_wide[:, :LAT])
    mixed = mixed + jnp.einsum('shj,jc->shc', new_weights, fresh_wide[:, :LAT])
    return mixed.astype(jnp.bfloat16)

def expert_apply(picked_rows, gate_matrix, up_matrix, down_matrix):
    row_count = picked_rows.shape[0]
    gate_part = jnp.dot(picked_rows, gate_matrix, preferred_element_type=jnp.float32)
    up_part = jnp.dot(picked_rows, up_matrix, preferred_element_type=jnp.float32)
    hidden_units = (jax.nn.silu(gate_part) * up_part).astype(jnp.bfloat16)
    shard_units = hidden_units.reshape(row_count, N_CTX, FFE // N_CTX).astype(jnp.float32)
    shard_down = down_matrix.reshape(N_CTX, FFE // N_CTX, D).astype(jnp.float32)
    pieces = jnp.einsum('ncf,cfd->ncd', shard_units, shard_down).astype(jnp.bfloat16)
    return lax.optimization_barrier(jnp.sum(pieces.astype(jnp.float32), axis=1)).astype(jnp.bfloat16)

def reference(prefill_pages, page_map, prompt_len, queries, new_latent, resid, w_uv, w_out, norm_gain, router_w, routes, w_gate, w_up, w_down):
    page_cache = build_cache(prefill_pages, page_map)
    attn_latent = lax.map(attend_one, (page_cache, prompt_len, jnp.swapaxes(queries, 0, 1), jnp.swapaxes(new_latent, 0, 1)))
    head_out = jnp.einsum('tshc,hcv->tshv', attn_latent.astype(jnp.float32), w_uv.astype(jnp.float32)).astype(jnp.bfloat16)
    projected = jnp.dot(head_out.reshape(TOKENS * STEPS, H * VH), w_out, preferred_element_type=jnp.float32)
    hidden = jnp.swapaxes(resid, 0, 1).astype(jnp.float32).reshape(TOKENS * STEPS, D) + projected
    mean_square = lax.optimization_barrier(jnp.mean(hidden * hidden, axis=-1, keepdims=True))
    normed = (hidden * lax.rsqrt(mean_square + norm_eps) * norm_gain.astype(jnp.float32)).astype(jnp.bfloat16)
    affinity = jax.nn.sigmoid(jnp.dot(normed, router_w, preferred_element_type=jnp.float32))
    flat_routes = jnp.swapaxes(routes, 0, 1).reshape(TOKENS * STEPS, TOPK)
    picked = jnp.take_along_axis(affinity, flat_routes, axis=1)
    gate_weights = route_scale * picked / lax.optimization_barrier(jnp.sum(picked, axis=1, keepdims=True))
    capacity_rows = N_CTX * N_EP * STEPS * MOST

    def one_expert(running, packed):
        gate_matrix, up_matrix, down_matrix, expert_index = packed
        hit_table = flat_routes == expert_index
        member = jnp.any(hit_table, axis=1).astype(jnp.int32)
        weight = lax.optimization_barrier(jnp.sum(jnp.where(hit_table, gate_weights, 0.0), axis=1))
        row_order = jnp.argsort(1 - member, stable=True)[:capacity_rows]
        result = expert_apply(normed[row_order], gate_matrix, up_matrix, down_matrix)
        factor = weight[row_order] * member[row_order].astype(jnp.float32)
        scaled = result.astype(jnp.float32) * factor[:, None]
        return (running.at[row_order].add(scaled), None)
    start = jnp.zeros((TOKENS * STEPS, D), jnp.float32)
    routed, _ = lax.scan(one_expert, start, (w_gate, w_up, w_down, jnp.arange(EXPERTS, dtype=jnp.int32)))
    layer_out = (hidden + routed).astype(jnp.bfloat16).reshape(TOKENS, STEPS, D)
    return jnp.swapaxes(layer_out, 0, 1)
```

```python
import jax
import jax.numpy as jnp
from jax import lax
from jax.experimental import pallas as pl
from jax.experimental.pallas import tpu as pltpu
from jax.sharding import PartitionSpec as P

LAT = 512
ROPE = 64
NOPE = 128
LATW = 576


norm_eps = 1e-06
route_scale = 2.5
masked_score = -1e30

HALF = 3584
GW = HALF + 128
MESH_IDS = pl.DeviceIdType.MESH
AG_PARTS = ((0, 640, 640), (1280, 640, 640), (2560, 640, 512))
RS_PARTS = ((0, 640, 512), (1152, 640, 512), (2304, 640, 640))
PLANE_PARTS = ((0, 896, 896), (1792, 896, 896))
COPIES = 160


class Links:
    def __init__(self, send_sem, recv_sem):
        self.send_sem, self.recv_sem, self.used = send_sem, recv_sem, 0
        self.z, ep = lax.axis_index("ctx"), lax.axis_index("ep")
        self.core = lax.rem(ep, 2)
        self.y, self.x = ep // 8, lax.rem(ep // 2, 4)
        self.ep = ep
        self.coords = (self.z, self.y, self.x)

    def shifted(self, axis, step):
        return lax.rem(self.coords[axis] + (step % 4), 4)

    def neighbour(self, axis, step):
        c = list(self.coords)
        c[axis] = self.shifted(axis, step)
        return (c[0], (c[1] * 4 + c[2]) * 2 + self.core)

    def partner(self):
        return (self.z, self.ep + 1 - 2 * self.core)

    def send(self, src, dst, device, landing):
        k = self.used
        self.used += 1
        make = lambda s, d: pltpu.make_async_remote_copy(
            src_ref=s,
            dst_ref=d,
            send_sem=self.send_sem.at[k],
            recv_sem=self.recv_sem.at[k],
            device_id=device,
            device_id_type=MESH_IDS,
        )
        out = make(src, dst)
        out.start()
        return out, make(landing, landing)


def wait_in(copies):
    for _, incoming in copies:
        incoming.wait_recv()


def wait_out(copies):
    for outgoing, _ in copies:
        outgoing.wait_send()


def pick(ref, chosen, start, width):
    index = tuple(chosen.get(a, slice(None)) for a in range(len(ref.shape) - 2))
    return ref.at[index + (slice(None), pl.ds(start, width))]


def gather_blocks(link, held, pushed):
    sent, pushes = [], []

    def push(part, axis, coord):
        start, wa, wb = AG_PARTS[part]
        src = pick(held, {axis: coord}, start, wa + wb)
        dst = pick(pushed, {axis: coord}, start, wa + wb)
        pushes.append(link.send(src, dst, link.partner(), dst))

    for stage in range(3):
        first = []
        for p, (start, wa, wb) in enumerate(AG_PARTS):
            order = [(p + j) % 3 for j in range(3)]
            axis = order[stage]
            rest = {a: link.coords[a] for a in order[stage + 1 :]}
            mine = pick(held, {**rest, axis: link.coords[axis]}, start, wa + wb)
            below = pick(held, {**rest, axis: link.shifted(axis, -1)}, start, wa + wb)
            above = pick(held, {**rest, axis: link.shifted(axis, 1)}, start, wa + wb)
            first.append(
                (
                    link.send(mine, mine, link.neighbour(axis, 1), below),
                    link.send(mine, mine, link.neighbour(axis, -1), above),
                )
            )
            if stage == 2:
                push(p, axis, link.coords[axis])
        second = []
        for p, (start, wa, wb) in enumerate(AG_PARTS):
            order = [(p + j) % 3 for j in range(3)]
            axis = order[stage]
            rest = {a: link.coords[a] for a in order[stage + 1 :]}
            wait_in(first[p])
            up = pick(held, {**rest, axis: link.shifted(axis, -1)}, start, wa)
            down = pick(held, {**rest, axis: link.shifted(axis, 1)}, start + wa, wb)
            far_a = pick(held, {**rest, axis: link.shifted(axis, 2)}, start, wa)
            far_b = pick(held, {**rest, axis: link.shifted(axis, 2)}, start + wa, wb)
            second.append(
                (
                    link.send(up, up, link.neighbour(axis, 1), far_a),
                    link.send(down, down, link.neighbour(axis, -1), far_b),
                )
            )
            if stage == 2:
                push(p, axis, link.shifted(axis, -1))
                push(p, axis, link.shifted(axis, 1))
        for p in range(3):
            wait_in(second[p])
            if stage == 2:
                push(p, (p + 2) % 3, link.shifted((p + 2) % 3, 2))
            sent += list(first[p]) + list(second[p])
    return sent, pushes


def scatter_sums(link, parts, axes, sums, landings, last):
    sent = []
    count = len(axes)
    for stage in range(count):
        far_in, low_in, high_in = landings[stage]
        steps = []
        for p, (start, wa, wb) in enumerate(parts):
            order = [axes[(p + j) % count] for j in range(count)]
            axis = order[stage]
            done = {a: link.coords[a] for a in order[:stage]}
            at = lambda coord, lo, w, done=done, axis=axis: pick(
                sums, {k - axes[0]: v for k, v in {**done, axis: coord}.items()}, lo, w
            )
            land = lambda ref, lo, w: ref.at[(slice(None),) * (count - stage) + (pl.ds(lo, w),)]
            far = link.shifted(axis, 2)
            la, lb = land(far_in, start, wa), land(far_in, start + wa, wb)
            steps.append(
                (
                    at,
                    land,
                    axis,
                    (
                        link.send(at(far, start, wa), la, link.neighbour(axis, 1), la),
                        link.send(at(far, start + wa, wb), lb, link.neighbour(axis, -1), lb),
                    ),
                )
            )
        final = []
        for p, (start, wa, wb) in enumerate(parts):
            at, land, axis, first = steps[p]
            wait_in(first)
            up, down = link.shifted(axis, 1), link.shifted(axis, -1)
            for coord, lo, w in ((up, start, wa), (down, start + wa, wb)):
                view, got = at(coord, lo, w), land(far_in, lo, w)
                view[...] = (
                    view[...].astype(jnp.float32) + got[...].astype(jnp.float32)
                ).astype(jnp.bfloat16)
            low, high = land(low_in, start, wa + wb), land(high_in, start, wa + wb)
            second = (
                link.send(at(up, start, wa + wb), low, link.neighbour(axis, 1), low),
                link.send(at(down, start, wa + wb), high, link.neighbour(axis, -1), high),
            )
            final.append((at(link.coords[axis], start, wa + wb), low, high, second))
            sent += list(first) + list(second)
        for p, (start, wa, wb) in enumerate(parts):
            view, low, high, second = final[p]
            wait_in(second)
            total = (
                view[...].astype(jnp.float32)
                + low[...].astype(jnp.float32)
                + high[...].astype(jnp.float32)
            )
            if stage == count - 1:
                last(start, wa + wb, total)
            else:
                view[...] = total.astype(jnp.bfloat16)
    return sent


def layer_kernel(
    heads_ref,
    w_uv_ref,
    resid_ref,
    chosen_ref,
    gain_ref,
    router_ref,
    w_out_hbm,
    w_gate_hbm,
    w_up_hbm,
    w_down_hbm,
    out_ref,
    big,
    wg,
    wu,
    wd,
    flat,
    part_send,
    part_land,
    part_sum,
    plane_a0,
    plane_a1,
    plane_b0,
    plane_b1,
    plane_c0,
    plane_c1,
    hid,
    picked,
    stat_out,
    stat_in,
    held,
    pushed,
    gate_acc,
    up_acc,
    units,
    far0,
    low0,
    high0,
    far1,
    low1,
    high1,
    far2,
    low2,
    high2,
    fin,
    fin_in,
    send_sem,
    recv_sem,
    load_sem,
):
    link = Links(send_sem, recv_sem)
    core = link.core
    other = 1 - core
    partner = link.partner()
    f32, bf16 = jnp.float32, jnp.bfloat16

    own_cols = pl.ds(pl.multiple_of(core * HALF, 128), HALF)
    other_cols = pl.ds(pl.multiple_of(other * HALF, 128), HALF)
    loads = []

    def load(src, dst):
        copy = pltpu.make_async_copy(src, dst, load_sem.at[len(loads)])
        copy.start()
        loads.append(copy)

    load(w_out_hbm.at[:, :, :, :, other_cols], big.at[pl.ds(2, 2)])
    load(w_out_hbm.at[:, :, :, :, own_cols], big.at[pl.ds(0, 2)])
    for slot, cols in ((0, own_cols), (1, other_cols)):
        load(w_gate_hbm.at[cols], wg.at[slot])
        load(w_up_hbm.at[cols], wu.at[slot])
        load(w_down_hbm.at[:, cols], wd.at[slot])

    barrier = pltpu.get_barrier_semaphore()
    for axis in range(3):
        for step in (1, -1):
            pl.semaphore_signal(
                barrier, inc=1, device_id=link.neighbour(axis, step), device_id_type=MESH_IDS
            )
    pl.semaphore_signal(barrier, inc=1, device_id=partner, device_id_type=MESH_IDS)
    pl.semaphore_wait(barrier, 7)

    sent = []
    swaps = [
        link.send(resid_ref.at[other], hid.at[core], partner, hid.at[other]),
        link.send(chosen_ref, picked.at[core], partner, picked.at[other]),
    ]
    sent += swaps

    for pair in range(2):
        rows = heads_ref[:, pl.ds(pair * 16, 16), :].reshape(512, LAT)
        for one in range(2):
            head = 2 * pair + one
            value = jnp.dot(rows, w_uv_ref[head], preferred_element_type=f32)
            value = value.reshape(32, 2, 8, 128)[:, one].reshape(256, 128)
            flat[:, pl.ds(head * 128, 128)] = value.astype(bf16)

    def project(slot, start):
        lanes = pl.ds(start, 256)
        weight = big[pl.ds(2 * slot, 2), :, :, :, lanes].reshape(512, 256)
        value = jnp.dot(flat[...], weight, preferred_element_type=f32)
        return value.reshape(4, 4, 16, 256)

    loads[0].wait()
    core_swap = []
    for start in (0, 1792):

        @pl.loop(0, 7)
        def _(j, start=start):
            at = pl.multiple_of(start + j * 256, 256)
            part_send[:, :, :, pl.ds(at, 256)] = project(1, at).astype(bf16)

        lanes = pl.ds(start, 1792)
        dst = part_land.at[:, :, :, lanes]
        core_swap.append(link.send(part_send.at[:, :, :, lanes], dst, partner, dst))
    sent += core_swap
    loads[1].wait()
    for turn, start in enumerate((0, 1792)):
        wait_in(core_swap[turn : turn + 1])

        @pl.loop(0, 7)
        def _(j, start=start):
            at = pl.multiple_of(start + j * 256, 256)
            value = project(0, at) + part_land[:, :, :, pl.ds(at, 256)].astype(f32)
            part_sum[:, :, :, pl.ds(at, 256)] = value.astype(bf16)

    hid[core] = resid_ref[core]
    picked[core] = chosen_ref[...]
    wait_in(swaps)

    def add_hidden(start, width, total):
        lanes = pl.ds(start, width)
        hid[:, :, lanes] = hid[:, :, lanes] + total.reshape(2, 8, width)

    sent += scatter_sums(
        link,
        PLANE_PARTS,
        (1, 2),
        part_sum,
        ((plane_a0, plane_b0, plane_c0), (plane_a1, plane_b1, plane_c1)),
        add_hidden,
    )

    hidden = hid[...].reshape(16, HALF)
    gain = gain_ref[core]
    logits = jnp.dot(
        (hidden * gain).astype(bf16), router_ref[core], preferred_element_type=f32
    )
    squares = jnp.sum(hidden * hidden, axis=1, keepdims=True)
    lane = lax.broadcasted_iota(jnp.int32, (16, 128), 1)
    mine = jnp.where(lane < 64, logits, jnp.broadcast_to(squares, (16, 128)))
    stat_out[...] = mine
    stat = link.send(stat_out, stat_in, partner, stat_in)
    sent.append(stat)
    wait_in([stat])
    both = mine + stat_in[...]
    scale = lax.rsqrt(both[:, 64:65] / (2 * HALF) + norm_eps)
    affinity = jax.nn.sigmoid(both * scale) * picked[...].reshape(16, 128)
    weights = route_scale * affinity / jnp.sum(affinity, axis=1, keepdims=True)
    high = weights.astype(bf16)
    low = (weights - high.astype(f32)).astype(bf16).astype(f32)
    table = high.astype(f32) + pltpu.roll(low, 32, axis=1)
    normed = (hid[...].reshape(16, HALF) * scale * gain).astype(bf16)
    held[link.z, link.y, link.x, :, pl.ds(0, HALF)] = normed
    held[link.z, link.y, link.x, :, pl.ds(HALF, 128)] = table.astype(bf16)

    gathers, pushes = gather_blocks(link, held, pushed)

    for copy in loads[2:]:
        copy.wait()

    def own_half(i, carry):
        rows = held[i, :, :, :, pl.ds(0, HALF)].reshape(256, HALF)
        gate_acc[i] = jnp.dot(rows, wg[0], preferred_element_type=f32)
        up_acc[i] = jnp.dot(rows, wu[0], preferred_element_type=f32)
        return carry

    lax.fori_loop(0, 4, own_half, 0)
    wait_in(pushes)

    def other_half(i, carry):
        rows = pushed[i, :, :, :, pl.ds(0, HALF)].reshape(256, HALF)
        gate_part = gate_acc[i] + jnp.dot(rows, wg[1], preferred_element_type=f32)
        up_part = up_acc[i] + jnp.dot(rows, wu[1], preferred_element_type=f32)
        table = held[i, :, :, :, pl.ds(HALF, 128)].reshape(256, 128).astype(f32)
        lane = lax.broadcasted_iota(jnp.int32, (256, 128), 1)
        here = (lane == link.ep) | (lane == link.ep + 32)
        factor = jnp.sum(jnp.where(here, table, 0.0), axis=1, keepdims=True)
        units[i] = (jax.nn.silu(gate_part) * up_part * factor).astype(bf16)
        return carry

    lax.fori_loop(0, 4, other_half, 0)
    wait_out(gathers + pushes)

    back = []
    for i in range(4):

        @pl.loop(0, 7)
        def _(j, i=i):
            lanes = pl.ds(pl.multiple_of(j * 512, 512), 512)
            value = jnp.dot(units[i], wd[1, :, lanes], preferred_element_type=f32)
            pushed[i, :, :, :, lanes] = value.astype(bf16).reshape(4, 4, 16, 512)

        dst = big.at[i]
        back.append(link.send(pushed.at[i, :, :, :, pl.ds(0, HALF)], dst, partner, dst))
    for i in range(4):
        wait_in(back[i : i + 1])

        @pl.loop(0, 7)
        def _(j, i=i):
            lanes = pl.ds(pl.multiple_of(j * 512, 512), 512)
            value = jnp.dot(units[i], wd[0, :, lanes], preferred_element_type=f32)
            value = value.reshape(4, 4, 16, 512) + big[i, :, :, :, lanes].astype(f32)
            held[i, :, :, :, lanes] = value.astype(bf16)

    sent += back

    def add_routed(start, width, total):
        lanes = pl.ds(start, width)
        fin[:, :, lanes] = hid[:, :, lanes] + total.reshape(2, 8, width)

    sent += scatter_sums(
        link,
        RS_PARTS,
        (0, 1, 2),
        held,
        ((far0, low0, high0), (far1, low1, high1), (far2, low2, high2)),
        add_routed,
    )
    swap = link.send(fin.at[other], fin_in, partner, fin_in)
    sent.append(swap)
    out_ref[core] = fin[core]
    wait_in([swap])
    out_ref[other] = fin_in[...]
    wait_out(sent)


def layer_call(head_rows, w_uv, resid_halves, chosen, gain, router, w_out, w_gate, w_up, w_down):
    vmem, hbm = pl.BlockSpec(memory_space=pltpu.VMEM), pl.BlockSpec(memory_space=pl.ANY)
    bf16, f32 = jnp.bfloat16, jnp.float32

    def block(*lead, lanes=HALF, kind=bf16):
        return pltpu.VMEM(lead + (lanes,), kind)

    plane = [block(4, 16), block(16)] * 3
    torus = [block(4, 4, 16)] * 3 + [block(4, 16)] * 3 + [block(16)] * 3
    scratch = (
        [block(4, 4, 4, 16)]
        + [pltpu.VMEM((2, HALF, 256), bf16)] * 2
        + [pltpu.VMEM((2, 256, HALF), bf16), pltpu.VMEM((256, 512), bf16)]
        + [block(4, 4, 16)] * 3
        + plane
        + [block(2, 8, kind=f32), pltpu.VMEM((2, 8, 128), f32)]
        + [pltpu.VMEM((16, 128), f32)] * 2
        + [block(4, 4, 4, 16, lanes=GW)] * 2
        + [pltpu.VMEM((4, 256, 256), f32)] * 2
        + [pltpu.VMEM((4, 256, 256), bf16)]
        + torus
        + [block(2, 8, kind=f32), block(8, kind=f32)]
        + [pltpu.SemaphoreType.DMA((COPIES,))] * 2
        + [pltpu.SemaphoreType.DMA((8,))]
    )
    return pl.pallas_call(
        layer_kernel,
        out_shape=jax.ShapeDtypeStruct((2, 8, HALF), f32),
        in_specs=[vmem] * 6 + [hbm] * 4,
        out_specs=vmem,
        scratch_shapes=scratch,
        compiler_params=pltpu.CompilerParams(
            collective_id=1, has_side_effects=True, vmem_limit_bytes=62 * 1024 * 1024
        ),
        cost_estimate=pl.CostEstimate(
            flops=20_000_000_000, bytes_accessed=22_000_000, transcendentals=300_000
        ),
        name="layer",
    )(head_rows, w_uv, resid_halves, chosen, gain, router, w_out, w_gate, w_up, w_down)


def layer_operands(resid, routes, w_out, norm_gain, router_w, w_gate, w_up, w_down):
    resid_halves = jnp.swapaxes(resid.reshape(8, 2, HALF), 0, 1).astype(jnp.float32)
    route_rows = routes.reshape(8, -1)
    chosen = jnp.any(route_rows[..., None] == jnp.arange(128), axis=1).astype(jnp.float32)
    gain = norm_gain.astype(jnp.float32).reshape(2, 1, HALF)
    router = jnp.pad(router_w, ((0, 0), (0, 128 - router_w.shape[1]))).reshape(2, HALF, 128)
    return (
        resid_halves,
        chosen,
        gain,
        router,
        w_out.reshape(2, 4, 4, 16, 2 * HALF),
        w_gate[0],
        w_up[0],
        w_down[0],
    )


def per_device(
    prefill_pages,
    page_map,
    prompt_len,
    queries,
    new_latent,
    resid,
    w_uv,
    w_out,
    norm_gain,
    router_w,
    routes,
    w_gate,
    w_up,
    w_down,
):
    received = lax.all_to_all(prefill_pages, "ctx", split_axis=2, concat_axis=0, tiled=True)
    page_width = received.shape[-1]
    stacked = received.reshape(-1, page_width)
    targets = page_map.reshape(-1)
    requests = prompt_len.shape[0]
    placed = jnp.zeros_like(stacked).at[targets].set(stacked)
    page_cache = placed.reshape(requests, -1, LATW)
    key_count = page_cache.shape[1]
    steps_count = queries.shape[0]
    query_rows = queries.reshape(steps_count, requests, -1, LATW)
    score_scale = (NOPE + ROPE) ** (-0.5)
    old_scores = (
        jnp.einsum("sqhd,qld->qshl", query_rows, page_cache, preferred_element_type=jnp.float32)
        * score_scale
    )
    new_scores = (
        jnp.einsum("sqhd,jqd->qshj", query_rows, new_latent, preferred_element_type=jnp.float32)
        * score_scale
    )
    live_keys = jnp.arange(key_count)[None, :] < prompt_len[:, None]
    old_scores = jnp.where(live_keys[:, None, None, :], old_scores, masked_score)
    causal = jnp.arange(steps_count)[None, :] <= jnp.arange(steps_count)[:, None]
    new_scores = jnp.where(causal[None, :, None, :], new_scores, masked_score)
    row_max = jnp.maximum(old_scores.max(-1), new_scores.max(-1))[..., None]
    old_exp = jnp.exp(old_scores - row_max)
    new_exp = jnp.exp(new_scores - row_max)
    row_total = old_exp.sum(-1, keepdims=True) + new_exp.sum(-1, keepdims=True)
    old_weights = (old_exp / row_total).astype(jnp.bfloat16)
    new_weights = (new_exp / row_total).astype(jnp.bfloat16)
    mixed = jnp.einsum(
        "qshl,qlc->qshc", old_weights, page_cache[:, :, :LAT], preferred_element_type=jnp.float32
    )
    mixed = mixed + jnp.einsum(
        "qshj,jqc->qshc", new_weights, new_latent[:, :, :LAT], preferred_element_type=jnp.float32
    )
    attn_latent = mixed.astype(jnp.bfloat16)
    by_target = attn_latent.reshape(requests, steps_count, 32, 4, LAT)
    by_target = jnp.transpose(by_target, (2, 3, 1, 0, 4)).reshape(32, 32, LAT)
    head_rows = lax.all_to_all(by_target, "ep", split_axis=0, concat_axis=0, tiled=True)
    operands = layer_operands(resid, routes, w_out, norm_gain, router_w, w_gate, w_up, w_down)
    halves = layer_call(head_rows, w_uv, *operands)
    rows = jnp.swapaxes(halves, 0, 1).astype(jnp.bfloat16)
    return rows.reshape(steps_count, requests, 2 * HALF)


def solution(mesh):
    placed = (
        P("ctx", "ep", None, None, None),
        P("ctx", "ep", None, None),
        P(("ctx", "ep")),
        P(None, ("ctx", "ep"), None),
        P(None, ("ctx", "ep"), None),
        P(None, ("ctx", "ep"), None),
        P("ep", None, None),
        P("ep", None),
        P(),
        P(),
        P(None, ("ctx", "ep"), None),
        P("ep", None, "ctx"),
        P("ep", None, "ctx"),
        P("ep", "ctx", None),
    )
    return jax.shard_map(
        per_device,
        mesh=mesh,
        in_specs=placed,
        out_specs=P(None, ("ctx", "ep"), None),
        check_vma=False,
    )
```

```python
import jax
import jax.numpy as jnp
from jax import lax
from jax.experimental import pallas as pl
from jax.experimental.pallas import tpu as pltpu
from jax.sharding import PartitionSpec as P

LAT = 512
ROPE = 64
NOPE = 128
LATW = 576


norm_eps = 1e-06
route_scale = 2.5
masked_score = -1e30

HALF = 3584
GW = HALF + 128
MESH_IDS = pl.DeviceIdType.MESH
AG_PARTS = ((0, 640, 640), (1280, 640, 640), (2560, 640, 512))
RS_PARTS = ((0, 640, 512), (1152, 640, 512), (2304, 640, 640))
PLANE_PARTS = ((0, 896, 896), (1792, 896, 896))
COPIES = 160


class Links:
    def __init__(self, send_sem, recv_sem):
        self.send_sem, self.recv_sem, self.used = send_sem, recv_sem, 0
        self.z, ep = lax.axis_index("ctx"), lax.axis_index("ep")
        self.core = lax.rem(ep, 2)
        self.y, self.x = ep // 8, lax.rem(ep // 2, 4)
        self.ep = ep
        self.coords = (self.z, self.y, self.x)

    def shifted(self, axis, step):
        return lax.rem(self.coords[axis] + (step % 4), 4)

    def neighbour(self, axis, step):
        c = list(self.coords)
        c[axis] = self.shifted(axis, step)
        return (c[0], (c[1] * 4 + c[2]) * 2 + self.core)

    def partner(self):
        return (self.z, self.ep + 1 - 2 * self.core)

    def send(self, src, dst, device, landing):
        k = self.used
        self.used += 1
        make = lambda s, d: pltpu.make_async_remote_copy(
            src_ref=s,
            dst_ref=d,
            send_sem=self.send_sem.at[k],
            recv_sem=self.recv_sem.at[k],
            device_id=device,
            device_id_type=MESH_IDS,
        )
        out = make(src, dst)
        out.start()
        return out, make(landing, landing)


def wait_in(copies):
    for _, incoming in copies:
        incoming.wait_recv()


def wait_out(copies):
    for outgoing, _ in copies:
        outgoing.wait_send()


def pick(ref, chosen, start, width):
    index = tuple(chosen.get(a, slice(None)) for a in range(len(ref.shape) - 2))
    return ref.at[index + (slice(None), pl.ds(start, width))]


def gather_blocks(link, held, pushed):
    sent, pushes = [], []

    def push(part, axis, coord):
        start, wa, wb = AG_PARTS[part]
        src = pick(held, {axis: coord}, start, wa + wb)
        dst = pick(pushed, {axis: coord}, start, wa + wb)
        pushes.append(link.send(src, dst, link.partner(), dst))

    for stage in range(3):
        first = []
        for p, (start, wa, wb) in enumerate(AG_PARTS):
            order = [(p + j) % 3 for j in range(3)]
            axis = order[stage]
            rest = {a: link.coords[a] for a in order[stage + 1 :]}
            mine = pick(held, {**rest, axis: link.coords[axis]}, start, wa + wb)
            below = pick(held, {**rest, axis: link.shifted(axis, -1)}, start, wa + wb)
            above = pick(held, {**rest, axis: link.shifted(axis, 1)}, start, wa + wb)
            first.append(
                (
                    link.send(mine, mine, link.neighbour(axis, 1), below),
                    link.send(mine, mine, link.neighbour(axis, -1), above),
                )
            )
            if stage == 2:
                push(p, axis, link.coords[axis])
        second = []
        for p, (start, wa, wb) in enumerate(AG_PARTS):
            order = [(p + j) % 3 for j in range(3)]
            axis = order[stage]
            rest = {a: link.coords[a] for a in order[stage + 1 :]}
            wait_in(first[p])
            up = pick(held, {**rest, axis: link.shifted(axis, -1)}, start, wa)
            down = pick(held, {**rest, axis: link.shifted(axis, 1)}, start + wa, wb)
            far_a = pick(held, {**rest, axis: link.shifted(axis, 2)}, start, wa)
            far_b = pick(held, {**rest, axis: link.shifted(axis, 2)}, start + wa, wb)
            second.append(
                (
                    link.send(up, up, link.neighbour(axis, 1), far_a),
                    link.send(down, down, link.neighbour(axis, -1), far_b),
                )
            )
            if stage == 2:
                push(p, axis, link.shifted(axis, -1))
                push(p, axis, link.shifted(axis, 1))
        for p in range(3):
            wait_in(second[p])
            if stage == 2:
                push(p, (p + 2) % 3, link.shifted((p + 2) % 3, 2))
            sent += list(first[p]) + list(second[p])
    return sent, pushes


def scatter_sums(link, parts, axes, sums, landings, last):
    sent = []
    count = len(axes)
    for stage in range(count):
        far_in, low_in, high_in = landings[stage]
        steps = []
        for p, (start, wa, wb) in enumerate(parts):
            order = [axes[(p + j) % count] for j in range(count)]
            axis = order[stage]
            done = {a: link.coords[a] for a in order[:stage]}
            at = lambda coord, lo, w, done=done, axis=axis: pick(
                sums, {k - axes[0]: v for k, v in {**done, axis: coord}.items()}, lo, w
            )
            land = lambda ref, lo, w: ref.at[(slice(None),) * (count - stage) + (pl.ds(lo, w),)]
            far = link.shifted(axis, 2)
            la, lb = land(far_in, start, wa), land(far_in, start + wa, wb)
            steps.append(
                (
                    at,
                    land,
                    axis,
                    (
                        link.send(at(far, start, wa), la, link.neighbour(axis, 1), la),
                        link.send(at(far, start + wa, wb), lb, link.neighbour(axis, -1), lb),
                    ),
                )
            )
        final = []
        for p, (start, wa, wb) in enumerate(parts):
            at, land, axis, first = steps[p]
            wait_in(first)
            up, down = link.shifted(axis, 1), link.shifted(axis, -1)
            for coord, lo, w in ((up, start, wa), (down, start + wa, wb)):
                view, got = at(coord, lo, w), land(far_in, lo, w)
                view[...] = (
                    view[...].astype(jnp.float32) + got[...].astype(jnp.float32)
                ).astype(jnp.bfloat16)
            low, high = land(low_in, start, wa + wb), land(high_in, start, wa + wb)
            second = (
                link.send(at(up, start, wa + wb), low, link.neighbour(axis, 1), low),
                link.send(at(down, start, wa + wb), high, link.neighbour(axis, -1), high),
            )
            final.append((at(link.coords[axis], start, wa + wb), low, high, second))
            sent += list(first) + list(second)
        for p, (start, wa, wb) in enumerate(parts):
            view, low, high, second = final[p]
            wait_in(second)
            total = (
                view[...].astype(jnp.float32)
                + low[...].astype(jnp.float32)
                + high[...].astype(jnp.float32)
            )
            if stage == count - 1:
                last(start, wa + wb, total)
            else:
                view[...] = total.astype(jnp.bfloat16)
    return sent


def layer_kernel(
    heads_ref,
    w_uv_ref,
    resid_ref,
    chosen_ref,
    gain_ref,
    router_ref,
    w_out_hbm,
    w_gate_hbm,
    w_up_hbm,
    w_down_hbm,
    out_ref,
    big,
    wg,
    wu,
    wd,
    flat,
    part_send,
    part_land,
    part_sum,
    plane_a0,
    plane_a1,
    plane_b0,
    plane_b1,
    plane_c0,
    plane_c1,
    hid,
    picked,
    stat_out,
    stat_in,
    held,
    pushed,
    gate_acc,
    up_acc,
    units,
    far0,
    low0,
    high0,
    far1,
    low1,
    high1,
    far2,
    low2,
    high2,
    fin,
    fin_in,
    send_sem,
    recv_sem,
    load_sem,
):
    link = Links(send_sem, recv_sem)
    core = link.core
    other = 1 - core
    partner = link.partner()
    f32, bf16 = jnp.float32, jnp.bfloat16

    own_cols = pl.ds(pl.multiple_of(core * HALF, 128), HALF)
    other_cols = pl.ds(pl.multiple_of(other * HALF, 128), HALF)
    loads = []

    def load(src, dst):
        copy = pltpu.make_async_copy(src, dst, load_sem.at[len(loads)])
        copy.start()
        loads.append(copy)

    load(w_out_hbm.at[:, :, :, :, other_cols], big.at[pl.ds(2, 2)])
    load(w_out_hbm.at[:, :, :, :, own_cols], big.at[pl.ds(0, 2)])
    for slot, cols in ((0, own_cols), (1, other_cols)):
        load(w_gate_hbm.at[cols], wg.at[slot])
        load(w_up_hbm.at[cols], wu.at[slot])
        load(w_down_hbm.at[:, cols], wd.at[slot])

    barrier = pltpu.get_barrier_semaphore()
    for axis in range(3):
        for step in (1, -1):
            pl.semaphore_signal(
                barrier, inc=1, device_id=link.neighbour(axis, step), device_id_type=MESH_IDS
            )
    pl.semaphore_signal(barrier, inc=1, device_id=partner, device_id_type=MESH_IDS)
    pl.semaphore_wait(barrier, 7)

    sent = []
    swaps = [
        link.send(resid_ref.at[other], hid.at[core], partner, hid.at[other]),
        link.send(chosen_ref, picked.at[core], partner, picked.at[other]),
    ]
    sent += swaps

    for pair in range(2):
        rows = heads_ref[:, pl.ds(pair * 16, 16), :].reshape(512, LAT)
        for one in range(2):
            head = 2 * pair + one
            value = jnp.dot(rows, w_uv_ref[head], preferred_element_type=f32)
            value = value.reshape(32, 2, 8, 128)[:, one].reshape(256, 128)
            flat[:, pl.ds(head * 128, 128)] = value.astype(bf16)

    def project(slot, start):
        lanes = pl.ds(start, 256)
        weight = big[pl.ds(2 * slot, 2), :, :, :, lanes].reshape(512, 256)
        value = jnp.dot(flat[...], weight, preferred_element_type=f32)
        return value.reshape(4, 4, 16, 256)

    loads[0].wait()
    core_swap = []
    for start in (0, 1792):

        @pl.loop(0, 7)
        def _(j, start=start):
            at = pl.multiple_of(start + j * 256, 256)
            part_send[:, :, :, pl.ds(at, 256)] = project(1, at).astype(bf16)

        lanes = pl.ds(start, 1792)
        dst = part_land.at[:, :, :, lanes]
        core_swap.append(link.send(part_send.at[:, :, :, lanes], dst, partner, dst))
    sent += core_swap
    loads[1].wait()
    for turn, start in enumerate((0, 1792)):
        wait_in(core_swap[turn : turn + 1])

        @pl.loop(0, 7)
        def _(j, start=start):
            at = pl.multiple_of(start + j * 256, 256)
            value = project(0, at) + part_land[:, :, :, pl.ds(at, 256)].astype(f32)
            part_sum[:, :, :, pl.ds(at, 256)] = value.astype(bf16)

    hid[core] = resid_ref[core]
    picked[core] = chosen_ref[...]
    wait_in(swaps)

    def add_hidden(start, width, total):
        lanes = pl.ds(start, width)
        hid[:, :, lanes] = hid[:, :, lanes] + total.reshape(2, 8, width)

    sent += scatter_sums(
        link,
        PLANE_PARTS,
        (1, 2),
        part_sum,
        ((plane_a0, plane_b0, plane_c0), (plane_a1, plane_b1, plane_c1)),
        add_hidden,
    )

    hidden = hid[...].reshape(16, HALF)
    gain = gain_ref[core]
    logits = jnp.dot(
        (hidden * gain).astype(bf16), router_ref[core], preferred_element_type=f32
    )
    squares = jnp.sum(hidden * hidden, axis=1, keepdims=True)
    lane = lax.broadcasted_iota(jnp.int32, (16, 128), 1)
    mine = jnp.where(lane < 64, logits, jnp.broadcast_to(squares, (16, 128)))
    stat_out[...] = mine
    stat = link.send(stat_out, stat_in, partner, stat_in)
    sent.append(stat)
    wait_in([stat])
    both = mine + stat_in[...]
    scale = lax.rsqrt(both[:, 64:65] / (2 * HALF) + norm_eps)
    affinity = jax.nn.sigmoid(both * scale) * picked[...].reshape(16, 128)
    weights = route_scale * affinity / jnp.sum(affinity, axis=1, keepdims=True)
    high = weights.astype(bf16)
    low = (weights - high.astype(f32)).astype(bf16).astype(f32)
    table = high.astype(f32) + pltpu.roll(low, 32, axis=1)
    normed = (hid[...].reshape(16, HALF) * scale * gain).astype(bf16)
    held[link.z, link.y, link.x, :, pl.ds(0, HALF)] = normed
    held[link.z, link.y, link.x, :, pl.ds(HALF, 128)] = table.astype(bf16)

    gathers, pushes = gather_blocks(link, held, pushed)

    for copy in loads[2:]:
        copy.wait()

    def own_half(i, carry):
        rows = held[i, :, :, :, pl.ds(0, HALF)].reshape(256, HALF)
        gate_acc[i] = jnp.dot(rows, wg[0], preferred_element_type=f32)
        up_acc[i] = jnp.dot(rows, wu[0], preferred_element_type=f32)
        return carry

    lax.fori_loop(0, 4, own_half, 0)
    wait_in(pushes)

    def other_half(i, carry):
        rows = pushed[i, :, :, :, pl.ds(0, HALF)].reshape(256, HALF)
        gate_part = gate_acc[i] + jnp.dot(rows, wg[1], preferred_element_type=f32)
        up_part = up_acc[i] + jnp.dot(rows, wu[1], preferred_element_type=f32)
        table = held[i, :, :, :, pl.ds(HALF, 128)].reshape(256, 128).astype(f32)
        lane = lax.broadcasted_iota(jnp.int32, (256, 128), 1)
        here = (lane == link.ep) | (lane == link.ep + 32)
        factor = jnp.sum(jnp.where(here, table, 0.0), axis=1, keepdims=True)
        units[i] = (jax.nn.silu(gate_part) * up_part * factor).astype(bf16)
        return carry

    lax.fori_loop(0, 4, other_half, 0)
    wait_out(gathers + pushes)

    back = []
    for i in range(4):

        @pl.loop(0, 7)
        def _(j, i=i):
            lanes = pl.ds(pl.multiple_of(j * 512, 512), 512)
            value = jnp.dot(units[i], wd[1, :, lanes], preferred_element_type=f32)
            pushed[i, :, :, :, lanes] = value.astype(bf16).reshape(4, 4, 16, 512)

        dst = big.at[i]
        back.append(link.send(pushed.at[i, :, :, :, pl.ds(0, HALF)], dst, partner, dst))
    for i in range(4):
        wait_in(back[i : i + 1])

        @pl.loop(0, 7)
        def _(j, i=i):
            lanes = pl.ds(pl.multiple_of(j * 512, 512), 512)
            value = jnp.dot(units[i], wd[0, :, lanes], preferred_element_type=f32)
            value = value.reshape(4, 4, 16, 512) + big[i, :, :, :, lanes].astype(f32)
            held[i, :, :, :, lanes] = value.astype(bf16)

    sent += back

    def add_routed(start, width, total):
        lanes = pl.ds(start, width)
        fin[:, :, lanes] = hid[:, :, lanes] + total.reshape(2, 8, width)

    sent += scatter_sums(
        link,
        RS_PARTS,
        (0, 1, 2),
        held,
        ((far0, low0, high0), (far1, low1, high1), (far2, low2, high2)),
        add_routed,
    )
    swap = link.send(fin.at[other], fin_in, partner, fin_in)
    sent.append(swap)
    out_ref[core] = fin[core]
    wait_in([swap])
    out_ref[other] = fin_in[...]
    wait_out(sent)


def layer_call(head_rows, w_uv, resid_halves, chosen, gain, router, w_out, w_gate, w_up, w_down):
    vmem, hbm = pl.BlockSpec(memory_space=pltpu.VMEM), pl.BlockSpec(memory_space=pl.ANY)
    bf16, f32 = jnp.bfloat16, jnp.float32

    def block(*lead, lanes=HALF, kind=bf16):
        return pltpu.VMEM(lead + (lanes,), kind)

    plane = [block(4, 16), block(16)] * 3
    torus = [block(4, 4, 16)] * 3 + [block(4, 16)] * 3 + [block(16)] * 3
    scratch = (
        [block(4, 4, 4, 16)]
        + [pltpu.VMEM((2, HALF, 256), bf16)] * 2
        + [pltpu.VMEM((2, 256, HALF), bf16), pltpu.VMEM((256, 512), bf16)]
        + [block(4, 4, 16)] * 3
        + plane
        + [block(2, 8, kind=f32), pltpu.VMEM((2, 8, 128), f32)]
        + [pltpu.VMEM((16, 128), f32)] * 2
        + [block(4, 4, 4, 16, lanes=GW)] * 2
        + [pltpu.VMEM((4, 256, 256), f32)] * 2
        + [pltpu.VMEM((4, 256, 256), bf16)]
        + torus
        + [block(2, 8, kind=f32), block(8, kind=f32)]
        + [pltpu.SemaphoreType.DMA((COPIES,))] * 2
        + [pltpu.SemaphoreType.DMA((8,))]
    )
    return pl.pallas_call(
        layer_kernel,
        out_shape=jax.ShapeDtypeStruct((2, 8, HALF), f32),
        in_specs=[vmem] * 6 + [hbm] * 4,
        out_specs=vmem,
        scratch_shapes=scratch,
        compiler_params=pltpu.CompilerParams(
            collective_id=1, has_side_effects=True, vmem_limit_bytes=62 * 1024 * 1024
        ),
        cost_estimate=pl.CostEstimate(
            flops=20_000_000_000, bytes_accessed=22_000_000, transcendentals=300_000
        ),
        name="layer",
    )(head_rows, w_uv, resid_halves, chosen, gain, router, w_out, w_gate, w_up, w_down)


def layer_operands(resid, routes, w_out, norm_gain, router_w, w_gate, w_up, w_down):
    resid_halves = jnp.swapaxes(resid.reshape(8, 2, HALF), 0, 1).astype(jnp.float32)
    route_rows = routes.reshape(8, -1)
    chosen = jnp.any(route_rows[..., None] == jnp.arange(128), axis=1).astype(jnp.float32)
    gain = norm_gain.astype(jnp.float32).reshape(2, 1, HALF)
    router = jnp.pad(router_w, ((0, 0), (0, 128 - router_w.shape[1]))).reshape(2, HALF, 128)
    return (
        resid_halves,
        chosen,
        gain,
        router,
        w_out.reshape(2, 4, 4, 16, 2 * HALF),
        w_gate[0],
        w_up[0],
        w_down[0],
    )


CHUNKS = 8
CHUNK = 4608
PAIR = 2 * LATW
WIDE = 640
AHEAD = 3


def attend_kernel(
    length_ref,
    pages_hbm,
    perm_ref,
    query_ref,
    fresh_ref,
    heads_ref,
    pages,
    passing,
    rows32,
    query_even,
    query_odd,
    keys,
    acc_even,
    acc_odd,
    row_max,
    row_sum,
    out32,
    out16,
    own_sem,
    link_send,
    link_recv,
    head_send,
    head_recv,
):
    f32, bf16 = jnp.float32, jnp.bfloat16
    z, ep = lax.axis_index("ctx"), lax.axis_index("ep")
    above, below, far = lax.rem(z + 1, 4), lax.rem(z + 3, 4), lax.rem(z + 2, 4)
    up, down = (above, ep), (below, ep)

    def lanes(j):
        return pl.ds(pl.multiple_of(j * CHUNK, 128), CHUNK)

    def half(j, k):
        return pl.ds(pl.multiple_of(j * CHUNK + k * (CHUNK // 2), 128), CHUNK // 2)

    def copy(kind, j, src, dst, device):
        return pltpu.make_async_remote_copy(
            src_ref=src,
            dst_ref=dst,
            send_sem=link_send.at[kind, j],
            recv_sem=link_recv.at[kind, j],
            device_id=device,
            device_id_type=MESH_IDS,
        )

    def outgoing(kind, j):
        if kind == 0:
            return copy(0, j, pages_hbm.at[far, :, half(j, 0)], passing.at[:, half(j, 0)], up)
        if kind == 1:
            return copy(1, j, pages_hbm.at[far, :, half(j, 1)], passing.at[:, half(j, 1)], down)
        if kind == 2:
            return copy(2, j, pages_hbm.at[above, :, lanes(j)], pages.at[z, :, lanes(j)], up)
        if kind == 3:
            return copy(3, j, pages_hbm.at[below, :, lanes(j)], pages.at[z, :, lanes(j)], down)
        if kind == 4:
            return copy(4, j, passing.at[:, half(j, 0)], pages.at[below, :, half(j, 0)], up)
        return copy(5, j, passing.at[:, half(j, 1)], pages.at[above, :, half(j, 1)], down)

    def arrived(kind, j):
        place = (
            passing.at[:, half(j, 0)],
            passing.at[:, half(j, 1)],
            pages.at[below, :, lanes(j)],
            pages.at[above, :, lanes(j)],
            pages.at[far, :, half(j, 0)],
            pages.at[far, :, half(j, 1)],
        )[kind]
        copy(kind, j, place, place, up).wait_recv()

    def own(j):
        return pltpu.make_async_copy(
            pages_hbm.at[z, :, lanes(j)], pages.at[z, :, lanes(j)], own_sem.at[j]
        )

    def issue(j):
        for kind in range(4):
            outgoing(kind, j).start()

    def forward(j):
        for kind in (0, 1):
            arrived(kind, j)
            outgoing(kind + 4, j).start()

    barrier = pltpu.get_barrier_semaphore()
    for device in (up, down):
        pl.semaphore_signal(barrier, inc=1, device_id=device, device_id_type=MESH_IDS)

    @pl.loop(1, 32)
    def _(d):
        device = (z, lax.rem(ep + d, 32))
        pl.semaphore_signal(barrier, inc=1, device_id=device, device_id_type=MESH_IDS)

    pl.semaphore_wait(barrier, 33)

    for j in range(AHEAD):
        issue(j)

    @pl.loop(0, CHUNKS)
    def _(j):
        own(j).start()

    forward(0)

    @pl.loop(0, 64)
    def _(pair):
        span = pl.ds(pl.multiple_of(pair * PAIR, 128), PAIR)
        both = [query_ref[s, :, span].astype(f32) for s in range(2)]
        both = jnp.concatenate(both, axis=0)
        for k in range(PAIR // 128):
            rows32[k, pl.ds(pl.multiple_of(pair * 8, 8), 8), :] = both[:, k * 128 : k * 128 + 128]

    lane = lax.broadcasted_iota(jnp.int32, (64, WIDE), 1)
    for q in range(4):
        for s in range(2):
            rows = jnp.concatenate(
                [rows32[k, pl.ds(s * 4 + q, 64, stride=8), :] for k in range(PAIR // 128)], axis=1
            )
            even = jnp.where(lane < LATW, rows[:, :WIDE], 0.0)
            odd = jnp.where(lane >= 64, rows[:, PAIR - WIDE :], 0.0)
            for parity, value, shift in ((0, even, 64), (1, odd, WIDE - 64)):
                place = pl.ds(s * 128 + parity * 64, 64)
                moved = pltpu.roll(value, shift, axis=1).astype(bf16)
                value = value.astype(bf16)
                query_even[q, place, :] = value if parity == 0 else moved
                query_odd[q, place, :] = moved if parity == 0 else value

    scale = (NOPE + ROPE) ** (-0.5)
    contract = (((1,), (1,)), ((), ()))

    @pl.loop(0, 4)
    def _(q):
        fresh = fresh_ref[q]
        score = (
            lax.dot_general(query_even[q], fresh, contract, preferred_element_type=f32) * scale
        )
        token = lax.broadcasted_iota(jnp.int32, (256, 128), 1)
        step = lax.broadcasted_iota(jnp.int32, (256, 128), 0) // 128
        score = jnp.where(token <= step, score, masked_score)
        top = jnp.max(score, axis=1, keepdims=True)
        weight = jnp.exp(score - top)
        row_max[q] = jnp.broadcast_to(top, (256, 128))
        row_sum[q] = jnp.broadcast_to(jnp.sum(weight, axis=1, keepdims=True), (256, 128))
        acc_even[q] = jnp.dot(weight.astype(bf16), fresh[:, :LAT], preferred_element_type=f32)
        acc_odd[q] = jnp.zeros((256, WIDE), f32)

    @pl.loop(0, CHUNKS)
    def _(j):
        @pl.when(j + AHEAD < CHUNKS)
        def _():
            issue(j + AHEAD)

        @pl.when(j + 1 < CHUNKS)
        def _():
            forward(j + 1)

        own(j).wait()
        for kind in (2, 3, 4, 5):
            arrived(kind, j)

        for i in range(4):
            span = pl.ds(pl.multiple_of(j * CHUNK + i * PAIR, 128), PAIR)
            found = [
                jnp.dot(perm_ref[c], pages[c, :, span], preferred_element_type=f32)
                for c in range(4)
            ]
            for q in range(4):
                rows = jnp.concatenate([one[q * 8 : q * 8 + 8] for one in found], axis=0)
                keys[q, pl.ds(i * 32, 32), :] = rows.astype(bf16)

        @pl.loop(0, 4)
        def _(q):
            key = keys[q]
            low, high = key[:, :WIDE], key[:, PAIR - WIDE :]
            score = jnp.concatenate(
                [
                    lax.dot_general(query_even[q], low, contract, preferred_element_type=f32),
                    lax.dot_general(query_odd[q], high, contract, preferred_element_type=f32),
                ],
                axis=1,
            )
            n = lax.broadcasted_iota(jnp.int32, (1, 256), 1)
            fifth = n % 8
            page = 4 * fifth + (n % 32) // 8
            position = page * 64 + 2 * (4 * j + (n % 128) // 32) + n // 128
            live = (fifth < 5) & (position < length_ref[q])
            score = jnp.where(live, score * scale, masked_score)
            before = row_max[q]
            top = jnp.maximum(before, jnp.max(score, axis=1, keepdims=True))
            shrink = jnp.exp(before - top)
            weight = jnp.exp(score - jnp.concatenate([top, top], axis=1))
            row_max[q] = top
            row_sum[q] = row_sum[q] * shrink + jnp.sum(weight, axis=1, keepdims=True)
            weight = weight.astype(bf16)
            acc_even[q] = acc_even[q] * shrink[:, :1] + jnp.dot(
                weight[:, :128], low[:, :LAT], preferred_element_type=f32
            )
            acc_odd[q] = acc_odd[q] * shrink[:, :1] + jnp.dot(
                weight[:, 128:], high, preferred_element_type=f32
            )

    for q in range(4):
        value = (acc_even[q] + acc_odd[q][:, 64 : 64 + LAT]) / row_sum[q][:, :1]
        for block in range(4):
            s, parity = block // 2, block % 2
            for k in range(LAT // 128):
                out32[k, pl.ds(parity * 8 + s * 4 + q, 64, stride=16), :] = value[
                    block * 64 : block * 64 + 64, k * 128 : k * 128 + 128
                ]

    @pl.loop(0, 32)
    def _(e):
        for k in range(LAT // 128):
            out16[e, :, pl.ds(k * 128, 128)] = out32[
                k, pl.ds(pl.multiple_of(e * 32, 32), 32), :
            ].astype(bf16)

    def head_copy(d, src, dst, device):
        return pltpu.make_async_remote_copy(
            src_ref=src,
            dst_ref=dst,
            send_sem=head_send.at[d],
            recv_sem=head_recv.at[d],
            device_id=device,
            device_id_type=MESH_IDS,
        )

    def head_block(d):
        target = lax.rem(ep + d, 32)
        return head_copy(d, out16.at[target], heads_ref.at[ep], (z, target))

    @pl.loop(1, 32)
    def _(d):
        head_block(d).start()

    heads_ref[ep] = out16[ep]

    @pl.loop(1, 32)
    def _(d):
        source = heads_ref.at[lax.rem(ep + 32 - d, 32)]
        head_copy(d, source, source, up).wait_recv()

    @pl.loop(1, 32)
    def _(d):
        head_block(d).wait_send()

    @pl.loop(0, CHUNKS)
    def _(j):
        for kind in range(6):
            outgoing(kind, j).wait_send()


def attend_call(prefill_pages, page_map, prompt_len, queries, new_latent):
    bf16, f32 = jnp.bfloat16, jnp.float32
    slots, width = prefill_pages.shape[3:]
    row = jnp.arange(32)
    request, fifth = row // 8, row % 8
    wanted = request[None, :] * 20 + 4 * fifth[None, :] + jnp.arange(4)[:, None]
    wanted = jnp.where(fifth[None, :] < 5, wanted, -1)
    perm = (page_map.reshape(4, 1, slots) == wanted[:, :, None]).astype(bf16)
    fresh = jnp.pad(jnp.swapaxes(new_latent, 0, 1), ((0, 0), (0, 126), (0, WIDE - LATW)))
    vmem, hbm = pl.BlockSpec(memory_space=pltpu.VMEM), pl.BlockSpec(memory_space=pl.ANY)
    return pl.pallas_call(
        attend_kernel,
        out_shape=jax.ShapeDtypeStruct((32, 32, LAT), bf16),
        in_specs=[pl.BlockSpec(memory_space=pltpu.SMEM), hbm, vmem, vmem, vmem],
        out_specs=vmem,
        scratch_shapes=[
            pltpu.VMEM((4, slots, width), bf16),
            pltpu.VMEM((slots, width), bf16),
            pltpu.VMEM((PAIR // 128, 512, 128), f32),
            pltpu.VMEM((4, 256, WIDE), bf16),
            pltpu.VMEM((4, 256, WIDE), bf16),
            pltpu.VMEM((4, 128, PAIR), bf16),
            pltpu.VMEM((4, 256, LAT), f32),
            pltpu.VMEM((4, 256, WIDE), f32),
            pltpu.VMEM((4, 256, 128), f32),
            pltpu.VMEM((4, 256, 128), f32),
            pltpu.VMEM((LAT // 128, 1024, 128), f32),
            pltpu.VMEM((32, 32, LAT), bf16),
            pltpu.SemaphoreType.DMA((CHUNKS,)),
            pltpu.SemaphoreType.DMA((6, CHUNKS)),
            pltpu.SemaphoreType.DMA((6, CHUNKS)),
            pltpu.SemaphoreType.DMA((32,)),
            pltpu.SemaphoreType.DMA((32,)),
        ],
        compiler_params=pltpu.CompilerParams(
            collective_id=2, has_side_effects=True, vmem_limit_bytes=56 * 1024 * 1024
        ),
        cost_estimate=pl.CostEstimate(
            flops=4_000_000_000, bytes_accessed=8_000_000, transcendentals=1_500_000
        ),
        name="attend",
    )(prompt_len, prefill_pages.reshape(4, slots, width), perm, queries, fresh)


def per_device(
    prefill_pages,
    page_map,
    prompt_len,
    queries,
    new_latent,
    resid,
    w_uv,
    w_out,
    norm_gain,
    router_w,
    routes,
    w_gate,
    w_up,
    w_down,
):
    head_rows = attend_call(prefill_pages, page_map, prompt_len, queries, new_latent)
    operands = layer_operands(resid, routes, w_out, norm_gain, router_w, w_gate, w_up, w_down)
    halves = layer_call(head_rows, w_uv, *operands)
    rows = jnp.swapaxes(halves, 0, 1).astype(jnp.bfloat16)
    return rows.reshape(resid.shape)


def solution(mesh):
    placed = (
        P("ctx", "ep", None, None, None),
        P("ctx", "ep", None, None),
        P(("ctx", "ep")),
        P(None, ("ctx", "ep"), None),
        P(None, ("ctx", "ep"), None),
        P(None, ("ctx", "ep"), None),
        P("ep", None, None),
        P("ep", None),
        P(),
        P(),
        P(None, ("ctx", "ep"), None),
        P("ep", None, "ctx"),
        P("ep", None, "ctx"),
        P("ep", "ctx", None),
    )
    return jax.shard_map(
        per_device,
        mesh=mesh,
        in_specs=placed,
        out_specs=P(None, ("ctx", "ep"), None),
        check_vma=False,
    )
```

```python
import jax
import jax.numpy as jnp
from jax import lax
from jax.experimental import pallas as pl
from jax.experimental.pallas import tpu as pltpu
from jax.sharding import PartitionSpec as P

LAT = 512
ROPE = 64
NOPE = 128
LATW = 576


norm_eps = 1e-06
route_scale = 2.5
masked_score = -1e30

HALF = 3584
GW = HALF + 128
MESH_IDS = pl.DeviceIdType.MESH
AG_PARTS = ((0, 640, 640), (1280, 640, 640), (2560, 640, 512))
RS_PARTS = ((0, 640, 512), (1152, 640, 512), (2304, 640, 640))
PLANE_PARTS = ((0, 896, 896), (1792, 896, 896))
COPIES = 160


class Links:
    def __init__(self, send_sem, recv_sem):
        self.send_sem, self.recv_sem, self.used = send_sem, recv_sem, 0
        self.z, ep = lax.axis_index("ctx"), lax.axis_index("ep")
        self.core = lax.rem(ep, 2)
        self.y, self.x = ep // 8, lax.rem(ep // 2, 4)
        self.ep = ep
        self.coords = (self.z, self.y, self.x)

    def shifted(self, axis, step):
        return lax.rem(self.coords[axis] + (step % 4), 4)

    def neighbour(self, axis, step):
        c = list(self.coords)
        c[axis] = self.shifted(axis, step)
        return (c[0], (c[1] * 4 + c[2]) * 2 + self.core)

    def partner(self):
        return (self.z, self.ep + 1 - 2 * self.core)

    def send(self, src, dst, device, landing):
        k = self.used
        self.used += 1
        make = lambda s, d: pltpu.make_async_remote_copy(
            src_ref=s,
            dst_ref=d,
            send_sem=self.send_sem.at[k],
            recv_sem=self.recv_sem.at[k],
            device_id=device,
            device_id_type=MESH_IDS,
        )
        out = make(src, dst)
        out.start()
        return out, make(landing, landing)


def wait_in(copies):
    for _, incoming in copies:
        incoming.wait_recv()


def wait_out(copies):
    for outgoing, _ in copies:
        outgoing.wait_send()


def pick(ref, chosen, start, width):
    index = tuple(chosen.get(a, slice(None)) for a in range(len(ref.shape) - 2))
    return ref.at[index + (slice(None), pl.ds(start, width))]


def gather_blocks(link, held, pushed):
    sent, pushes = [], []

    def push(part, axis, coord):
        start, wa, wb = AG_PARTS[part]
        src = pick(held, {axis: coord}, start, wa + wb)
        dst = pick(pushed, {axis: coord}, start, wa + wb)
        pushes.append(link.send(src, dst, link.partner(), dst))

    for stage in range(3):
        first = []
        for p, (start, wa, wb) in enumerate(AG_PARTS):
            order = [(p + j) % 3 for j in range(3)]
            axis = order[stage]
            rest = {a: link.coords[a] for a in order[stage + 1 :]}
            mine = pick(held, {**rest, axis: link.coords[axis]}, start, wa + wb)
            below = pick(held, {**rest, axis: link.shifted(axis, -1)}, start, wa + wb)
            above = pick(held, {**rest, axis: link.shifted(axis, 1)}, start, wa + wb)
            first.append(
                (
                    link.send(mine, mine, link.neighbour(axis, 1), below),
                    link.send(mine, mine, link.neighbour(axis, -1), above),
                )
            )
            if stage == 2:
                push(p, axis, link.coords[axis])
        second = []
        for p, (start, wa, wb) in enumerate(AG_PARTS):
            order = [(p + j) % 3 for j in range(3)]
            axis = order[stage]
            rest = {a: link.coords[a] for a in order[stage + 1 :]}
            wait_in(first[p])
            up = pick(held, {**rest, axis: link.shifted(axis, -1)}, start, wa)
            down = pick(held, {**rest, axis: link.shifted(axis, 1)}, start + wa, wb)
            far_a = pick(held, {**rest, axis: link.shifted(axis, 2)}, start, wa)
            far_b = pick(held, {**rest, axis: link.shifted(axis, 2)}, start + wa, wb)
            second.append(
                (
                    link.send(up, up, link.neighbour(axis, 1), far_a),
                    link.send(down, down, link.neighbour(axis, -1), far_b),
                )
            )
            if stage == 2:
                push(p, axis, link.shifted(axis, -1))
                push(p, axis, link.shifted(axis, 1))
        for p in range(3):
            wait_in(second[p])
            if stage == 2:
                push(p, (p + 2) % 3, link.shifted((p + 2) % 3, 2))
            sent += list(first[p]) + list(second[p])
    return sent, pushes


def scatter_sums(link, parts, axes, sums, landings, last):
    sent = []
    count = len(axes)
    for stage in range(count):
        far_in, low_in, high_in = landings[stage]
        steps = []
        for p, (start, wa, wb) in enumerate(parts):
            order = [axes[(p + j) % count] for j in range(count)]
            axis = order[stage]
            done = {a: link.coords[a] for a in order[:stage]}
            at = lambda coord, lo, w, done=done, axis=axis: pick(
                sums, {k - axes[0]: v for k, v in {**done, axis: coord}.items()}, lo, w
            )
            land = lambda ref, lo, w: ref.at[(slice(None),) * (count - stage) + (pl.ds(lo, w),)]
            far = link.shifted(axis, 2)
            la, lb = land(far_in, start, wa), land(far_in, start + wa, wb)
            steps.append(
                (
                    at,
                    land,
                    axis,
                    (
                        link.send(at(far, start, wa), la, link.neighbour(axis, 1), la),
                        link.send(at(far, start + wa, wb), lb, link.neighbour(axis, -1), lb),
                    ),
                )
            )
        final = []
        for p, (start, wa, wb) in enumerate(parts):
            at, land, axis, first = steps[p]
            wait_in(first)
            up, down = link.shifted(axis, 1), link.shifted(axis, -1)
            for coord, lo, w in ((up, start, wa), (down, start + wa, wb)):
                view, got = at(coord, lo, w), land(far_in, lo, w)
                view[...] = (
                    view[...].astype(jnp.float32) + got[...].astype(jnp.float32)
                ).astype(jnp.bfloat16)
            low, high = land(low_in, start, wa + wb), land(high_in, start, wa + wb)
            second = (
                link.send(at(up, start, wa + wb), low, link.neighbour(axis, 1), low),
                link.send(at(down, start, wa + wb), high, link.neighbour(axis, -1), high),
            )
            final.append((at(link.coords[axis], start, wa + wb), low, high, second))
            sent += list(first) + list(second)
        for p, (start, wa, wb) in enumerate(parts):
            view, low, high, second = final[p]
            wait_in(second)
            total = (
                view[...].astype(jnp.float32)
                + low[...].astype(jnp.float32)
                + high[...].astype(jnp.float32)
            )
            if stage == count - 1:
                last(start, wa + wb, total)
            else:
                view[...] = total.astype(jnp.bfloat16)
    return sent


def layer_kernel(
    heads_ref,
    w_uv_ref,
    resid_ref,
    chosen_ref,
    gain_ref,
    router_ref,
    w_out_hbm,
    w_gate_hbm,
    w_up_hbm,
    w_down_hbm,
    out_ref,
    big,
    wg,
    wu,
    wd,
    flat,
    part_send,
    part_land,
    part_sum,
    plane_a0,
    plane_a1,
    plane_b0,
    plane_b1,
    plane_c0,
    plane_c1,
    hid,
    picked,
    stat_out,
    stat_in,
    held,
    pushed,
    gate_acc,
    up_acc,
    units,
    far0,
    low0,
    high0,
    far1,
    low1,
    high1,
    far2,
    low2,
    high2,
    fin,
    fin_in,
    send_sem,
    recv_sem,
    load_sem,
):
    link = Links(send_sem, recv_sem)
    core = link.core
    other = 1 - core
    partner = link.partner()
    f32, bf16 = jnp.float32, jnp.bfloat16

    own_cols = pl.ds(pl.multiple_of(core * HALF, 128), HALF)
    other_cols = pl.ds(pl.multiple_of(other * HALF, 128), HALF)
    loads = []

    def load(src, dst):
        copy = pltpu.make_async_copy(src, dst, load_sem.at[len(loads)])
        copy.start()
        loads.append(copy)

    load(w_out_hbm.at[:, :, :, :, other_cols], big.at[pl.ds(2, 2)])
    load(w_out_hbm.at[:, :, :, :, own_cols], big.at[pl.ds(0, 2)])
    for slot, cols in ((0, own_cols), (1, other_cols)):
        load(w_gate_hbm.at[cols], wg.at[slot])
        load(w_up_hbm.at[cols], wu.at[slot])
        load(w_down_hbm.at[:, cols], wd.at[slot])

    barrier = pltpu.get_barrier_semaphore()
    for axis in range(3):
        for step in (1, -1):
            pl.semaphore_signal(
                barrier, inc=1, device_id=link.neighbour(axis, step), device_id_type=MESH_IDS
            )
    pl.semaphore_signal(barrier, inc=1, device_id=partner, device_id_type=MESH_IDS)
    pl.semaphore_wait(barrier, 7)

    sent = []
    swaps = [
        link.send(resid_ref.at[other], hid.at[core], partner, hid.at[other]),
        link.send(chosen_ref, picked.at[core], partner, picked.at[other]),
    ]
    sent += swaps

    for pair in range(2):
        rows = heads_ref[:, pl.ds(pair * 16, 16), :].reshape(512, LAT)
        for one in range(2):
            head = 2 * pair + one
            value = jnp.dot(rows, w_uv_ref[head], preferred_element_type=f32)
            value = value.reshape(32, 2, 8, 128)[:, one].reshape(256, 128)
            flat[:, pl.ds(head * 128, 128)] = value.astype(bf16)

    def project(slot, start):
        lanes = pl.ds(start, 256)
        weight = big[pl.ds(2 * slot, 2), :, :, :, lanes].reshape(512, 256)
        value = jnp.dot(flat[...], weight, preferred_element_type=f32)
        return value.reshape(4, 4, 16, 256)

    loads[0].wait()
    core_swap = []
    for start in (0, 1792):

        @pl.loop(0, 7)
        def _(j, start=start):
            at = pl.multiple_of(start + j * 256, 256)
            part_send[:, :, :, pl.ds(at, 256)] = project(1, at).astype(bf16)

        lanes = pl.ds(start, 1792)
        dst = part_land.at[:, :, :, lanes]
        core_swap.append(link.send(part_send.at[:, :, :, lanes], dst, partner, dst))
    sent += core_swap
    loads[1].wait()
    for turn, start in enumerate((0, 1792)):
        wait_in(core_swap[turn : turn + 1])

        @pl.loop(0, 7)
        def _(j, start=start):
            at = pl.multiple_of(start + j * 256, 256)
            value = project(0, at) + part_land[:, :, :, pl.ds(at, 256)].astype(f32)
            part_sum[:, :, :, pl.ds(at, 256)] = value.astype(bf16)

    hid[core] = resid_ref[core]
    picked[core] = chosen_ref[...]
    wait_in(swaps)

    def add_hidden(start, width, total):
        lanes = pl.ds(start, width)
        hid[:, :, lanes] = hid[:, :, lanes] + total.reshape(2, 8, width)

    sent += scatter_sums(
        link,
        PLANE_PARTS,
        (1, 2),
        part_sum,
        ((plane_a0, plane_b0, plane_c0), (plane_a1, plane_b1, plane_c1)),
        add_hidden,
    )

    hidden = hid[...].reshape(16, HALF)
    gain = gain_ref[core]
    logits = jnp.dot(
        (hidden * gain).astype(bf16), router_ref[core], preferred_element_type=f32
    )
    squares = jnp.sum(hidden * hidden, axis=1, keepdims=True)
    lane = lax.broadcasted_iota(jnp.int32, (16, 128), 1)
    mine = jnp.where(lane < 64, logits, jnp.broadcast_to(squares, (16, 128)))
    stat_out[...] = mine
    stat = link.send(stat_out, stat_in, partner, stat_in)
    sent.append(stat)
    wait_in([stat])
    both = mine + stat_in[...]
    scale = lax.rsqrt(both[:, 64:65] / (2 * HALF) + norm_eps)
    affinity = jax.nn.sigmoid(both * scale) * picked[...].reshape(16, 128)
    weights = route_scale * affinity / jnp.sum(affinity, axis=1, keepdims=True)
    high = weights.astype(bf16)
    low = (weights - high.astype(f32)).astype(bf16).astype(f32)
    table = high.astype(f32) + pltpu.roll(low, 32, axis=1)
    normed = (hid[...].reshape(16, HALF) * scale * gain).astype(bf16)
    held[link.z, link.y, link.x, :, pl.ds(0, HALF)] = normed
    held[link.z, link.y, link.x, :, pl.ds(HALF, 128)] = table.astype(bf16)

    gathers, pushes = gather_blocks(link, held, pushed)

    for copy in loads[2:]:
        copy.wait()

    def own_half(i, carry):
        rows = held[i, :, :, :, pl.ds(0, HALF)].reshape(256, HALF)
        gate_acc[i] = jnp.dot(rows, wg[0], preferred_element_type=f32)
        up_acc[i] = jnp.dot(rows, wu[0], preferred_element_type=f32)
        return carry

    lax.fori_loop(0, 4, own_half, 0)
    wait_in(pushes)

    def other_half(i, carry):
        rows = pushed[i, :, :, :, pl.ds(0, HALF)].reshape(256, HALF)
        gate_part = gate_acc[i] + jnp.dot(rows, wg[1], preferred_element_type=f32)
        up_part = up_acc[i] + jnp.dot(rows, wu[1], preferred_element_type=f32)
        table = held[i, :, :, :, pl.ds(HALF, 128)].reshape(256, 128).astype(f32)
        lane = lax.broadcasted_iota(jnp.int32, (256, 128), 1)
        here = (lane == link.ep) | (lane == link.ep + 32)
        factor = jnp.sum(jnp.where(here, table, 0.0), axis=1, keepdims=True)
        units[i] = (jax.nn.silu(gate_part) * up_part * factor).astype(bf16)
        return carry

    lax.fori_loop(0, 4, other_half, 0)
    wait_out(gathers + pushes)

    back = []
    for i in range(4):

        @pl.loop(0, 7)
        def _(j, i=i):
            lanes = pl.ds(pl.multiple_of(j * 512, 512), 512)
            value = jnp.dot(units[i], wd[1, :, lanes], preferred_element_type=f32)
            pushed[i, :, :, :, lanes] = value.astype(bf16).reshape(4, 4, 16, 512)

        dst = big.at[i]
        back.append(link.send(pushed.at[i, :, :, :, pl.ds(0, HALF)], dst, partner, dst))
    for i in range(4):
        wait_in(back[i : i + 1])

        @pl.loop(0, 7)
        def _(j, i=i):
            lanes = pl.ds(pl.multiple_of(j * 512, 512), 512)
            value = jnp.dot(units[i], wd[0, :, lanes], preferred_element_type=f32)
            value = value.reshape(4, 4, 16, 512) + big[i, :, :, :, lanes].astype(f32)
            held[i, :, :, :, lanes] = value.astype(bf16)

    sent += back

    def add_routed(start, width, total):
        lanes = pl.ds(start, width)
        fin[:, :, lanes] = hid[:, :, lanes] + total.reshape(2, 8, width)

    sent += scatter_sums(
        link,
        RS_PARTS,
        (0, 1, 2),
        held,
        ((far0, low0, high0), (far1, low1, high1), (far2, low2, high2)),
        add_routed,
    )
    swap = link.send(fin.at[other], fin_in, partner, fin_in)
    sent.append(swap)
    out_ref[core] = fin[core]
    wait_in([swap])
    out_ref[other] = fin_in[...]
    wait_out(sent)


def layer_call(head_rows, w_uv, resid_halves, chosen, gain, router, w_out, w_gate, w_up, w_down):
    vmem, hbm = pl.BlockSpec(memory_space=pltpu.VMEM), pl.BlockSpec(memory_space=pl.ANY)
    bf16, f32 = jnp.bfloat16, jnp.float32

    def block(*lead, lanes=HALF, kind=bf16):
        return pltpu.VMEM(lead + (lanes,), kind)

    plane = [block(4, 16), block(16)] * 3
    torus = [block(4, 4, 16)] * 3 + [block(4, 16)] * 3 + [block(16)] * 3
    scratch = (
        [block(4, 4, 4, 16)]
        + [pltpu.VMEM((2, HALF, 256), bf16)] * 2
        + [pltpu.VMEM((2, 256, HALF), bf16), pltpu.VMEM((256, 512), bf16)]
        + [block(4, 4, 16)] * 3
        + plane
        + [block(2, 8, kind=f32), pltpu.VMEM((2, 8, 128), f32)]
        + [pltpu.VMEM((16, 128), f32)] * 2
        + [block(4, 4, 4, 16, lanes=GW)] * 2
        + [pltpu.VMEM((4, 256, 256), f32)] * 2
        + [pltpu.VMEM((4, 256, 256), bf16)]
        + torus
        + [block(2, 8, kind=f32), block(8, kind=f32)]
        + [pltpu.SemaphoreType.DMA((COPIES,))] * 2
        + [pltpu.SemaphoreType.DMA((8,))]
    )
    return pl.pallas_call(
        layer_kernel,
        out_shape=jax.ShapeDtypeStruct((2, 8, HALF), f32),
        in_specs=[vmem] * 6 + [hbm] * 4,
        out_specs=vmem,
        scratch_shapes=scratch,
        compiler_params=pltpu.CompilerParams(
            collective_id=1, has_side_effects=True, vmem_limit_bytes=62 * 1024 * 1024
        ),
        cost_estimate=pl.CostEstimate(
            flops=20_000_000_000, bytes_accessed=22_000_000, transcendentals=300_000
        ),
        name="layer",
    )(head_rows, w_uv, resid_halves, chosen, gain, router, w_out, w_gate, w_up, w_down)


def layer_operands(resid, routes, w_out, norm_gain, router_w, w_gate, w_up, w_down):
    resid_halves = jnp.swapaxes(resid.reshape(8, 2, HALF), 0, 1).astype(jnp.float32)
    route_rows = routes.reshape(8, -1)
    chosen = jnp.any(route_rows[..., None] == jnp.arange(128), axis=1).astype(jnp.float32)
    gain = norm_gain.astype(jnp.float32).reshape(2, 1, HALF)
    router = jnp.pad(router_w, ((0, 0), (0, 128 - router_w.shape[1]))).reshape(2, HALF, 128)
    return (
        resid_halves,
        chosen,
        gain,
        router,
        w_out.reshape(2, 4, 4, 16, 2 * HALF),
        w_gate[0],
        w_up[0],
        w_down[0],
    )


CHUNKS = 8
PAIR = 2 * LATW
WIDE = 640
QUARTER = 9216
SPREAD = (2, 1, 3)


def attend_kernel(
    length_ref,
    pages_hbm,
    perm_ref,
    query_ref,
    fresh_ref,
    heads_ref,
    raw,
    rows_raw,
    packed,
    pages,
    rows32,
    query_even,
    query_odd,
    keys,
    acc_even,
    acc_odd,
    row_max,
    row_sum,
    out32,
    out16,
    raw_sem,
    own_sem,
    link_send,
    link_recv,
    head_send,
    head_recv,
):
    f32, bf16 = jnp.float32, jnp.bfloat16
    z, ep = lax.axis_index("ctx"), lax.axis_index("ep")

    def lanes(j):
        return pl.ds(pl.multiple_of(j * PAIR, 128), PAIR)

    def ring(step):
        return lax.rem(z + step, 4)

    def copy(kind, j, src, dst, device):
        return pltpu.make_async_remote_copy(
            src_ref=src,
            dst_ref=dst,
            send_sem=link_send.at[kind, j],
            recv_sem=link_recv.at[kind, j],
            device_id=device,
            device_id_type=MESH_IDS,
        )

    def outgoing(kind, j):
        owner = ring(SPREAD[kind])
        return copy(
            kind, j, packed.at[owner, :, lanes(j)], pages.at[z, :, lanes(j)], (owner, ep)
        )

    def arrived(kind, j):
        producer = ring(4 - SPREAD[kind])
        place = pages.at[producer, :, lanes(j)]
        copy(kind, j, place, place, (producer, ep)).wait_recv()

    def own(j):
        return pltpu.make_async_copy(
            packed.at[z, :, lanes(j)], pages.at[z, :, lanes(j)], own_sem.at[j]
        )

    def fetch(j, quarter):
        span = pl.ds(pl.multiple_of(quarter * QUARTER + j * PAIR, 128), PAIR)
        return pltpu.make_async_copy(
            pages_hbm.at[:, :, span], raw.at[:, :, span], raw_sem.at[j, quarter]
        )

    @pl.loop(0, CHUNKS)
    def _(j):
        for quarter in range(4):
            fetch(j, quarter).start()

    barrier = pltpu.get_barrier_semaphore()
    for step in SPREAD:
        pl.semaphore_signal(barrier, inc=1, device_id=(ring(step), ep), device_id_type=MESH_IDS)

    @pl.loop(1, 32)
    def _(d):
        device = (z, lax.rem(ep + d, 32))
        pl.semaphore_signal(barrier, inc=1, device_id=device, device_id_type=MESH_IDS)

    pl.semaphore_wait(barrier, 34)

    @pl.loop(0, CHUNKS)
    def _(j):
        for quarter in range(4):
            fetch(j, quarter).wait()
        for quarter in range(4):
            span = pl.ds(pl.multiple_of(quarter * QUARTER + j * PAIR, 128), PAIR)

            @pl.loop(0, 5)
            def _(group, quarter=quarter, span=span):
                for two in range(2):
                    slot = group * 4 + two * 2
                    both = jnp.concatenate(
                        [raw[slot, :, span].astype(f32), raw[slot + 1, :, span].astype(f32)], axis=0
                    )
                    place = pl.ds(pl.multiple_of((group * 4 + quarter) * 16 + two * 8, 8), 8)
                    for k in range(PAIR // 128):
                        rows_raw[k, place, :] = both[:, k * 128 : k * 128 + 128]

        for owner in range(4):
            for k in range(PAIR // 128):
                column = pl.ds(pl.multiple_of(j * PAIR + k * 128, 128), 128)
                packed[owner, :, column] = rows_raw[k, pl.ds(owner, 80, stride=4), :].astype(bf16)
        own(j).start()
        for kind in range(3):
            outgoing(kind, j).start()

    @pl.loop(0, 64)
    def _(pair):
        span = pl.ds(pl.multiple_of(pair * PAIR, 128), PAIR)
        both = [query_ref[s, :, span].astype(f32) for s in range(2)]
        both = jnp.concatenate(both, axis=0)
        for k in range(PAIR // 128):
            rows32[k, pl.ds(pl.multiple_of(pair * 8, 8), 8), :] = both[:, k * 128 : k * 128 + 128]

    lane = lax.broadcasted_iota(jnp.int32, (64, WIDE), 1)
    for q in range(4):
        for s in range(2):
            rows = jnp.concatenate(
                [rows32[k, pl.ds(s * 4 + q, 64, stride=8), :] for k in range(PAIR // 128)], axis=1
            )
            even = jnp.where(lane < LATW, rows[:, :WIDE], 0.0)
            odd = jnp.where(lane >= 64, rows[:, PAIR - WIDE :], 0.0)
            for parity, value, shift in ((0, even, 64), (1, odd, WIDE - 64)):
                place = pl.ds(s * 128 + parity * 64, 64)
                moved = pltpu.roll(value, shift, axis=1).astype(bf16)
                value = value.astype(bf16)
                query_even[q, place, :] = value if parity == 0 else moved
                query_odd[q, place, :] = moved if parity == 0 else value

    scale = (NOPE + ROPE) ** (-0.5)
    contract = (((1,), (1,)), ((), ()))

    @pl.loop(0, 4)
    def _(q):
        fresh = fresh_ref[q]
        score = (
            lax.dot_general(query_even[q], fresh, contract, preferred_element_type=f32) * scale
        )
        token = lax.broadcasted_iota(jnp.int32, (256, 128), 1)
        step = lax.broadcasted_iota(jnp.int32, (256, 128), 0) // 128
        score = jnp.where(token <= step, score, masked_score)
        top = jnp.max(score, axis=1, keepdims=True)
        weight = jnp.exp(score - top)
        row_max[q] = jnp.broadcast_to(top, (256, 128))
        row_sum[q] = jnp.broadcast_to(jnp.sum(weight, axis=1, keepdims=True), (256, 128))
        acc_even[q] = jnp.dot(weight.astype(bf16), fresh[:, :LAT], preferred_element_type=f32)
        acc_odd[q] = jnp.zeros((256, WIDE), f32)

    @pl.loop(0, CHUNKS)
    def _(j):
        own(j).wait()
        for kind in range(3):
            arrived(kind, j)

        found = [
            jnp.dot(perm_ref[c], pages[c, :, lanes(j)], preferred_element_type=f32)
            for c in range(4)
        ]
        for quarter in range(4):
            for q in range(4):
                at = quarter * 32 + q * 8
                rows = jnp.concatenate([one[at : at + 8] for one in found], axis=0)
                keys[q, pl.ds(quarter * 32, 32), :] = rows.astype(bf16)

        @pl.loop(0, 4)
        def _(q):
            key = keys[q]
            low, high = key[:, :WIDE], key[:, PAIR - WIDE :]
            score = jnp.concatenate(
                [
                    lax.dot_general(query_even[q], low, contract, preferred_element_type=f32),
                    lax.dot_general(query_odd[q], high, contract, preferred_element_type=f32),
                ],
                axis=1,
            )
            n = lax.broadcasted_iota(jnp.int32, (1, 256), 1)
            fifth = n % 8
            page = 4 * fifth + (n % 32) // 8
            position = page * 64 + 2 * (8 * ((n % 128) // 32) + j) + n // 128
            live = (fifth < 5) & (position < length_ref[q])
            score = jnp.where(live, score * scale, masked_score)
            before = row_max[q]
            top = jnp.maximum(before, jnp.max(score, axis=1, keepdims=True))
            shrink = jnp.exp(before - top)
            weight = jnp.exp(score - jnp.concatenate([top, top], axis=1))
            row_max[q] = top
            row_sum[q] = row_sum[q] * shrink + jnp.sum(weight, axis=1, keepdims=True)
            weight = weight.astype(bf16)
            acc_even[q] = acc_even[q] * shrink[:, :1] + jnp.dot(
                weight[:, :128], low[:, :LAT], preferred_element_type=f32
            )
            acc_odd[q] = acc_odd[q] * shrink[:, :1] + jnp.dot(
                weight[:, 128:], high, preferred_element_type=f32
            )

    for q in range(4):
        value = (acc_even[q] + acc_odd[q][:, 64 : 64 + LAT]) / row_sum[q][:, :1]
        for block in range(4):
            s, parity = block // 2, block % 2
            for k in range(LAT // 128):
                out32[k, pl.ds(parity * 8 + s * 4 + q, 64, stride=16), :] = value[
                    block * 64 : block * 64 + 64, k * 128 : k * 128 + 128
                ]

    @pl.loop(0, 32)
    def _(e):
        for k in range(LAT // 128):
            out16[e, :, pl.ds(k * 128, 128)] = out32[
                k, pl.ds(pl.multiple_of(e * 32, 32), 32), :
            ].astype(bf16)

    def head_copy(d, src, dst, device):
        return pltpu.make_async_remote_copy(
            src_ref=src,
            dst_ref=dst,
            send_sem=head_send.at[d],
            recv_sem=head_recv.at[d],
            device_id=device,
            device_id_type=MESH_IDS,
        )

    def head_block(d):
        target = lax.rem(ep + d, 32)
        return head_copy(d, out16.at[target], heads_ref.at[ep], (z, target))

    @pl.loop(1, 32)
    def _(d):
        head_block(d).start()

    heads_ref[ep] = out16[ep]

    @pl.loop(1, 32)
    def _(d):
        source = heads_ref.at[lax.rem(ep + 32 - d, 32)]
        head_copy(d, source, source, (z, ep)).wait_recv()

    @pl.loop(1, 32)
    def _(d):
        head_block(d).wait_send()

    @pl.loop(0, CHUNKS)
    def _(j):
        for kind in range(3):
            outgoing(kind, j).wait_send()


def attend_call(prefill_pages, page_map, prompt_len, queries, new_latent):
    bf16, f32 = jnp.bfloat16, jnp.float32
    slots, width = prefill_pages.shape[3:]
    row = jnp.arange(32)
    request, fifth = row // 8, row % 8
    wanted = request[None, :] * 20 + 4 * fifth[None, :] + jnp.arange(4)[:, None]
    wanted = jnp.where(fifth[None, :] < 5, wanted, -1)
    slot_hit = (page_map.reshape(4, 1, 5, 1, 4) == wanted[:, :, None, None, None]).astype(bf16)
    same = jnp.eye(4, dtype=bf16)[:, None, None, :, None]
    perm = (slot_hit[:, None] * same).reshape(4, 128, 80)
    fresh = jnp.pad(jnp.swapaxes(new_latent, 0, 1), ((0, 0), (0, 126), (0, WIDE - LATW)))
    vmem, hbm = pl.BlockSpec(memory_space=pltpu.VMEM), pl.BlockSpec(memory_space=pl.ANY)
    return pl.pallas_call(
        attend_kernel,
        out_shape=jax.ShapeDtypeStruct((32, 32, LAT), bf16),
        in_specs=[pl.BlockSpec(memory_space=pltpu.SMEM), hbm, vmem, vmem, vmem],
        out_specs=vmem,
        scratch_shapes=[
            pltpu.VMEM((slots, 4, width), bf16),
            pltpu.VMEM((PAIR // 128, 320, 128), f32),
            pltpu.VMEM((4, 80, QUARTER), bf16),
            pltpu.VMEM((4, 80, QUARTER), bf16),
            pltpu.VMEM((PAIR // 128, 512, 128), f32),
            pltpu.VMEM((4, 256, WIDE), bf16),
            pltpu.VMEM((4, 256, WIDE), bf16),
            pltpu.VMEM((4, 128, PAIR), bf16),
            pltpu.VMEM((4, 256, LAT), f32),
            pltpu.VMEM((4, 256, WIDE), f32),
            pltpu.VMEM((4, 256, 128), f32),
            pltpu.VMEM((4, 256, 128), f32),
            pltpu.VMEM((LAT // 128, 1024, 128), f32),
            pltpu.VMEM((32, 32, LAT), bf16),
            pltpu.SemaphoreType.DMA((CHUNKS, 4)),
            pltpu.SemaphoreType.DMA((CHUNKS,)),
            pltpu.SemaphoreType.DMA((3, CHUNKS)),
            pltpu.SemaphoreType.DMA((3, CHUNKS)),
            pltpu.SemaphoreType.DMA((32,)),
            pltpu.SemaphoreType.DMA((32,)),
        ],
        compiler_params=pltpu.CompilerParams(
            collective_id=2, has_side_effects=True, vmem_limit_bytes=56 * 1024 * 1024
        ),
        cost_estimate=pl.CostEstimate(
            flops=4_000_000_000, bytes_accessed=8_000_000, transcendentals=1_500_000
        ),
        name="attend",
    )(prompt_len, jnp.swapaxes(prefill_pages[0, 0], 0, 1), perm, queries, fresh)


def per_device(
    prefill_pages,
    page_map,
    prompt_len,
    queries,
    new_latent,
    resid,
    w_uv,
    w_out,
    norm_gain,
    router_w,
    routes,
    w_gate,
    w_up,
    w_down,
):
    head_rows = attend_call(prefill_pages, page_map, prompt_len, queries, new_latent)
    operands = layer_operands(resid, routes, w_out, norm_gain, router_w, w_gate, w_up, w_down)
    halves = layer_call(head_rows, w_uv, *operands)
    rows = jnp.swapaxes(halves, 0, 1).astype(jnp.bfloat16)
    return rows.reshape(resid.shape)


def solution(mesh):
    placed = (
        P("ctx", "ep", None, None, None),
        P("ctx", "ep", None, None),
        P(("ctx", "ep")),
        P(None, ("ctx", "ep"), None),
        P(None, ("ctx", "ep"), None),
        P(None, ("ctx", "ep"), None),
        P("ep", None, None),
        P("ep", None),
        P(),
        P(),
        P(None, ("ctx", "ep"), None),
        P("ep", None, "ctx"),
        P("ep", None, "ctx"),
        P("ep", "ctx", None),
    )
    return jax.shard_map(
        per_device,
        mesh=mesh,
        in_specs=placed,
        out_specs=P(None, ("ctx", "ep"), None),
        check_vma=False,
    )
```

```python
import jax
import jax.numpy as jnp
from jax import lax
from jax.experimental import pallas as pl
from jax.experimental.pallas import tpu as pltpu
from jax.sharding import PartitionSpec as P

LAT = 512
ROPE = 64
NOPE = 128
LATW = 576


norm_eps = 1e-06
route_scale = 2.5
masked_score = -1e30

HALF = 3584
GW = HALF + 128
MESH_IDS = pl.DeviceIdType.MESH
AG_PARTS = tuple((640 * i, 384, 256) for i in range(5)) + ((3200, 256, 256),)
AG_SPLIT = 1920
RS_PARTS = (
    (0, 384, 256),
    (640, 384, 256),
    (1280, 256, 256),
    (1792, 384, 256),
    (2432, 384, 256),
    (3072, 256, 256),
)
PLANE_PARTS = tuple((896 * i, 512, 384) for i in range(4))
COPIES = 256


class Links:
    def __init__(self, send_sem, recv_sem):
        self.send_sem, self.recv_sem, self.used = send_sem, recv_sem, 0
        self.z, ep = lax.axis_index("ctx"), lax.axis_index("ep")
        self.core = lax.rem(ep, 2)
        self.y, self.x = ep // 8, lax.rem(ep // 2, 4)
        self.ep = ep
        self.coords = (self.z, self.y, self.x)

    def shifted(self, axis, step):
        return lax.rem(self.coords[axis] + (step % 4), 4)

    def neighbour(self, axis, step):
        c = list(self.coords)
        c[axis] = self.shifted(axis, step)
        return (c[0], (c[1] * 4 + c[2]) * 2 + self.core)

    def partner(self):
        return (self.z, self.ep + 1 - 2 * self.core)

    def take(self, count):
        first = self.used
        self.used += count
        return first

    def send(self, src, dst, device, landing, k=None, start=True):
        if k is None:
            k = self.take(1)
        make = lambda s, d: pltpu.make_async_remote_copy(
            src_ref=s,
            dst_ref=d,
            send_sem=self.send_sem.at[k],
            recv_sem=self.recv_sem.at[k],
            device_id=device,
            device_id_type=MESH_IDS,
        )
        out = make(src, dst)
        if start:
            out.start()
        return out, make(landing, landing)


def wait_in(copies):
    for _, incoming in copies:
        incoming.wait_recv()


def wait_out(copies):
    for outgoing, _ in copies:
        outgoing.wait_send()


def pick(ref, chosen, start, width):
    index = tuple(chosen.get(a, slice(None)) for a in range(len(ref.shape) - 2))
    return ref.at[index + (slice(None), pl.ds(start, width))]


def gather_part(link, held, pushed, index, sent, pushes):
    start, wa, wb = AG_PARTS[index]
    order = [(index + j) % 3 for j in range(3)]

    def push(coord):
        src = pick(held, {order[2]: coord}, start, wa + wb)
        dst = pick(pushed, {order[2]: coord}, start, wa + wb)
        pushes.append(link.send(src, dst, link.partner(), dst))

    for stage in range(3):
        axis = order[stage]
        rest = {a: link.coords[a] for a in order[stage + 1 :]}

        def block(step, lo, w):
            coord = link.shifted(axis, step) if step else link.coords[axis]
            return pick(held, {**rest, axis: coord}, lo, w)

        mine = block(0, start, wa + wb)
        first = (
            link.send(mine, mine, link.neighbour(axis, 1), block(-1, start, wa + wb)),
            link.send(mine, mine, link.neighbour(axis, -1), block(1, start, wa + wb)),
        )
        if stage == 2:
            push(link.coords[axis])
        yield
        wait_in(first)
        up, down = block(-1, start, wa), block(1, start + wa, wb)
        second = (
            link.send(up, up, link.neighbour(axis, 1), block(2, start, wa)),
            link.send(down, down, link.neighbour(axis, -1), block(2, start + wa, wb)),
        )
        if stage == 2:
            push(link.shifted(axis, -1))
            push(link.shifted(axis, 1))
        sent += list(first) + list(second)
        yield
        wait_in(second)
        if stage == 2:
            push(link.shifted(axis, 2))


def scatter_part(link, parts, index, axes, sums, landings, last, sent):
    start, wa, wb = parts[index]
    count = len(axes)
    order = [axes[(index + j) % count] for j in range(count)]
    f32, bf16 = jnp.float32, jnp.bfloat16
    for stage in range(count):
        far_in, low_in, high_in = landings[stage]
        axis = order[stage]
        done = {a: link.coords[a] for a in order[:stage]}

        def at(coord, lo, w):
            return pick(sums, {k - axes[0]: v for k, v in {**done, axis: coord}.items()}, lo, w)

        def land(ref, lo, w):
            return ref.at[(slice(None),) * (count - stage) + (pl.ds(lo, w),)]

        far = link.shifted(axis, 2)
        la, lb = land(far_in, start, wa), land(far_in, start + wa, wb)
        first = (
            link.send(at(far, start, wa), la, link.neighbour(axis, 1), la),
            link.send(at(far, start + wa, wb), lb, link.neighbour(axis, -1), lb),
        )
        yield
        wait_in(first)
        up, down = link.shifted(axis, 1), link.shifted(axis, -1)
        for coord, lo, w in ((up, start, wa), (down, start + wa, wb)):
            view, got = at(coord, lo, w), land(far_in, lo, w)
            view[...] = (view[...].astype(f32) + got[...].astype(f32)).astype(bf16)
        low, high = land(low_in, start, wa + wb), land(high_in, start, wa + wb)
        second = (
            link.send(at(up, start, wa + wb), low, link.neighbour(axis, 1), low),
            link.send(at(down, start, wa + wb), high, link.neighbour(axis, -1), high),
        )
        sent += list(first) + list(second)
        yield
        wait_in(second)
        view = at(link.coords[axis], start, wa + wb)
        total = view[...].astype(f32) + low[...].astype(f32) + high[...].astype(f32)
        if stage == count - 1:
            last(start, wa + wb, total)
        else:
            view[...] = total.astype(bf16)


def resume(threads):
    for thread in threads:
        next(thread, None)


def layer_kernel(
    heads_ref,
    w_uv_ref,
    resid_ref,
    chosen_ref,
    gain_ref,
    router_ref,
    w_out_hbm,
    w_gate_hbm,
    w_up_hbm,
    w_down_hbm,
    out_ref,
    big,
    wg,
    wu,
    wd,
    flat,
    part_send,
    part_land,
    part_sum,
    plane_a0,
    plane_a1,
    plane_b0,
    plane_b1,
    plane_c0,
    plane_c1,
    resid_out,
    hid,
    picked,
    stat_out,
    stat_in,
    held,
    pushed,
    gate_acc,
    up_acc,
    units,
    far0,
    low0,
    high0,
    far1,
    low1,
    high1,
    far2,
    low2,
    high2,
    fin,
    fin_in,
    send_sem,
    recv_sem,
    load_sem,
):
    link = Links(send_sem, recv_sem)
    core = link.core
    other = 1 - core
    partner = link.partner()
    f32, bf16 = jnp.float32, jnp.bfloat16

    own_cols = pl.ds(pl.multiple_of(core * HALF, 128), HALF)
    other_cols = pl.ds(pl.multiple_of(other * HALF, 128), HALF)
    loads = []

    def load(src, dst):
        copy = pltpu.make_async_copy(src, dst, load_sem.at[len(loads)])
        copy.start()
        loads.append(copy)

    load(w_out_hbm.at[:, :, :, :, other_cols], big.at[pl.ds(2, 2)])
    load(w_out_hbm.at[:, :, :, :, own_cols], big.at[pl.ds(0, 2)])
    barrier = pltpu.get_barrier_semaphore()
    for axis in range(3):
        for step in (1, -1):
            pl.semaphore_signal(
                barrier, inc=1, device_id=link.neighbour(axis, step), device_id_type=MESH_IDS
            )
    pl.semaphore_signal(barrier, inc=1, device_id=partner, device_id_type=MESH_IDS)
    pl.semaphore_wait(barrier, 7)

    def token_rows(cols):
        return jnp.concatenate([resid_ref[s, :, cols].astype(f32) for s in range(2)], axis=0)

    resid_out[...] = token_rows(other_cols)
    sent = []
    swaps = [
        link.send(resid_out, hid.at[core], partner, hid.at[other]),
        link.send(chosen_ref, picked.at[core], partner, picked.at[other]),
    ]
    sent += swaps

    for pair in range(2):
        rows = heads_ref[:, pl.ds(pair * 16, 16), :].reshape(512, LAT)
        for one in range(2):
            head = 2 * pair + one
            value = jnp.dot(rows, w_uv_ref[head], preferred_element_type=f32)
            value = value.reshape(32, 2, 8, 128)[:, one].reshape(256, 128)
            flat[:, pl.ds(head * 128, 128)] = value.astype(bf16)

    def project(slot, start):
        lanes = pl.ds(start, 896)
        weight = big[pl.ds(2 * slot, 2), :, :, :, lanes].reshape(512, 896)
        value = jnp.dot(flat[...], weight, preferred_element_type=f32)
        return value.reshape(4, 4, 16, 896)

    loads[0].wait()
    core_swap = []
    for start in (0, 1792):

        @pl.loop(0, 2)
        def _(j, start=start):
            at = pl.multiple_of(start + j * 896, 128)
            part_send[:, :, :, pl.ds(at, 896)] = project(1, at).astype(bf16)

        lanes = pl.ds(start, 1792)
        dst = part_land.at[:, :, :, lanes]
        core_swap.append(link.send(part_send.at[:, :, :, lanes], dst, partner, dst))
    sent += core_swap
    loads[1].wait()
    for slot, cols in ((0, own_cols), (1, other_cols)):
        load(w_gate_hbm.at[cols], wg.at[slot])
        load(w_up_hbm.at[cols], wu.at[slot])
        load(w_down_hbm.at[:, cols], wd.at[slot])

    hid[core] = token_rows(own_cols)
    picked[core] = chosen_ref[...]
    wait_in(swaps)

    def add_hidden(start, width, total):
        lanes = pl.ds(start, width)
        hid[:, :, lanes] = hid[:, :, lanes] + total.reshape(2, 8, width)

    plane_land = ((plane_a0, plane_b0, plane_c0), (plane_a1, plane_b1, plane_c1))
    threads = []
    for turn, start in enumerate((0, 1792)):
        wait_in(core_swap[turn : turn + 1])

        @pl.loop(0, 2)
        def _(j, start=start):
            at = pl.multiple_of(start + j * 896, 128)
            value = project(0, at) + part_land[:, :, :, pl.ds(at, 896)].astype(f32)
            part_sum[:, :, :, pl.ds(at, 896)] = value.astype(bf16)

        for index in (2 * turn, 2 * turn + 1):
            threads.append(
                scatter_part(
                    link, PLANE_PARTS, index, (1, 2), part_sum, plane_land, add_hidden, sent
                )
            )
            next(threads[-1])
    for _ in range(4):
        resume(threads)

    hidden = hid[...].reshape(16, HALF)
    gain = gain_ref[core]
    logits = lax.dot_general(
        (hidden * gain).astype(bf16),
        router_ref[:, own_cols],
        (((1,), (1,)), ((), ())),
        preferred_element_type=f32,
    )
    logits = jnp.concatenate([logits, jnp.zeros((16, 96), f32)], axis=1)
    squares = jnp.sum(hidden * hidden, axis=1, keepdims=True)
    lane = lax.broadcasted_iota(jnp.int32, (16, 128), 1)
    mine = jnp.where(lane < 64, logits, jnp.broadcast_to(squares, (16, 128)))
    stat_out[...] = mine
    stat = link.send(stat_out, stat_in, partner, stat_in)
    sent.append(stat)
    wait_in([stat])
    both = mine + stat_in[...]
    scale = lax.rsqrt(both[:, 64:65] / (2 * HALF) + norm_eps)
    affinity = jax.nn.sigmoid(both * scale) * picked[...].reshape(16, 128)
    weights = route_scale * affinity / jnp.sum(affinity, axis=1, keepdims=True)
    high = weights.astype(bf16)
    low = (weights - high.astype(f32)).astype(bf16).astype(f32)
    table = high.astype(f32) + pltpu.roll(low, 32, axis=1)
    normed = (hid[...].reshape(16, HALF) * scale * gain).astype(bf16)
    held[link.z, link.y, link.x, :, pl.ds(0, HALF)] = normed
    held[link.z, link.y, link.x, :, pl.ds(HALF, 128)] = table.astype(bf16)

    gathers, pushes = [], []
    threads = [gather_part(link, held, pushed, i, gathers, pushes) for i in range(6)]
    for _ in range(6):
        resume(threads)
    resume(threads[:3])
    for copy in loads[2:]:
        copy.wait()

    def own_first(i, carry):
        rows = held[i, :, :, :, pl.ds(0, AG_SPLIT)].reshape(256, AG_SPLIT)
        cut = pl.ds(0, AG_SPLIT)
        gate_acc[i] = jnp.dot(rows, wg[0, cut], preferred_element_type=f32)
        up_acc[i] = jnp.dot(rows, wu[0, cut], preferred_element_type=f32)
        return carry

    lax.fori_loop(0, 4, own_first, 0)
    resume(threads[3:])

    def own_half(i, carry):
        cut = pl.ds(AG_SPLIT, HALF - AG_SPLIT)
        rows = held[i, :, :, :, cut].reshape(256, HALF - AG_SPLIT)
        gate_acc[i] += jnp.dot(rows, wg[0, cut], preferred_element_type=f32)
        up_acc[i] += jnp.dot(rows, wu[0, cut], preferred_element_type=f32)
        return carry

    lax.fori_loop(0, 4, own_half, 0)
    wait_in(pushes)

    def other_half(i, carry):
        rows = pushed[i, :, :, :, pl.ds(0, HALF)].reshape(256, HALF)
        gate_part = gate_acc[i] + jnp.dot(rows, wg[1], preferred_element_type=f32)
        up_part = up_acc[i] + jnp.dot(rows, wu[1], preferred_element_type=f32)
        table = held[i, :, :, :, pl.ds(HALF, 128)].reshape(256, 128).astype(f32)
        lane = lax.broadcasted_iota(jnp.int32, (256, 128), 1)
        here = (lane == link.ep) | (lane == link.ep + 32)
        factor = jnp.sum(jnp.where(here, table, 0.0), axis=1, keepdims=True)
        units[i] = (jax.nn.silu(gate_part) * up_part * factor).astype(bf16)
        return carry

    lax.fori_loop(0, 4, other_half, 0)
    wait_out(gathers + pushes)

    def routed_chunk(slot, i, at):
        weight = wd[slot, :, pl.ds(at, 896)]
        value = jnp.dot(units[i], weight, preferred_element_type=f32)
        return value.reshape(4, 4, 16, 896)

    back_first = link.take(8)

    def back(turn, i, start):
        lanes = pl.ds(1792 * turn, 1792)
        dst = big.at[i, :, :, :, lanes]
        k = back_first + 4 * turn + i
        return link.send(pushed.at[i, :, :, :, lanes], dst, partner, dst, k, start)

    for turn in range(2):

        @pl.loop(0, 4)
        def _(i, turn=turn):
            for at in (1792 * turn, 1792 * turn + 896):
                pushed[i, :, :, :, pl.ds(at, 896)] = routed_chunk(1, i, at).astype(bf16)
            back(turn, i, True)

    def add_routed(start, width, total):
        lanes = pl.ds(start, width)
        fin[:, :, lanes] = hid[:, :, lanes] + total.reshape(2, 8, width)

    torus_land = ((far0, low0, high0), (far1, low1, high1), (far2, low2, high2))
    threads = []
    for turn in range(2):

        @pl.loop(0, 4)
        def _(i, turn=turn):
            wait_in([back(turn, i, False)])
            for at in (1792 * turn, 1792 * turn + 896):
                value = routed_chunk(0, i, at) + big[i, :, :, :, pl.ds(at, 896)].astype(f32)
                held[i, :, :, :, pl.ds(at, 896)] = value.astype(bf16)

        for index in range(3 * turn, 3 * turn + 3):
            threads.append(
                scatter_part(
                    link, RS_PARTS, index, (0, 1, 2), held, torus_land, add_routed, sent
                )
            )
            next(threads[-1])
    for _ in range(6):
        resume(threads)
    swap = link.send(fin.at[other], fin_in, partner, fin_in)
    sent.append(swap)
    for s in range(2):
        out_ref[s, :, own_cols] = fin[core, pl.ds(4 * s, 4)].astype(bf16)
    wait_in([swap])
    for s in range(2):
        out_ref[s, :, other_cols] = fin_in[pl.ds(4 * s, 4)].astype(bf16)
    wait_out(sent)
    for turn in range(2):

        @pl.loop(0, 4)
        def _(i, turn=turn):
            wait_out([back(turn, i, False)])


def layer_call(head_rows, w_uv, resid, chosen, gain, router, w_out, w_gate, w_up, w_down):
    vmem, hbm = pl.BlockSpec(memory_space=pltpu.VMEM), pl.BlockSpec(memory_space=pl.ANY)
    bf16, f32 = jnp.bfloat16, jnp.float32

    def block(*lead, lanes=HALF, kind=bf16):
        return pltpu.VMEM(lead + (lanes,), kind)

    plane = [block(4, 16), block(16)] * 3
    torus = [block(4, 4, 16)] * 3 + [block(4, 16)] * 3 + [block(16)] * 3
    scratch = (
        [block(4, 4, 4, 16)]
        + [pltpu.VMEM((2, HALF, 256), bf16)] * 2
        + [pltpu.VMEM((2, 256, HALF), bf16), pltpu.VMEM((256, 512), bf16)]
        + [block(4, 4, 16)] * 3
        + plane
        + [block(8, kind=f32), block(2, 8, kind=f32), pltpu.VMEM((2, 8, 128), f32)]
        + [pltpu.VMEM((16, 128), f32)] * 2
        + [block(4, 4, 4, 16, lanes=GW)] * 2
        + [pltpu.VMEM((4, 256, 256), f32)] * 2
        + [pltpu.VMEM((4, 256, 256), bf16)]
        + torus
        + [block(2, 8, kind=f32), block(8, kind=f32)]
        + [pltpu.SemaphoreType.DMA((COPIES,))] * 2
        + [pltpu.SemaphoreType.DMA((8,))]
    )
    return pl.pallas_call(
        layer_kernel,
        out_shape=jax.ShapeDtypeStruct((2, 4, 2 * HALF), bf16),
        in_specs=[vmem] * 6 + [hbm] * 4,
        out_specs=vmem,
        scratch_shapes=scratch,
        compiler_params=pltpu.CompilerParams(
            collective_id=1, has_side_effects=True, vmem_limit_bytes=62 * 1024 * 1024
        ),
        cost_estimate=pl.CostEstimate(
            flops=20_000_000_000, bytes_accessed=22_000_000, transcendentals=300_000
        ),
        name="layer",
    )(head_rows, w_uv, resid, chosen, gain, router, w_out, w_gate, w_up, w_down)


def layer_operands(resid, routes, w_out, norm_gain, router_w, w_gate, w_up, w_down):
    route_rows = routes.reshape(8, -1)
    chosen = jnp.any(route_rows[..., None] == jnp.arange(128), axis=1).astype(jnp.float32)
    gain = norm_gain.astype(jnp.float32).reshape(2, 1, HALF)
    return (
        resid,
        chosen,
        gain,
        router_w.T,
        w_out.reshape(2, 4, 4, 16, 2 * HALF),
        w_gate[0],
        w_up[0],
        w_down[0],
    )


CHUNKS = 8
PAIR = 2 * LATW
WIDE = 640
QUARTER = 9216
SPREAD = (2, 1, 3)


def attend_kernel(
    length_ref,
    pages_hbm,
    perm_ref,
    query_ref,
    fresh_ref,
    heads_ref,
    fresh_rows,
    raw,
    rows_raw,
    packed,
    pages,
    rows32,
    query_even,
    query_odd,
    keys,
    acc_even,
    acc_odd,
    row_max,
    row_sum,
    out32,
    out16,
    raw_sem,
    own_sem,
    link_send,
    link_recv,
    head_send,
    head_recv,
):
    f32, bf16 = jnp.float32, jnp.bfloat16
    z, ep = lax.axis_index("ctx"), lax.axis_index("ep")

    def lanes(j):
        return pl.ds(pl.multiple_of(j * PAIR, 128), PAIR)

    def ring(step):
        return lax.rem(z + step, 4)

    def copy(kind, j, src, dst, device):
        return pltpu.make_async_remote_copy(
            src_ref=src,
            dst_ref=dst,
            send_sem=link_send.at[kind, j],
            recv_sem=link_recv.at[kind, j],
            device_id=device,
            device_id_type=MESH_IDS,
        )

    def outgoing(kind, j):
        owner = ring(SPREAD[kind])
        return copy(
            kind, j, packed.at[owner, :, lanes(j)], pages.at[z, :, lanes(j)], (owner, ep)
        )

    def arrived(kind, j):
        producer = ring(4 - SPREAD[kind])
        place = pages.at[producer, :, lanes(j)]
        copy(kind, j, place, place, (producer, ep)).wait_recv()

    def own(j):
        return pltpu.make_async_copy(
            packed.at[z, :, lanes(j)], pages.at[z, :, lanes(j)], own_sem.at[j]
        )

    def fetch(j, quarter):
        span = pl.ds(pl.multiple_of(quarter * QUARTER + j * PAIR, 128), PAIR)
        return pltpu.make_async_copy(
            pages_hbm.at[:, :, span], raw.at[:, :, span], raw_sem.at[j, quarter]
        )

    @pl.loop(0, CHUNKS)
    def _(j):
        for quarter in range(4):
            fetch(j, quarter).start()

    barrier = pltpu.get_barrier_semaphore()
    for step in SPREAD:
        pl.semaphore_signal(barrier, inc=1, device_id=(ring(step), ep), device_id_type=MESH_IDS)

    @pl.loop(1, 32)
    def _(d):
        device = (z, lax.rem(ep + d, 32))
        pl.semaphore_signal(barrier, inc=1, device_id=device, device_id_type=MESH_IDS)

    pl.semaphore_wait(barrier, 34)

    @pl.loop(0, CHUNKS)
    def _(j):
        for quarter in range(4):
            fetch(j, quarter).wait()
        for quarter in range(4):
            span = pl.ds(pl.multiple_of(quarter * QUARTER + j * PAIR, 128), PAIR)

            @pl.loop(0, 5)
            def _(group, quarter=quarter, span=span):
                for two in range(2):
                    slot = group * 4 + two * 2
                    both = jnp.concatenate(
                        [raw[slot, :, span].astype(f32), raw[slot + 1, :, span].astype(f32)], axis=0
                    )
                    place = pl.ds(pl.multiple_of((group * 4 + quarter) * 16 + two * 8, 8), 8)
                    for k in range(PAIR // 128):
                        rows_raw[k, place, :] = both[:, k * 128 : k * 128 + 128]

        for owner in range(4):
            for k in range(PAIR // 128):
                column = pl.ds(pl.multiple_of(j * PAIR + k * 128, 128), 128)
                packed[owner, :, column] = rows_raw[k, pl.ds(owner, 80, stride=4), :].astype(bf16)
        own(j).start()
        for kind in range(3):
            outgoing(kind, j).start()

    @pl.loop(0, 64)
    def _(pair):
        span = pl.ds(pl.multiple_of(pair * PAIR, 128), PAIR)
        both = [query_ref[s, :, span].astype(f32) for s in range(2)]
        both = jnp.concatenate(both, axis=0)
        for k in range(PAIR // 128):
            rows32[k, pl.ds(pl.multiple_of(pair * 8, 8), 8), :] = both[:, k * 128 : k * 128 + 128]

    lane = lax.broadcasted_iota(jnp.int32, (64, WIDE), 1)
    for q in range(4):
        for s in range(2):
            rows = jnp.concatenate(
                [rows32[k, pl.ds(s * 4 + q, 64, stride=8), :] for k in range(PAIR // 128)], axis=1
            )
            even = jnp.where(lane < LATW, rows[:, :WIDE], 0.0)
            odd = jnp.where(lane >= 64, rows[:, PAIR - WIDE :], 0.0)
            for parity, value, shift in ((0, even, 64), (1, odd, WIDE - 64)):
                place = pl.ds(s * 128 + parity * 64, 64)
                moved = pltpu.roll(value, shift, axis=1).astype(bf16)
                value = value.astype(bf16)
                query_even[q, place, :] = value if parity == 0 else moved
                query_odd[q, place, :] = moved if parity == 0 else value

    scale = (NOPE + ROPE) ** (-0.5)
    contract = (((1,), (1,)), ((), ()))

    drawn = [fresh_ref[j].astype(f32) for j in range(2)]
    for q in range(4):
        rows = jnp.concatenate([one[q : q + 1] for one in drawn] + [jnp.zeros((6, LATW), f32)], 0)
        rows = jnp.concatenate([rows, jnp.zeros((8, WIDE - LATW), f32)], axis=1)
        rows = jnp.concatenate([rows, jnp.zeros((120, WIDE), f32)], axis=0)
        fresh_rows[q] = rows.astype(bf16)

    @pl.loop(0, 4)
    def _(q):
        fresh = fresh_rows[q]
        score = (
            lax.dot_general(query_even[q], fresh, contract, preferred_element_type=f32) * scale
        )
        token = lax.broadcasted_iota(jnp.int32, (256, 128), 1)
        step = lax.broadcasted_iota(jnp.int32, (256, 128), 0) // 128
        score = jnp.where(token <= step, score, masked_score)
        top = jnp.max(score, axis=1, keepdims=True)
        weight = jnp.exp(score - top)
        row_max[q] = jnp.broadcast_to(top, (256, 128))
        row_sum[q] = jnp.broadcast_to(jnp.sum(weight, axis=1, keepdims=True), (256, 128))
        acc_even[q] = jnp.dot(weight.astype(bf16), fresh[:, :LAT], preferred_element_type=f32)
        acc_odd[q] = jnp.zeros((256, WIDE), f32)

    @pl.loop(0, CHUNKS)
    def _(j):
        own(j).wait()
        for kind in range(3):
            arrived(kind, j)

        found = [
            jnp.dot(perm_ref[c], pages[c, :, lanes(j)], preferred_element_type=f32)
            for c in range(4)
        ]
        for quarter in range(4):
            for q in range(4):
                at = quarter * 32 + q * 8
                rows = jnp.concatenate([one[at : at + 8] for one in found], axis=0)
                keys[q, pl.ds(quarter * 32, 32), :] = rows.astype(bf16)

        @pl.loop(0, 4)
        def _(q):
            key = keys[q]
            low, high = key[:, :WIDE], key[:, PAIR - WIDE :]
            score = jnp.concatenate(
                [
                    lax.dot_general(query_even[q], low, contract, preferred_element_type=f32),
                    lax.dot_general(query_odd[q], high, contract, preferred_element_type=f32),
                ],
                axis=1,
            )
            n = lax.broadcasted_iota(jnp.int32, (1, 256), 1)
            fifth = n % 8
            page = 4 * fifth + (n % 32) // 8
            position = page * 64 + 2 * (8 * ((n % 128) // 32) + j) + n // 128
            live = (fifth < 5) & (position < length_ref[q])
            score = jnp.where(live, score * scale, masked_score)
            before = row_max[q]
            top = jnp.maximum(before, jnp.max(score, axis=1, keepdims=True))
            shrink = jnp.exp(before - top)
            weight = jnp.exp(score - jnp.concatenate([top, top], axis=1))
            row_max[q] = top
            row_sum[q] = row_sum[q] * shrink + jnp.sum(weight, axis=1, keepdims=True)
            weight = weight.astype(bf16)
            acc_even[q] = acc_even[q] * shrink[:, :1] + jnp.dot(
                weight[:, :128], low[:, :LAT], preferred_element_type=f32
            )
            acc_odd[q] = acc_odd[q] * shrink[:, :1] + jnp.dot(
                weight[:, 128:], high, preferred_element_type=f32
            )

    for q in range(4):
        value = (acc_even[q] + acc_odd[q][:, 64 : 64 + LAT]) / row_sum[q][:, :1]
        for block in range(4):
            s, parity = block // 2, block % 2
            for k in range(LAT // 128):
                out32[k, pl.ds(parity * 8 + s * 4 + q, 64, stride=16), :] = value[
                    block * 64 : block * 64 + 64, k * 128 : k * 128 + 128
                ]

    @pl.loop(0, 32)
    def _(e):
        for k in range(LAT // 128):
            out16[e, :, pl.ds(k * 128, 128)] = out32[
                k, pl.ds(pl.multiple_of(e * 32, 32), 32), :
            ].astype(bf16)

    def head_copy(d, src, dst, device):
        return pltpu.make_async_remote_copy(
            src_ref=src,
            dst_ref=dst,
            send_sem=head_send.at[d],
            recv_sem=head_recv.at[d],
            device_id=device,
            device_id_type=MESH_IDS,
        )

    def head_block(d):
        target = lax.rem(ep + d, 32)
        return head_copy(d, out16.at[target], heads_ref.at[ep], (z, target))

    @pl.loop(1, 32)
    def _(d):
        head_block(d).start()

    heads_ref[ep] = out16[ep]

    @pl.loop(1, 32)
    def _(d):
        source = heads_ref.at[lax.rem(ep + 32 - d, 32)]
        head_copy(d, source, source, (z, ep)).wait_recv()

    @pl.loop(1, 32)
    def _(d):
        head_block(d).wait_send()

    @pl.loop(0, CHUNKS)
    def _(j):
        for kind in range(3):
            outgoing(kind, j).wait_send()


def attend_call(prefill_pages, page_map, prompt_len, queries, new_latent):
    bf16, f32 = jnp.bfloat16, jnp.float32
    slots, width = prefill_pages.shape[3:]
    row = jnp.arange(32)
    request, fifth = row // 8, row % 8
    wanted = request[None, :] * 20 + 4 * fifth[None, :] + jnp.arange(4)[:, None]
    wanted = jnp.where(fifth[None, :] < 5, wanted, -1)
    slot_hit = (page_map.reshape(4, 1, 5, 1, 4) == wanted[:, :, None, None, None]).astype(bf16)
    same = jnp.eye(4, dtype=bf16)[:, None, None, :, None]
    perm = (slot_hit[:, None] * same).reshape(4, 128, 80)
    vmem, hbm = pl.BlockSpec(memory_space=pltpu.VMEM), pl.BlockSpec(memory_space=pl.ANY)
    return pl.pallas_call(
        attend_kernel,
        out_shape=jax.ShapeDtypeStruct((32, 32, LAT), bf16),
        in_specs=[pl.BlockSpec(memory_space=pltpu.SMEM), hbm, vmem, vmem, vmem],
        out_specs=vmem,
        scratch_shapes=[
            pltpu.VMEM((4, 128, WIDE), bf16),
            pltpu.VMEM((slots, 4, width), bf16),
            pltpu.VMEM((PAIR // 128, 320, 128), f32),
            pltpu.VMEM((4, 80, QUARTER), bf16),
            pltpu.VMEM((4, 80, QUARTER), bf16),
            pltpu.VMEM((PAIR // 128, 512, 128), f32),
            pltpu.VMEM((4, 256, WIDE), bf16),
            pltpu.VMEM((4, 256, WIDE), bf16),
            pltpu.VMEM((4, 128, PAIR), bf16),
            pltpu.VMEM((4, 256, LAT), f32),
            pltpu.VMEM((4, 256, WIDE), f32),
            pltpu.VMEM((4, 256, 128), f32),
            pltpu.VMEM((4, 256, 128), f32),
            pltpu.VMEM((LAT // 128, 1024, 128), f32),
            pltpu.VMEM((32, 32, LAT), bf16),
            pltpu.SemaphoreType.DMA((CHUNKS, 4)),
            pltpu.SemaphoreType.DMA((CHUNKS,)),
            pltpu.SemaphoreType.DMA((3, CHUNKS)),
            pltpu.SemaphoreType.DMA((3, CHUNKS)),
            pltpu.SemaphoreType.DMA((32,)),
            pltpu.SemaphoreType.DMA((32,)),
        ],
        compiler_params=pltpu.CompilerParams(
            collective_id=2, has_side_effects=True, vmem_limit_bytes=56 * 1024 * 1024
        ),
        cost_estimate=pl.CostEstimate(
            flops=4_000_000_000, bytes_accessed=8_000_000, transcendentals=1_500_000
        ),
        name="attend",
    )(prompt_len, jnp.swapaxes(prefill_pages[0, 0], 0, 1), perm, queries, new_latent)


def per_device(
    prefill_pages,
    page_map,
    prompt_len,
    queries,
    new_latent,
    resid,
    w_uv,
    w_out,
    norm_gain,
    router_w,
    routes,
    w_gate,
    w_up,
    w_down,
):
    head_rows = attend_call(prefill_pages, page_map, prompt_len, queries, new_latent)
    operands = layer_operands(resid, routes, w_out, norm_gain, router_w, w_gate, w_up, w_down)
    return layer_call(head_rows, w_uv, *operands)


def solution(mesh):
    placed = (
        P("ctx", "ep", None, None, None),
        P("ctx", "ep", None, None),
        P(("ctx", "ep")),
        P(None, ("ctx", "ep"), None),
        P(None, ("ctx", "ep"), None),
        P(None, ("ctx", "ep"), None),
        P("ep", None, None),
        P("ep", None),
        P(),
        P(),
        P(None, ("ctx", "ep"), None),
        P("ep", None, "ctx"),
        P("ep", None, "ctx"),
        P("ep", "ctx", None),
    )
    return jax.shard_map(
        per_device,
        mesh=mesh,
        in_specs=placed,
        out_specs=P(None, ("ctx", "ep"), None),
        check_vma=False,
    )
```

```python
import jax
import jax.numpy as jnp
from jax import lax
from jax.experimental import pallas as pl
from jax.experimental.pallas import tpu as pltpu
from jax.sharding import PartitionSpec as P

LAT = 512
ROPE = 64
NOPE = 128
LATW = 576


norm_eps = 1e-06
route_scale = 2.5
masked_score = -1e30

HALF = 3584
GW = HALF + 128
MESH_IDS = pl.DeviceIdType.MESH
AG_PARTS = tuple((640 * i, 384, 256) for i in range(5)) + ((3200, 256, 256),)
AG_SPLIT = 1920
GENERATIONS = ((0, 896), (896, 2688))
RS_PARTS = (
    (0, 128, 128),
    (256, 128, 128),
    (512, 256, 128),
    (896, 512, 384),
    (1792, 512, 384),
    (2688, 512, 384),
)
PLANE_PARTS = ((0, 256, 256), (512, 256, 128), (896, 768, 640), (2304, 640, 640))
COPIES = 256


class Links:
    def __init__(self, send_sem, recv_sem):
        self.send_sem, self.recv_sem, self.used = send_sem, recv_sem, 0
        self.z, ep = lax.axis_index("ctx"), lax.axis_index("ep")
        self.core = lax.rem(ep, 2)
        self.y, self.x = ep // 8, lax.rem(ep // 2, 4)
        self.ep = ep
        self.coords = (self.z, self.y, self.x)

    def shifted(self, axis, step):
        return lax.rem(self.coords[axis] + (step % 4), 4)

    def neighbour(self, axis, step):
        c = list(self.coords)
        c[axis] = self.shifted(axis, step)
        return (c[0], (c[1] * 4 + c[2]) * 2 + self.core)

    def partner(self):
        return (self.z, self.ep + 1 - 2 * self.core)

    def take(self, count):
        first = self.used
        self.used += count
        return first

    def send(self, src, dst, device, landing, k=None, start=True):
        if k is None:
            k = self.take(1)
        make = lambda s, d: pltpu.make_async_remote_copy(
            src_ref=s,
            dst_ref=d,
            send_sem=self.send_sem.at[k],
            recv_sem=self.recv_sem.at[k],
            device_id=device,
            device_id_type=MESH_IDS,
        )
        out = make(src, dst)
        if start:
            out.start()
        return out, make(landing, landing)


def wait_in(copies):
    for _, incoming in copies:
        incoming.wait_recv()


def wait_out(copies):
    for outgoing, _ in copies:
        outgoing.wait_send()


def pick(ref, chosen, start, width):
    index = tuple(chosen.get(a, slice(None)) for a in range(len(ref.shape) - 2))
    return ref.at[index + (slice(None), pl.ds(start, width))]


def gather_part(link, held, pushed, index, sent, pushes):
    start, wa, wb = AG_PARTS[index]
    order = [(index + j) % 3 for j in range(3)]

    def push(coord):
        src = pick(held, {order[2]: coord}, start, wa + wb)
        dst = pick(pushed, {order[2]: coord}, start, wa + wb)
        pushes.append(link.send(src, dst, link.partner(), dst))

    for stage in range(3):
        axis = order[stage]
        rest = {a: link.coords[a] for a in order[stage + 1 :]}

        def block(step, lo, w):
            coord = link.shifted(axis, step) if step else link.coords[axis]
            return pick(held, {**rest, axis: coord}, lo, w)

        mine = block(0, start, wa + wb)
        if stage == 0:
            near = [
                link.send(mine, mine, link.neighbour(axis, step), block(-step, start, wa + wb))
                for step in (2, 1, -1)
            ]
            sent += near
            yield
            wait_in(near)
            continue
        first = (
            link.send(mine, mine, link.neighbour(axis, 1), block(-1, start, wa + wb)),
            link.send(mine, mine, link.neighbour(axis, -1), block(1, start, wa + wb)),
        )
        if stage == 2:
            push(link.coords[axis])
        yield
        wait_in(first)
        up, down = block(-1, start, wa), block(1, start + wa, wb)
        second = (
            link.send(up, up, link.neighbour(axis, 1), block(2, start, wa)),
            link.send(down, down, link.neighbour(axis, -1), block(2, start + wa, wb)),
        )
        if stage == 2:
            push(link.shifted(axis, -1))
            push(link.shifted(axis, 1))
        sent += list(first) + list(second)
        yield
        wait_in(second)
        if stage == 2:
            push(link.shifted(axis, 2))


def scatter_part(link, parts, index, axes, sums, landings, last, sent):
    start, wa, wb = parts[index]
    count = len(axes)
    order = [axes[(index + j) % count] for j in range(count)]
    f32, bf16 = jnp.float32, jnp.bfloat16
    for stage in range(count):
        far_in, low_in, high_in = landings[stage]
        axis = order[stage]
        done = {a: link.coords[a] for a in order[:stage]}

        def at(coord, lo, w):
            return pick(sums, {k - axes[0]: v for k, v in {**done, axis: coord}.items()}, lo, w)

        def land(ref, lo, w):
            return ref.at[(slice(None),) * (count - stage) + (pl.ds(lo, w),)]

        far = link.shifted(axis, 2)
        if stage == count - 1:
            whole = (start, wa + wb)
            near = []
            for ref, step in ((far_in, 2), (low_in, 1), (high_in, -1)):
                place = land(ref, *whole)
                src = at(link.shifted(axis, step), *whole)
                near.append(link.send(src, place, link.neighbour(axis, step), place))
            sent += near
            yield
            wait_in(near)
            total = at(link.coords[axis], *whole)[...].astype(f32)
            for ref in (far_in, low_in, high_in):
                total = total + land(ref, *whole)[...].astype(f32)
            last(start, wa + wb, total)
            continue
        la, lb = land(far_in, start, wa), land(far_in, start + wa, wb)
        first = (
            link.send(at(far, start, wa), la, link.neighbour(axis, 1), la),
            link.send(at(far, start + wa, wb), lb, link.neighbour(axis, -1), lb),
        )
        yield
        wait_in(first)
        up, down = link.shifted(axis, 1), link.shifted(axis, -1)
        for coord, lo, w in ((up, start, wa), (down, start + wa, wb)):
            view, got = at(coord, lo, w), land(far_in, lo, w)
            view[...] = (view[...].astype(f32) + got[...].astype(f32)).astype(bf16)
        low, high = land(low_in, start, wa + wb), land(high_in, start, wa + wb)
        second = (
            link.send(at(up, start, wa + wb), low, link.neighbour(axis, 1), low),
            link.send(at(down, start, wa + wb), high, link.neighbour(axis, -1), high),
        )
        sent += list(first) + list(second)
        yield
        wait_in(second)
        view = at(link.coords[axis], start, wa + wb)
        total = view[...].astype(f32) + low[...].astype(f32) + high[...].astype(f32)
        view[...] = total.astype(bf16)


def resume(threads):
    for thread in threads:
        next(thread, None)


def layer_kernel(
    heads_ref,
    w_uv_ref,
    resid_ref,
    chosen_ref,
    gain_ref,
    router_ref,
    w_out_hbm,
    w_gate_hbm,
    w_up_hbm,
    w_down_hbm,
    out_ref,
    big,
    wg,
    wu,
    wd,
    flat,
    part_send,
    part_land,
    part_sum,
    plane_a0,
    plane_a1,
    plane_b0,
    plane_b1,
    plane_c0,
    plane_c1,
    resid_out,
    hid,
    picked,
    stat_out,
    stat_in,
    held,
    pushed,
    gate_acc,
    up_acc,
    units,
    far0,
    low0,
    high0,
    far1,
    low1,
    high1,
    far2,
    low2,
    high2,
    fin,
    fin_in,
    send_sem,
    recv_sem,
    load_sem,
):
    link = Links(send_sem, recv_sem)
    core = link.core
    other = 1 - core
    partner = link.partner()
    f32, bf16 = jnp.float32, jnp.bfloat16

    own_cols = pl.ds(pl.multiple_of(core * HALF, 128), HALF)
    other_cols = pl.ds(pl.multiple_of(other * HALF, 128), HALF)
    loads = []

    def load(src, dst):
        copy = pltpu.make_async_copy(src, dst, load_sem.at[len(loads)])
        copy.start()
        loads.append(copy)

    load(w_out_hbm.at[:, :, :, :, other_cols], big.at[pl.ds(2, 2)])
    load(w_out_hbm.at[:, :, :, :, own_cols], big.at[pl.ds(0, 2)])
    barrier = pltpu.get_barrier_semaphore()
    for axis in range(3):
        for step in (1, -1, 2):
            pl.semaphore_signal(
                barrier, inc=1, device_id=link.neighbour(axis, step), device_id_type=MESH_IDS
            )
    pl.semaphore_signal(barrier, inc=1, device_id=partner, device_id_type=MESH_IDS)

    for pair in range(2):
        rows = heads_ref[:, pl.ds(pair * 16, 16), :].reshape(512, LAT)
        for one in range(2):
            head = 2 * pair + one
            value = jnp.dot(rows, w_uv_ref[head], preferred_element_type=f32)
            value = value.reshape(32, 2, 8, 128)[:, one].reshape(256, 128)
            flat[:, pl.ds(head * 128, 128)] = value.astype(bf16)

    def project(slot, start):
        lanes = pl.ds(start, 896)
        weight = big[pl.ds(2 * slot, 2), :, :, :, lanes].reshape(512, 896)
        value = jnp.dot(flat[...], weight, preferred_element_type=f32)
        return value.reshape(4, 4, 16, 896)

    def project_away(start, width):
        @pl.loop(0, width // 896)
        def _(j):
            at = pl.multiple_of(start + j * 896, 128)
            part_send[:, :, :, pl.ds(at, 896)] = project(1, at).astype(bf16)

    def swap_sums(start, width):
        lanes = pl.ds(start, width)
        dst = part_land.at[:, :, :, lanes]
        return link.send(part_send.at[:, :, :, lanes], dst, partner, dst)

    loads[0].wait()
    project_away(*GENERATIONS[0])
    pl.semaphore_wait(barrier, 10)

    def token_rows(cols):
        return jnp.concatenate([resid_ref[s, :, cols].astype(f32) for s in range(2)], axis=0)

    resid_out[...] = token_rows(other_cols)
    sent = []
    swaps = [
        link.send(resid_out, hid.at[core], partner, hid.at[other]),
        link.send(chosen_ref, picked.at[core], partner, picked.at[other]),
    ]
    sent += swaps

    core_swap = [swap_sums(*GENERATIONS[0])]
    project_away(*GENERATIONS[1])
    core_swap.append(swap_sums(*GENERATIONS[1]))
    sent += core_swap
    loads[1].wait()
    for slot, cols in ((0, own_cols), (1, other_cols)):
        load(w_gate_hbm.at[cols], wg.at[slot])
        load(w_up_hbm.at[cols], wu.at[slot])
        load(w_down_hbm.at[:, cols], wd.at[slot])

    hid[core] = token_rows(own_cols)
    picked[core] = chosen_ref[...]
    wait_in(swaps)

    def add_hidden(start, width, total):
        lanes = pl.ds(start, width)
        hid[:, :, lanes] = hid[:, :, lanes] + total.reshape(2, 8, width)

    plane_land = ((plane_a0, plane_b0, plane_c0), (plane_a1, plane_b1, plane_c1))
    threads = []
    for turn, (start, width) in enumerate(GENERATIONS):
        wait_in(core_swap[turn : turn + 1])

        @pl.loop(0, width // 896)
        def _(j, start=start):
            at = pl.multiple_of(start + j * 896, 128)
            value = project(0, at) + part_land[:, :, :, pl.ds(at, 896)].astype(f32)
            part_sum[:, :, :, pl.ds(at, 896)] = value.astype(bf16)

        for index in (2 * turn, 2 * turn + 1):
            threads.append(
                scatter_part(
                    link, PLANE_PARTS, index, (1, 2), part_sum, plane_land, add_hidden, sent
                )
            )
            next(threads[-1])
    for _ in range(3):
        resume(threads)

    hidden = hid[...].reshape(16, HALF)
    gain = gain_ref[core]
    logits = lax.dot_general(
        (hidden * gain).astype(bf16),
        router_ref[:, own_cols],
        (((1,), (1,)), ((), ())),
        preferred_element_type=f32,
    )
    logits = jnp.concatenate([logits, jnp.zeros((16, 96), f32)], axis=1)
    squares = jnp.sum(hidden * hidden, axis=1, keepdims=True)
    lane = lax.broadcasted_iota(jnp.int32, (16, 128), 1)
    mine = jnp.where(lane < 64, logits, jnp.broadcast_to(squares, (16, 128)))
    stat_out[...] = mine
    stat = link.send(stat_out, stat_in, partner, stat_in)
    sent.append(stat)
    wait_in([stat])
    both = mine + stat_in[...]
    scale = lax.rsqrt(both[:, 64:65] / (2 * HALF) + norm_eps)
    affinity = jax.nn.sigmoid(both * scale) * picked[...].reshape(16, 128)
    weights = route_scale * affinity / jnp.sum(affinity, axis=1, keepdims=True)
    high = weights.astype(bf16)
    low = (weights - high.astype(f32)).astype(bf16).astype(f32)
    table = high.astype(f32) + pltpu.roll(low, 32, axis=1)
    normed = (hid[...].reshape(16, HALF) * scale * gain).astype(bf16)
    held[link.z, link.y, link.x, :, pl.ds(0, HALF)] = normed
    held[link.z, link.y, link.x, :, pl.ds(HALF, 128)] = table.astype(bf16)

    gathers, pushes = [], []
    threads = [gather_part(link, held, pushed, i, gathers, pushes) for i in range(6)]
    for _ in range(5):
        resume(threads)
    resume(threads[:3])
    for copy in loads[2:]:
        copy.wait()

    def own_first(i, carry):
        rows = held[i, :, :, :, pl.ds(0, AG_SPLIT)].reshape(256, AG_SPLIT)
        cut = pl.ds(0, AG_SPLIT)
        gate_acc[i] = jnp.dot(rows, wg[0, cut], preferred_element_type=f32)
        up_acc[i] = jnp.dot(rows, wu[0, cut], preferred_element_type=f32)
        return carry

    lax.fori_loop(0, 4, own_first, 0)
    resume(threads[3:])

    def own_half(i, carry):
        cut = pl.ds(AG_SPLIT, HALF - AG_SPLIT)
        rows = held[i, :, :, :, cut].reshape(256, HALF - AG_SPLIT)
        gate_acc[i] += jnp.dot(rows, wg[0, cut], preferred_element_type=f32)
        up_acc[i] += jnp.dot(rows, wu[0, cut], preferred_element_type=f32)
        return carry

    lax.fori_loop(0, 4, own_half, 0)
    wait_in(pushes)

    def other_half(i, carry):
        rows = pushed[i, :, :, :, pl.ds(0, HALF)].reshape(256, HALF)
        gate_part = gate_acc[i] + jnp.dot(rows, wg[1], preferred_element_type=f32)
        up_part = up_acc[i] + jnp.dot(rows, wu[1], preferred_element_type=f32)
        table = held[i, :, :, :, pl.ds(HALF, 128)].reshape(256, 128).astype(f32)
        lane = lax.broadcasted_iota(jnp.int32, (256, 128), 1)
        here = (lane == link.ep) | (lane == link.ep + 32)
        factor = jnp.sum(jnp.where(here, table, 0.0), axis=1, keepdims=True)
        units[i] = (jax.nn.silu(gate_part) * up_part * factor).astype(bf16)
        return carry

    lax.fori_loop(0, 4, other_half, 0)
    wait_out(gathers + pushes)

    def routed_chunk(slot, i, at):
        weight = wd[slot, :, pl.ds(at, 896)]
        value = jnp.dot(units[i], weight, preferred_element_type=f32)
        return value.reshape(4, 4, 16, 896)

    chunks = [range(start, start + width, 896) for start, width in GENERATIONS]
    back_first = link.take(8)

    def back(turn, i, start):
        lanes = pl.ds(*GENERATIONS[turn])
        dst = big.at[i, :, :, :, lanes]
        k = back_first + 4 * turn + i
        return link.send(pushed.at[i, :, :, :, lanes], dst, partner, dst, k, start)

    for turn in range(2):

        @pl.loop(0, 4)
        def _(i, turn=turn):
            for at in chunks[turn]:
                pushed[i, :, :, :, pl.ds(at, 896)] = routed_chunk(1, i, at).astype(bf16)
            back(turn, i, True)

    def add_routed(start, width, total):
        lanes = pl.ds(start, width)
        fin[:, :, lanes] = hid[:, :, lanes] + total.reshape(2, 8, width)

    torus_land = ((far0, low0, high0), (far1, low1, high1), (far2, low2, high2))
    threads = []
    for turn in range(2):

        @pl.loop(0, 4)
        def _(i, turn=turn):
            wait_in([back(turn, i, False)])
            for at in chunks[turn]:
                value = routed_chunk(0, i, at) + big[i, :, :, :, pl.ds(at, 896)].astype(f32)
                held[i, :, :, :, pl.ds(at, 896)] = value.astype(bf16)

        for index in range(3 * turn, 3 * turn + 3):
            threads.append(
                scatter_part(
                    link, RS_PARTS, index, (0, 1, 2), held, torus_land, add_routed, sent
                )
            )
            next(threads[-1])
    for _ in range(5):
        resume(threads)
    swap = link.send(fin.at[other], fin_in, partner, fin_in)
    sent.append(swap)
    for s in range(2):
        out_ref[s, :, own_cols] = fin[core, pl.ds(4 * s, 4)].astype(bf16)
    wait_in([swap])
    for s in range(2):
        out_ref[s, :, other_cols] = fin_in[pl.ds(4 * s, 4)].astype(bf16)
    wait_out(sent)
    for turn in range(2):

        @pl.loop(0, 4)
        def _(i, turn=turn):
            wait_out([back(turn, i, False)])


def layer_call(head_rows, w_uv, resid, chosen, gain, router, w_out, w_gate, w_up, w_down):
    vmem, hbm = pl.BlockSpec(memory_space=pltpu.VMEM), pl.BlockSpec(memory_space=pl.ANY)
    bf16, f32 = jnp.bfloat16, jnp.float32

    def block(*lead, lanes=HALF, kind=bf16):
        return pltpu.VMEM(lead + (lanes,), kind)

    plane = [block(4, 16), block(16)] * 3
    torus = [block(4, 4, 16)] * 3 + [block(4, 16)] * 3 + [block(16)] * 3
    scratch = (
        [block(4, 4, 4, 16)]
        + [pltpu.VMEM((2, HALF, 256), bf16)] * 2
        + [pltpu.VMEM((2, 256, HALF), bf16), pltpu.VMEM((256, 512), bf16)]
        + [block(4, 4, 16)] * 3
        + plane
        + [block(8, kind=f32), block(2, 8, kind=f32), pltpu.VMEM((2, 8, 128), f32)]
        + [pltpu.VMEM((16, 128), f32)] * 2
        + [block(4, 4, 4, 16, lanes=GW)] * 2
        + [pltpu.VMEM((4, 256, 256), f32)] * 2
        + [pltpu.VMEM((4, 256, 256), bf16)]
        + torus
        + [block(2, 8, kind=f32), block(8, kind=f32)]
        + [pltpu.SemaphoreType.DMA((COPIES,))] * 2
        + [pltpu.SemaphoreType.DMA((8,))]
    )
    return pl.pallas_call(
        layer_kernel,
        out_shape=jax.ShapeDtypeStruct((2, 4, 2 * HALF), bf16),
        in_specs=[vmem] * 6 + [hbm] * 4,
        out_specs=vmem,
        scratch_shapes=scratch,
        compiler_params=pltpu.CompilerParams(
            collective_id=1, has_side_effects=True, vmem_limit_bytes=62 * 1024 * 1024
        ),
        cost_estimate=pl.CostEstimate(
            flops=20_000_000_000, bytes_accessed=22_000_000, transcendentals=300_000
        ),
        name="layer",
    )(head_rows, w_uv, resid, chosen, gain, router, w_out, w_gate, w_up, w_down)


def layer_operands(resid, routes, w_out, norm_gain, router_w, w_gate, w_up, w_down):
    route_rows = routes.reshape(8, -1)
    chosen = jnp.any(route_rows[..., None] == jnp.arange(128), axis=1).astype(jnp.float32)
    gain = norm_gain.astype(jnp.float32).reshape(2, 1, HALF)
    return (
        resid,
        chosen,
        gain,
        router_w.T,
        w_out.reshape(2, 4, 4, 16, 2 * HALF),
        w_gate[0],
        w_up[0],
        w_down[0],
    )


CHUNKS = 8
PAIR = 2 * LATW
WIDE = 640
QUARTER = 9216
SPREAD = (2, 1, 3)


def attend_kernel(
    length_ref,
    pages_hbm,
    perm_ref,
    query_ref,
    fresh_ref,
    heads_ref,
    fresh_rows,
    raw,
    rows_raw,
    packed,
    pages,
    rows32,
    query_even,
    query_odd,
    keys,
    acc_even,
    acc_odd,
    row_max,
    row_sum,
    out32,
    out16,
    raw_sem,
    own_sem,
    link_send,
    link_recv,
    head_send,
    head_recv,
):
    f32, bf16 = jnp.float32, jnp.bfloat16
    z, ep = lax.axis_index("ctx"), lax.axis_index("ep")

    def lanes(j):
        return pl.ds(pl.multiple_of(j * PAIR, 128), PAIR)

    def ring(step):
        return lax.rem(z + step, 4)

    def copy(kind, j, src, dst, device):
        return pltpu.make_async_remote_copy(
            src_ref=src,
            dst_ref=dst,
            send_sem=link_send.at[kind, j],
            recv_sem=link_recv.at[kind, j],
            device_id=device,
            device_id_type=MESH_IDS,
        )

    def outgoing(kind, j):
        owner = ring(SPREAD[kind])
        return copy(
            kind, j, packed.at[owner, :, lanes(j)], pages.at[z, :, lanes(j)], (owner, ep)
        )

    def arrived(kind, j):
        producer = ring(4 - SPREAD[kind])
        place = pages.at[producer, :, lanes(j)]
        copy(kind, j, place, place, (producer, ep)).wait_recv()

    def own(j):
        return pltpu.make_async_copy(
            packed.at[z, :, lanes(j)], pages.at[z, :, lanes(j)], own_sem.at[j]
        )

    def fetch(j, quarter):
        span = pl.ds(pl.multiple_of(quarter * QUARTER + j * PAIR, 128), PAIR)
        return pltpu.make_async_copy(
            pages_hbm.at[:, :, span], raw.at[:, :, span], raw_sem.at[j, quarter]
        )

    @pl.loop(0, CHUNKS)
    def _(j):
        for quarter in range(4):
            fetch(j, quarter).start()

    barrier = pltpu.get_barrier_semaphore()
    for step in SPREAD:
        pl.semaphore_signal(barrier, inc=1, device_id=(ring(step), ep), device_id_type=MESH_IDS)

    @pl.loop(1, 32)
    def _(d):
        device = (z, lax.rem(ep + d, 32))
        pl.semaphore_signal(barrier, inc=1, device_id=device, device_id_type=MESH_IDS)


    def repack(j):
        for quarter in range(4):
            fetch(j, quarter).wait()
        for quarter in range(4):
            span = pl.ds(pl.multiple_of(quarter * QUARTER + j * PAIR, 128), PAIR)

            @pl.loop(0, 5)
            def _(group, quarter=quarter, span=span):
                for two in range(2):
                    slot = group * 4 + two * 2
                    both = jnp.concatenate(
                        [raw[slot, :, span].astype(f32), raw[slot + 1, :, span].astype(f32)], axis=0
                    )
                    place = pl.ds(pl.multiple_of((group * 4 + quarter) * 16 + two * 8, 8), 8)
                    for k in range(PAIR // 128):
                        rows_raw[k, place, :] = both[:, k * 128 : k * 128 + 128]

        for owner in range(4):
            for k in range(PAIR // 128):
                column = pl.ds(pl.multiple_of(j * PAIR + k * 128, 128), 128)
                packed[owner, :, column] = rows_raw[k, pl.ds(owner, 80, stride=4), :].astype(bf16)

    repack(0)
    pl.semaphore_wait(barrier, 34)

    @pl.loop(0, CHUNKS)
    def _(j):
        for kind in range(3):
            outgoing(kind, j).start()
        own(j).start()

        @pl.when(j + 1 < CHUNKS)
        def _():
            repack(j + 1)

    @pl.loop(0, 64)
    def _(pair):
        span = pl.ds(pl.multiple_of(pair * PAIR, 128), PAIR)
        both = [query_ref[s, :, span].astype(f32) for s in range(2)]
        both = jnp.concatenate(both, axis=0)
        for k in range(PAIR // 128):
            rows32[k, pl.ds(pl.multiple_of(pair * 8, 8), 8), :] = both[:, k * 128 : k * 128 + 128]

    lane = lax.broadcasted_iota(jnp.int32, (64, WIDE), 1)
    for q in range(4):
        for s in range(2):
            rows = jnp.concatenate(
                [rows32[k, pl.ds(s * 4 + q, 64, stride=8), :] for k in range(PAIR // 128)], axis=1
            )
            even = jnp.where(lane < LATW, rows[:, :WIDE], 0.0)
            odd = jnp.where(lane >= 64, rows[:, PAIR - WIDE :], 0.0)
            for parity, value, shift in ((0, even, 64), (1, odd, WIDE - 64)):
                place = pl.ds(s * 128 + parity * 64, 64)
                moved = pltpu.roll(value, shift, axis=1).astype(bf16)
                value = value.astype(bf16)
                query_even[q, place, :] = value if parity == 0 else moved
                query_odd[q, place, :] = moved if parity == 0 else value

    scale = (NOPE + ROPE) ** (-0.5)
    contract = (((1,), (1,)), ((), ()))

    drawn = [fresh_ref[j].astype(f32) for j in range(2)]
    for q in range(4):
        rows = jnp.concatenate([one[q : q + 1] for one in drawn] + [jnp.zeros((6, LATW), f32)], 0)
        rows = jnp.concatenate([rows, jnp.zeros((8, WIDE - LATW), f32)], axis=1)
        rows = jnp.concatenate([rows, jnp.zeros((120, WIDE), f32)], axis=0)
        fresh_rows[q] = rows.astype(bf16)

    @pl.loop(0, 4)
    def _(q):
        fresh = fresh_rows[q]
        score = (
            lax.dot_general(query_even[q], fresh, contract, preferred_element_type=f32) * scale
        )
        token = lax.broadcasted_iota(jnp.int32, (256, 128), 1)
        step = lax.broadcasted_iota(jnp.int32, (256, 128), 0) // 128
        score = jnp.where(token <= step, score, masked_score)
        top = jnp.max(score, axis=1, keepdims=True)
        weight = jnp.exp(score - top)
        row_max[q] = jnp.broadcast_to(top, (256, 128))
        row_sum[q] = jnp.broadcast_to(jnp.sum(weight, axis=1, keepdims=True), (256, 128))
        acc_even[q] = jnp.dot(weight.astype(bf16), fresh[:, :LAT], preferred_element_type=f32)
        acc_odd[q] = jnp.zeros((256, WIDE), f32)

    @pl.loop(0, CHUNKS)
    def _(j):
        own(j).wait()
        for kind in range(3):
            arrived(kind, j)

        found = [
            jnp.dot(perm_ref[c], pages[c, :, lanes(j)], preferred_element_type=f32)
            for c in range(4)
        ]
        for quarter in range(4):
            for q in range(4):
                at = quarter * 32 + q * 8
                rows = jnp.concatenate([one[at : at + 8] for one in found], axis=0)
                keys[q, pl.ds(quarter * 32, 32), :] = rows.astype(bf16)

        @pl.loop(0, 4)
        def _(q):
            key = keys[q]
            low, high = key[:, :WIDE], key[:, PAIR - WIDE :]
            score = jnp.concatenate(
                [
                    lax.dot_general(query_even[q], low, contract, preferred_element_type=f32),
                    lax.dot_general(query_odd[q], high, contract, preferred_element_type=f32),
                ],
                axis=1,
            )
            n = lax.broadcasted_iota(jnp.int32, (1, 256), 1)
            fifth = n % 8
            page = 4 * fifth + (n % 32) // 8
            position = page * 64 + 2 * (8 * ((n % 128) // 32) + j) + n // 128
            live = (fifth < 5) & (position < length_ref[q])
            score = jnp.where(live, score * scale, masked_score)
            before = row_max[q]
            top = jnp.maximum(before, jnp.max(score, axis=1, keepdims=True))
            shrink = jnp.exp(before - top)
            weight = jnp.exp(score - jnp.concatenate([top, top], axis=1))
            row_max[q] = top
            row_sum[q] = row_sum[q] * shrink + jnp.sum(weight, axis=1, keepdims=True)
            weight = weight.astype(bf16)
            acc_even[q] = acc_even[q] * shrink[:, :1] + jnp.dot(
                weight[:, :128], low[:, :LAT], preferred_element_type=f32
            )
            acc_odd[q] = acc_odd[q] * shrink[:, :1] + jnp.dot(
                weight[:, 128:], high, preferred_element_type=f32
            )

    for q in range(4):
        value = (acc_even[q] + acc_odd[q][:, 64 : 64 + LAT]) / row_sum[q][:, :1]
        for block in range(4):
            s, parity = block // 2, block % 2
            for k in range(LAT // 128):
                out32[k, pl.ds(parity * 8 + s * 4 + q, 64, stride=16), :] = value[
                    block * 64 : block * 64 + 64, k * 128 : k * 128 + 128
                ]

    @pl.loop(0, 32)
    def _(e):
        for k in range(LAT // 128):
            out16[e, :, pl.ds(k * 128, 128)] = out32[
                k, pl.ds(pl.multiple_of(e * 32, 32), 32), :
            ].astype(bf16)

    def head_copy(d, src, dst, device):
        return pltpu.make_async_remote_copy(
            src_ref=src,
            dst_ref=dst,
            send_sem=head_send.at[d],
            recv_sem=head_recv.at[d],
            device_id=device,
            device_id_type=MESH_IDS,
        )

    def head_block(d):
        target = lax.rem(ep + d, 32)
        return head_copy(d, out16.at[target], heads_ref.at[ep], (z, target))

    @pl.loop(1, 32)
    def _(d):
        head_block(d).start()

    heads_ref[ep] = out16[ep]

    @pl.loop(1, 32)
    def _(d):
        source = heads_ref.at[lax.rem(ep + 32 - d, 32)]
        head_copy(d, source, source, (z, ep)).wait_recv()

    @pl.loop(1, 32)
    def _(d):
        head_block(d).wait_send()

    @pl.loop(0, CHUNKS)
    def _(j):
        for kind in range(3):
            outgoing(kind, j).wait_send()


def attend_call(prefill_pages, page_map, prompt_len, queries, new_latent):
    bf16, f32 = jnp.bfloat16, jnp.float32
    slots, width = prefill_pages.shape[3:]
    row = jnp.arange(32)
    request, fifth = row // 8, row % 8
    wanted = request[None, :] * 20 + 4 * fifth[None, :] + jnp.arange(4)[:, None]
    wanted = jnp.where(fifth[None, :] < 5, wanted, -1)
    slot_hit = (page_map.reshape(4, 1, 5, 1, 4) == wanted[:, :, None, None, None]).astype(bf16)
    same = jnp.eye(4, dtype=bf16)[:, None, None, :, None]
    perm = (slot_hit[:, None] * same).reshape(4, 128, 80)
    vmem, hbm = pl.BlockSpec(memory_space=pltpu.VMEM), pl.BlockSpec(memory_space=pl.ANY)
    return pl.pallas_call(
        attend_kernel,
        out_shape=jax.ShapeDtypeStruct((32, 32, LAT), bf16),
        in_specs=[pl.BlockSpec(memory_space=pltpu.SMEM), hbm, vmem, vmem, vmem],
        out_specs=vmem,
        scratch_shapes=[
            pltpu.VMEM((4, 128, WIDE), bf16),
            pltpu.VMEM((slots, 4, width), bf16),
            pltpu.VMEM((PAIR // 128, 320, 128), f32),
            pltpu.VMEM((4, 80, QUARTER), bf16),
            pltpu.VMEM((4, 80, QUARTER), bf16),
            pltpu.VMEM((PAIR // 128, 512, 128), f32),
            pltpu.VMEM((4, 256, WIDE), bf16),
            pltpu.VMEM((4, 256, WIDE), bf16),
            pltpu.VMEM((4, 128, PAIR), bf16),
            pltpu.VMEM((4, 256, LAT), f32),
            pltpu.VMEM((4, 256, WIDE), f32),
            pltpu.VMEM((4, 256, 128), f32),
            pltpu.VMEM((4, 256, 128), f32),
            pltpu.VMEM((LAT // 128, 1024, 128), f32),
            pltpu.VMEM((32, 32, LAT), bf16),
            pltpu.SemaphoreType.DMA((CHUNKS, 4)),
            pltpu.SemaphoreType.DMA((CHUNKS,)),
            pltpu.SemaphoreType.DMA((3, CHUNKS)),
            pltpu.SemaphoreType.DMA((3, CHUNKS)),
            pltpu.SemaphoreType.DMA((32,)),
            pltpu.SemaphoreType.DMA((32,)),
        ],
        compiler_params=pltpu.CompilerParams(
            collective_id=2, has_side_effects=True, vmem_limit_bytes=56 * 1024 * 1024
        ),
        cost_estimate=pl.CostEstimate(
            flops=4_000_000_000, bytes_accessed=8_000_000, transcendentals=1_500_000
        ),
        name="attend",
    )(prompt_len, jnp.swapaxes(prefill_pages[0, 0], 0, 1), perm, queries, new_latent)


def per_device(
    prefill_pages,
    page_map,
    prompt_len,
    queries,
    new_latent,
    resid,
    w_uv,
    w_out,
    norm_gain,
    router_w,
    routes,
    w_gate,
    w_up,
    w_down,
):
    head_rows = attend_call(prefill_pages, page_map, prompt_len, queries, new_latent)
    operands = layer_operands(resid, routes, w_out, norm_gain, router_w, w_gate, w_up, w_down)
    return layer_call(head_rows, w_uv, *operands)


def solution(mesh):
    placed = (
        P("ctx", "ep", None, None, None),
        P("ctx", "ep", None, None),
        P(("ctx", "ep")),
        P(None, ("ctx", "ep"), None),
        P(None, ("ctx", "ep"), None),
        P(None, ("ctx", "ep"), None),
        P("ep", None, None),
        P("ep", None),
        P(),
        P(),
        P(None, ("ctx", "ep"), None),
        P("ep", None, "ctx"),
        P("ep", None, "ctx"),
        P("ep", "ctx", None),
    )
    return jax.shard_map(
        per_device,
        mesh=mesh,
        in_specs=placed,
        out_specs=P(None, ("ctx", "ep"), None),
        check_vma=False,
    )
```

```python
import jax
import jax.numpy as jnp
from jax import lax
from jax.experimental import pallas as pl
from jax.experimental.pallas import tpu as pltpu
from jax.sharding import PartitionSpec as P

LAT = 512
ROPE = 64
NOPE = 128
LATW = 576


norm_eps = 1e-06
route_scale = 2.5
masked_score = -1e30

HALF = 3584
GW = HALF + 128
MESH_IDS = pl.DeviceIdType.MESH
AG_PARTS = tuple((640 * i, 384, 256) for i in range(5)) + ((3200, 256, 256),)
AG_SPLIT = 1920
GENERATIONS = ((0, 896), (896, 2688))
RS_PARTS = (
    (0, 128, 128),
    (256, 128, 128),
    (512, 256, 128),
    (896, 512, 384),
    (1792, 512, 384),
    (2688, 512, 384),
)
PLANE_PARTS = ((0, 256, 256), (512, 256, 128), (896, 768, 640), (2304, 640, 640))
COPIES = 256


class Links:
    def __init__(self, send_sem, recv_sem):
        self.send_sem, self.recv_sem, self.used = send_sem, recv_sem, 0
        self.z, ep = lax.axis_index("ctx"), lax.axis_index("ep")
        self.core = lax.rem(ep, 2)
        self.y, self.x = ep // 8, lax.rem(ep // 2, 4)
        self.ep = ep
        self.coords = (self.z, self.y, self.x)

    def shifted(self, axis, step):
        return lax.rem(self.coords[axis] + (step % 4), 4)

    def neighbour(self, axis, step):
        c = list(self.coords)
        c[axis] = self.shifted(axis, step)
        return (c[0], (c[1] * 4 + c[2]) * 2 + self.core)

    def partner(self):
        return (self.z, self.ep + 1 - 2 * self.core)

    def take(self, count):
        first = self.used
        self.used += count
        return first

    def send(self, src, dst, device, landing, k=None, start=True):
        if k is None:
            k = self.take(1)
        make = lambda s, d: pltpu.make_async_remote_copy(
            src_ref=s,
            dst_ref=d,
            send_sem=self.send_sem.at[k],
            recv_sem=self.recv_sem.at[k],
            device_id=device,
            device_id_type=MESH_IDS,
        )
        out = make(src, dst)
        if start:
            out.start()
        return out, make(landing, landing)


def wait_in(copies):
    for _, incoming in copies:
        incoming.wait_recv()


def wait_out(copies):
    for outgoing, _ in copies:
        outgoing.wait_send()


def pick(ref, chosen, start, width):
    index = tuple(chosen.get(a, slice(None)) for a in range(len(ref.shape) - 2))
    return ref.at[index + (slice(None), pl.ds(start, width))]


def gather_part(link, held, pushed, index, sent, pushes):
    start, wa, wb = AG_PARTS[index]
    order = [(index + j) % 3 for j in range(3)]

    def push(coord):
        src = pick(held, {order[2]: coord}, start, wa + wb)
        dst = pick(pushed, {order[2]: coord}, start, wa + wb)
        pushes.append(link.send(src, dst, link.partner(), dst))

    for stage in range(3):
        axis = order[stage]
        rest = {a: link.coords[a] for a in order[stage + 1 :]}

        def block(step, lo, w):
            coord = link.shifted(axis, step) if step else link.coords[axis]
            return pick(held, {**rest, axis: coord}, lo, w)

        mine = block(0, start, wa + wb)
        if stage == 0:
            near = [
                link.send(mine, mine, link.neighbour(axis, step), block(-step, start, wa + wb))
                for step in (2, 1, -1)
            ]
            sent += near
            yield
            wait_in(near)
            continue
        first = (
            link.send(mine, mine, link.neighbour(axis, 1), block(-1, start, wa + wb)),
            link.send(mine, mine, link.neighbour(axis, -1), block(1, start, wa + wb)),
        )
        if stage == 2:
            push(link.coords[axis])
        yield
        wait_in(first)
        up, down = block(-1, start, wa), block(1, start + wa, wb)
        second = (
            link.send(up, up, link.neighbour(axis, 1), block(2, start, wa)),
            link.send(down, down, link.neighbour(axis, -1), block(2, start + wa, wb)),
        )
        if stage == 2:
            push(link.shifted(axis, -1))
            push(link.shifted(axis, 1))
        sent += list(first) + list(second)
        yield
        wait_in(second)
        if stage == 2:
            push(link.shifted(axis, 2))


def scatter_part(link, parts, index, axes, sums, landings, last, sent):
    start, wa, wb = parts[index]
    count = len(axes)
    order = [axes[(index + j) % count] for j in range(count)]
    f32, bf16 = jnp.float32, jnp.bfloat16
    for stage in range(count):
        far_in, low_in, high_in = landings[stage]
        axis = order[stage]
        done = {a: link.coords[a] for a in order[:stage]}

        def at(coord, lo, w):
            return pick(sums, {k - axes[0]: v for k, v in {**done, axis: coord}.items()}, lo, w)

        def land(ref, lo, w):
            return ref.at[(slice(None),) * (count - stage) + (pl.ds(lo, w),)]

        far = link.shifted(axis, 2)
        if stage == count - 1:
            whole = (start, wa + wb)
            near = []
            for ref, step in ((far_in, 2), (low_in, 1), (high_in, -1)):
                place = land(ref, *whole)
                src = at(link.shifted(axis, step), *whole)
                near.append(link.send(src, place, link.neighbour(axis, step), place))
            sent += near
            yield
            wait_in(near)
            total = at(link.coords[axis], *whole)[...].astype(f32)
            for ref in (far_in, low_in, high_in):
                total = total + land(ref, *whole)[...].astype(f32)
            last(start, wa + wb, total)
            continue
        la, lb = land(far_in, start, wa), land(far_in, start + wa, wb)
        first = (
            link.send(at(far, start, wa), la, link.neighbour(axis, 1), la),
            link.send(at(far, start + wa, wb), lb, link.neighbour(axis, -1), lb),
        )
        yield
        wait_in(first)
        up, down = link.shifted(axis, 1), link.shifted(axis, -1)
        for coord, lo, w in ((up, start, wa), (down, start + wa, wb)):
            view, got = at(coord, lo, w), land(far_in, lo, w)
            view[...] = (view[...].astype(f32) + got[...].astype(f32)).astype(bf16)
        low, high = land(low_in, start, wa + wb), land(high_in, start, wa + wb)
        second = (
            link.send(at(up, start, wa + wb), low, link.neighbour(axis, 1), low),
            link.send(at(down, start, wa + wb), high, link.neighbour(axis, -1), high),
        )
        sent += list(first) + list(second)
        yield
        wait_in(second)
        view = at(link.coords[axis], start, wa + wb)
        total = view[...].astype(f32) + low[...].astype(f32) + high[...].astype(f32)
        view[...] = total.astype(bf16)


def resume(threads):
    for thread in threads:
        next(thread, None)


def layer_kernel(
    heads_ref,
    w_uv_ref,
    resid_ref,
    routes_ref,
    gain_ref,
    router_ref,
    w_out_hbm,
    w_gate_hbm,
    w_up_hbm,
    w_down_hbm,
    out_ref,
    big,
    wg,
    wu,
    wd,
    flat,
    part_send,
    part_land,
    part_sum,
    plane_a0,
    plane_a1,
    plane_b0,
    plane_b1,
    plane_c0,
    plane_c1,
    mask_out,
    resid_out,
    hid,
    picked,
    stat_out,
    stat_in,
    held,
    pushed,
    gate_acc,
    up_acc,
    units,
    far0,
    low0,
    high0,
    far1,
    low1,
    high1,
    far2,
    low2,
    high2,
    fin,
    fin_in,
    send_sem,
    recv_sem,
    load_sem,
):
    link = Links(send_sem, recv_sem)
    core = link.core
    other = 1 - core
    partner = link.partner()
    f32, bf16 = jnp.float32, jnp.bfloat16

    own_cols = pl.ds(pl.multiple_of(core * HALF, 128), HALF)
    other_cols = pl.ds(pl.multiple_of(other * HALF, 128), HALF)
    loads = []

    def load(src, dst):
        copy = pltpu.make_async_copy(src, dst, load_sem.at[len(loads)])
        copy.start()
        loads.append(copy)

    load(w_out_hbm.at[:, :, :, :, other_cols], big.at[pl.ds(2, 2)])
    load(w_out_hbm.at[:, :, :, :, own_cols], big.at[pl.ds(0, 2)])
    barrier = pltpu.get_barrier_semaphore()
    for axis in range(3):
        for step in (1, -1, 2):
            pl.semaphore_signal(
                barrier, inc=1, device_id=link.neighbour(axis, step), device_id_type=MESH_IDS
            )
    pl.semaphore_signal(barrier, inc=1, device_id=partner, device_id_type=MESH_IDS)

    for pair in range(2):
        rows = heads_ref[:, pl.ds(pair * 16, 16), :].reshape(512, LAT)
        for one in range(2):
            head = 2 * pair + one
            value = jnp.dot(rows, w_uv_ref[head], preferred_element_type=f32)
            value = value.reshape(32, 2, 8, 128)[:, one].reshape(256, 128)
            flat[:, pl.ds(head * 128, 128)] = value.astype(bf16)

    def project(slot, start):
        lanes = pl.ds(start, 896)
        weight = big[pl.ds(2 * slot, 2), :, :, :, lanes].reshape(512, 896)
        value = jnp.dot(flat[...], weight, preferred_element_type=f32)
        return value.reshape(4, 4, 16, 896)

    def project_away(start, width):
        @pl.loop(0, width // 896)
        def _(j):
            at = pl.multiple_of(start + j * 896, 128)
            part_send[:, :, :, pl.ds(at, 896)] = project(1, at).astype(bf16)

    def swap_sums(start, width):
        lanes = pl.ds(start, width)
        dst = part_land.at[:, :, :, lanes]
        return link.send(part_send.at[:, :, :, lanes], dst, partner, dst)

    loads[0].wait()
    project_away(*GENERATIONS[0])
    pl.semaphore_wait(barrier, 10)

    def token_rows(cols):
        return jnp.concatenate([resid_ref[s, :, cols].astype(f32) for s in range(2)], axis=0)

    resid_out[...] = token_rows(other_cols)
    names = jnp.concatenate([routes_ref[s] for s in range(2)], axis=0)
    expert = lax.broadcasted_iota(jnp.int32, (8, 128), 1)
    mask = jnp.zeros((8, 128), f32)
    for k in range(routes_ref.shape[2]):
        mask = jnp.where(expert == names[:, k : k + 1], 1.0, mask)
    mask_out[...] = mask
    sent = []
    swaps = [
        link.send(resid_out, hid.at[core], partner, hid.at[other]),
        link.send(mask_out, picked.at[core], partner, picked.at[other]),
    ]
    sent += swaps

    core_swap = [swap_sums(*GENERATIONS[0])]
    project_away(*GENERATIONS[1])
    core_swap.append(swap_sums(*GENERATIONS[1]))
    sent += core_swap
    loads[1].wait()
    for slot, cols in ((0, own_cols), (1, other_cols)):
        load(w_gate_hbm.at[cols], wg.at[slot])
        load(w_up_hbm.at[cols], wu.at[slot])
        load(w_down_hbm.at[:, cols], wd.at[slot])

    hid[core] = token_rows(own_cols)
    picked[core] = mask_out[...]
    wait_in(swaps)

    def add_hidden(start, width, total):
        lanes = pl.ds(start, width)
        hid[:, :, lanes] = hid[:, :, lanes] + total.reshape(2, 8, width)

    plane_land = ((plane_a0, plane_b0, plane_c0), (plane_a1, plane_b1, plane_c1))
    threads = []
    for turn, (start, width) in enumerate(GENERATIONS):
        wait_in(core_swap[turn : turn + 1])

        @pl.loop(0, width // 896)
        def _(j, start=start):
            at = pl.multiple_of(start + j * 896, 128)
            value = project(0, at) + part_land[:, :, :, pl.ds(at, 896)].astype(f32)
            part_sum[:, :, :, pl.ds(at, 896)] = value.astype(bf16)

        for index in (2 * turn, 2 * turn + 1):
            threads.append(
                scatter_part(
                    link, PLANE_PARTS, index, (1, 2), part_sum, plane_land, add_hidden, sent
                )
            )
            next(threads[-1])
    for _ in range(3):
        resume(threads)

    hidden = hid[...].reshape(16, HALF)
    gain = gain_ref[core]
    logits = lax.dot_general(
        (hidden * gain).astype(bf16),
        router_ref[:, own_cols],
        (((1,), (1,)), ((), ())),
        preferred_element_type=f32,
    )
    logits = jnp.concatenate([logits, jnp.zeros((16, 96), f32)], axis=1)
    squares = jnp.sum(hidden * hidden, axis=1, keepdims=True)
    lane = lax.broadcasted_iota(jnp.int32, (16, 128), 1)
    mine = jnp.where(lane < 64, logits, jnp.broadcast_to(squares, (16, 128)))
    stat_out[...] = mine
    stat = link.send(stat_out, stat_in, partner, stat_in)
    sent.append(stat)
    wait_in([stat])
    both = mine + stat_in[...]
    scale = lax.rsqrt(both[:, 64:65] / (2 * HALF) + norm_eps)
    affinity = jax.nn.sigmoid(both * scale) * picked[...].reshape(16, 128)
    weights = route_scale * affinity / jnp.sum(affinity, axis=1, keepdims=True)
    high = weights.astype(bf16)
    low = (weights - high.astype(f32)).astype(bf16).astype(f32)
    table = high.astype(f32) + pltpu.roll(low, 32, axis=1)
    normed = (hid[...].reshape(16, HALF) * scale * gain).astype(bf16)
    held[link.z, link.y, link.x, :, pl.ds(0, HALF)] = normed
    held[link.z, link.y, link.x, :, pl.ds(HALF, 128)] = table.astype(bf16)

    gathers, pushes = [], []
    threads = [gather_part(link, held, pushed, i, gathers, pushes) for i in range(6)]
    for _ in range(5):
        resume(threads)
    resume(threads[:3])
    for copy in loads[2:]:
        copy.wait()

    def own_first(i, carry):
        rows = held[pl.ds(4 * i, 4), :, :, :, pl.ds(0, AG_SPLIT)].reshape(1024, AG_SPLIT)
        cut = pl.ds(0, AG_SPLIT)
        gate_acc[i] = jnp.dot(rows, wg[0, cut], preferred_element_type=f32)
        up_acc[i] = jnp.dot(rows, wu[0, cut], preferred_element_type=f32)
        return carry

    lax.fori_loop(0, 1, own_first, 0)
    resume(threads[3:])

    def own_half(i, carry):
        cut = pl.ds(AG_SPLIT, HALF - AG_SPLIT)
        rows = held[pl.ds(4 * i, 4), :, :, :, cut].reshape(1024, HALF - AG_SPLIT)
        gate_acc[i] += jnp.dot(rows, wg[0, cut], preferred_element_type=f32)
        up_acc[i] += jnp.dot(rows, wu[0, cut], preferred_element_type=f32)
        return carry

    lax.fori_loop(0, 1, own_half, 0)
    wait_in(pushes)

    def other_half(i, carry):
        rows = pushed[pl.ds(4 * i, 4), :, :, :, pl.ds(0, HALF)].reshape(1024, HALF)
        gate_part = gate_acc[i] + jnp.dot(rows, wg[1], preferred_element_type=f32)
        up_part = up_acc[i] + jnp.dot(rows, wu[1], preferred_element_type=f32)
        table = held[pl.ds(4 * i, 4), :, :, :, pl.ds(HALF, 128)].reshape(1024, 128).astype(f32)
        lane = lax.broadcasted_iota(jnp.int32, (1024, 128), 1)
        here = (lane == link.ep) | (lane == link.ep + 32)
        factor = jnp.sum(jnp.where(here, table, 0.0), axis=1, keepdims=True)
        value = (jax.nn.silu(gate_part) * up_part * factor).astype(bf16)
        units[pl.ds(4 * i, 4)] = value.reshape(4, 256, 256)
        return carry

    lax.fori_loop(0, 1, other_half, 0)
    wait_out(gathers + pushes)

    def routed_chunk(slot, i, at):
        weight = wd[slot, :, pl.ds(at, 896)]
        value = jnp.dot(units[i], weight, preferred_element_type=f32)
        return value.reshape(4, 4, 16, 896)

    chunks = [range(start, start + width, 896) for start, width in GENERATIONS]
    back_first = link.take(8)

    def back(turn, i, start):
        lanes = pl.ds(*GENERATIONS[turn])
        dst = big.at[i, :, :, :, lanes]
        k = back_first + 4 * turn + i
        return link.send(pushed.at[i, :, :, :, lanes], dst, partner, dst, k, start)

    for turn in range(2):

        @pl.loop(0, 4)
        def _(i, turn=turn):
            for at in chunks[turn]:
                pushed[i, :, :, :, pl.ds(at, 896)] = routed_chunk(1, i, at).astype(bf16)
            back(turn, i, True)

    def add_routed(start, width, total):
        lanes = pl.ds(start, width)
        fin[:, :, lanes] = hid[:, :, lanes] + total.reshape(2, 8, width)

    torus_land = ((far0, low0, high0), (far1, low1, high1), (far2, low2, high2))
    threads = []
    for turn in range(2):

        @pl.loop(0, 4)
        def _(i, turn=turn):
            wait_in([back(turn, i, False)])
            for at in chunks[turn]:
                value = routed_chunk(0, i, at) + big[i, :, :, :, pl.ds(at, 896)].astype(f32)
                held[i, :, :, :, pl.ds(at, 896)] = value.astype(bf16)

        for index in range(3 * turn, 3 * turn + 3):
            threads.append(
                scatter_part(
                    link, RS_PARTS, index, (0, 1, 2), held, torus_land, add_routed, sent
                )
            )
            next(threads[-1])
    for _ in range(5):
        resume(threads)
    swap = link.send(fin.at[other], fin_in, partner, fin_in)
    sent.append(swap)
    for s in range(2):
        out_ref[s, :, own_cols] = fin[core, pl.ds(4 * s, 4)]
    wait_in([swap])
    for s in range(2):
        out_ref[s, :, other_cols] = fin_in[pl.ds(4 * s, 4)]
    wait_out(sent)
    for turn in range(2):

        @pl.loop(0, 4)
        def _(i, turn=turn):
            wait_out([back(turn, i, False)])


def layer_call(head_rows, w_uv, resid, routes, gain, router, w_out, w_gate, w_up, w_down):
    vmem, hbm = pl.BlockSpec(memory_space=pltpu.VMEM), pl.BlockSpec(memory_space=pl.ANY)
    bf16, f32 = jnp.bfloat16, jnp.float32

    def block(*lead, lanes=HALF, kind=bf16):
        return pltpu.VMEM(lead + (lanes,), kind)

    plane = [block(4, 16), block(16)] * 3
    torus = [block(4, 4, 16)] * 3 + [block(4, 16)] * 3 + [block(16)] * 3
    scratch = (
        [block(4, 4, 4, 16)]
        + [pltpu.VMEM((2, HALF, 256), bf16)] * 2
        + [pltpu.VMEM((2, 256, HALF), bf16), pltpu.VMEM((256, 512), bf16)]
        + [block(4, 4, 16)] * 3
        + plane
        + [pltpu.VMEM((8, 128), f32), block(8, kind=f32), block(2, 8, kind=f32), pltpu.VMEM((2, 8, 128), f32)]
        + [pltpu.VMEM((16, 128), f32)] * 2
        + [block(4, 4, 4, 16, lanes=GW)] * 2
        + [pltpu.VMEM((1, 1024, 256), f32)] * 2
        + [pltpu.VMEM((4, 256, 256), bf16)]
        + torus
        + [block(2, 8, kind=f32), block(8, kind=f32)]
        + [pltpu.SemaphoreType.DMA((COPIES,))] * 2
        + [pltpu.SemaphoreType.DMA((8,))]
    )
    return pl.pallas_call(
        layer_kernel,
        out_shape=jax.ShapeDtypeStruct((2, 4, 2 * HALF), f32),
        in_specs=[vmem] * 6 + [hbm] * 4,
        out_specs=vmem,
        scratch_shapes=scratch,
        compiler_params=pltpu.CompilerParams(
            collective_id=1, has_side_effects=True, vmem_limit_bytes=62 * 1024 * 1024
        ),
        cost_estimate=pl.CostEstimate(
            flops=20_000_000_000, bytes_accessed=22_000_000, transcendentals=300_000
        ),
        name="layer",
    )(head_rows, w_uv, resid, routes, gain, router, w_out, w_gate, w_up, w_down)


def layer_operands(resid, routes, w_out, norm_gain, router_w, w_gate, w_up, w_down):
    gain = norm_gain.astype(jnp.float32).reshape(2, 1, HALF)
    return (
        resid,
        routes,
        gain,
        router_w.T,
        w_out.reshape(2, 4, 4, 16, 2 * HALF),
        w_gate[0],
        w_up[0],
        w_down[0],
    )


CHUNKS = 8
PAIR = 2 * LATW
WIDE = 640
QUARTER = 9216
SPREAD = (2, 1, 3)
AHEAD = 4


def attend_kernel(
    length_ref,
    pages_hbm,
    perm_ref,
    query_ref,
    fresh_ref,
    heads_ref,
    fresh_rows,
    raw,
    rows_raw,
    packed,
    pages,
    rows32,
    query_even,
    query_odd,
    keys,
    acc_even,
    acc_odd,
    row_max,
    row_sum,
    out32,
    out16,
    raw_sem,
    own_sem,
    link_send,
    link_recv,
    head_send,
    head_recv,
):
    f32, bf16 = jnp.float32, jnp.bfloat16
    z, ep = lax.axis_index("ctx"), lax.axis_index("ep")

    def lanes(j):
        return pl.ds(pl.multiple_of(j * PAIR, 128), PAIR)

    def ring(step):
        return lax.rem(z + step, 4)

    def copy(kind, j, src, dst, device):
        return pltpu.make_async_remote_copy(
            src_ref=src,
            dst_ref=dst,
            send_sem=link_send.at[kind, j],
            recv_sem=link_recv.at[kind, j],
            device_id=device,
            device_id_type=MESH_IDS,
        )

    def outgoing(kind, j):
        owner = ring(SPREAD[kind])
        return copy(
            kind, j, packed.at[owner, :, lanes(j)], pages.at[z, :, lanes(j)], (owner, ep)
        )

    def arrived(kind, j):
        producer = ring(4 - SPREAD[kind])
        place = pages.at[producer, :, lanes(j)]
        copy(kind, j, place, place, (producer, ep)).wait_recv()

    def own(j):
        return pltpu.make_async_copy(
            packed.at[z, :, lanes(j)], pages.at[z, :, lanes(j)], own_sem.at[j]
        )

    def fetch(j, quarter):
        span = pl.ds(pl.multiple_of(quarter * QUARTER + j * PAIR, 128), PAIR)
        return pltpu.make_async_copy(
            pages_hbm.at[:, :, span], raw.at[:, :, span], raw_sem.at[j, quarter]
        )

    @pl.loop(0, CHUNKS)
    def _(j):
        for quarter in range(4):
            fetch(j, quarter).start()

    barrier = pltpu.get_barrier_semaphore()
    for step in SPREAD:
        pl.semaphore_signal(barrier, inc=1, device_id=(ring(step), ep), device_id_type=MESH_IDS)

    @pl.loop(1, 32)
    def _(d):
        device = (z, lax.rem(ep + d, 32))
        pl.semaphore_signal(barrier, inc=1, device_id=device, device_id_type=MESH_IDS)


    def repack(j):
        for quarter in range(4):
            fetch(j, quarter).wait()
        for quarter in range(4):
            span = pl.ds(pl.multiple_of(quarter * QUARTER + j * PAIR, 128), PAIR)

            @pl.loop(0, 5)
            def _(group, quarter=quarter, span=span):
                for two in range(2):
                    slot = group * 4 + two * 2
                    both = jnp.concatenate(
                        [raw[slot, :, span].astype(f32), raw[slot + 1, :, span].astype(f32)], axis=0
                    )
                    place = pl.ds(pl.multiple_of((group * 4 + quarter) * 16 + two * 8, 8), 8)
                    for k in range(PAIR // 128):
                        rows_raw[k, place, :] = both[:, k * 128 : k * 128 + 128]

        for owner in range(4):
            for k in range(PAIR // 128):
                column = pl.ds(pl.multiple_of(j * PAIR + k * 128, 128), 128)
                packed[owner, :, column] = rows_raw[k, pl.ds(owner, 80, stride=4), :].astype(bf16)

    repack(0)
    pl.semaphore_wait(barrier, 34)

    @pl.loop(0, CHUNKS)
    def _(j):
        @pl.when(j < AHEAD)
        def _():
            for kind in range(3):
                outgoing(kind, j).start()

        own(j).start()

        @pl.when(j + 1 < CHUNKS)
        def _():
            repack(j + 1)

    @pl.loop(0, 64)
    def _(pair):
        span = pl.ds(pl.multiple_of(pair * PAIR, 128), PAIR)
        both = [query_ref[s, :, span].astype(f32) for s in range(2)]
        both = jnp.concatenate(both, axis=0)
        for k in range(PAIR // 128):
            rows32[k, pl.ds(pl.multiple_of(pair * 8, 8), 8), :] = both[:, k * 128 : k * 128 + 128]

    lane = lax.broadcasted_iota(jnp.int32, (64, WIDE), 1)
    for q in range(4):
        for s in range(2):
            rows = jnp.concatenate(
                [rows32[k, pl.ds(s * 4 + q, 64, stride=8), :] for k in range(PAIR // 128)], axis=1
            )
            even = jnp.where(lane < LATW, rows[:, :WIDE], 0.0)
            odd = jnp.where(lane >= 64, rows[:, PAIR - WIDE :], 0.0)
            for parity, value, shift in ((0, even, 64), (1, odd, WIDE - 64)):
                place = pl.ds(s * 128 + parity * 64, 64)
                moved = pltpu.roll(value, shift, axis=1).astype(bf16)
                value = value.astype(bf16)
                query_even[q, place, :] = value if parity == 0 else moved
                query_odd[q, place, :] = moved if parity == 0 else value

    scale = (NOPE + ROPE) ** (-0.5)
    contract = (((1,), (1,)), ((), ()))

    drawn = [fresh_ref[j].astype(f32) for j in range(2)]
    for q in range(4):
        rows = jnp.concatenate([one[q : q + 1] for one in drawn] + [jnp.zeros((6, LATW), f32)], 0)
        rows = jnp.concatenate([rows, jnp.zeros((8, WIDE - LATW), f32)], axis=1)
        rows = jnp.concatenate([rows, jnp.zeros((120, WIDE), f32)], axis=0)
        fresh_rows[q] = rows.astype(bf16)

    @pl.loop(0, 4)
    def _(q):
        fresh = fresh_rows[q]
        score = (
            lax.dot_general(query_even[q], fresh, contract, preferred_element_type=f32) * scale
        )
        token = lax.broadcasted_iota(jnp.int32, (256, 128), 1)
        step = lax.broadcasted_iota(jnp.int32, (256, 128), 0) // 128
        score = jnp.where(token <= step, score, masked_score)
        top = jnp.max(score, axis=1, keepdims=True)
        weight = jnp.exp(score - top)
        row_max[q] = jnp.broadcast_to(top, (256, 128))
        row_sum[q] = jnp.broadcast_to(jnp.sum(weight, axis=1, keepdims=True), (256, 128))
        acc_even[q] = jnp.dot(weight.astype(bf16), fresh[:, :LAT], preferred_element_type=f32)
        acc_odd[q] = jnp.zeros((256, WIDE), f32)

    @pl.loop(0, CHUNKS)
    def _(j):
        @pl.when(j + AHEAD < CHUNKS)
        def _():
            for kind in range(3):
                outgoing(kind, j + AHEAD).start()

        own(j).wait()
        for kind in range(3):
            arrived(kind, j)

        found = [
            jnp.dot(perm_ref[c], pages[c, :, lanes(j)], preferred_element_type=f32)
            for c in range(4)
        ]
        for quarter in range(4):
            for q in range(4):
                at = quarter * 32 + q * 8
                rows = jnp.concatenate([one[at : at + 8] for one in found], axis=0)
                keys[q, pl.ds(quarter * 32, 32), :] = rows.astype(bf16)

        @pl.loop(0, 4)
        def _(q):
            key = keys[q]
            low, high = key[:, :WIDE], key[:, PAIR - WIDE :]
            score = jnp.concatenate(
                [
                    lax.dot_general(query_even[q], low, contract, preferred_element_type=f32),
                    lax.dot_general(query_odd[q], high, contract, preferred_element_type=f32),
                ],
                axis=1,
            )
            n = lax.broadcasted_iota(jnp.int32, (1, 256), 1)
            fifth = n % 8
            page = 4 * fifth + (n % 32) // 8
            position = page * 64 + 2 * (8 * ((n % 128) // 32) + j) + n // 128
            live = (fifth < 5) & (position < length_ref[q])
            score = jnp.where(live, score * scale, masked_score)
            before = row_max[q]
            top = jnp.maximum(before, jnp.max(score, axis=1, keepdims=True))
            shrink = jnp.exp(before - top)
            weight = jnp.exp(score - jnp.concatenate([top, top], axis=1))
            row_max[q] = top
            row_sum[q] = row_sum[q] * shrink + jnp.sum(weight, axis=1, keepdims=True)
            weight = weight.astype(bf16)
            acc_even[q] = acc_even[q] * shrink[:, :1] + jnp.dot(
                weight[:, :128], low[:, :LAT], preferred_element_type=f32
            )
            acc_odd[q] = acc_odd[q] * shrink[:, :1] + jnp.dot(
                weight[:, 128:], high, preferred_element_type=f32
            )

    for q in range(4):
        value = (acc_even[q] + acc_odd[q][:, 64 : 64 + LAT]) / row_sum[q][:, :1]
        for block in range(4):
            s, parity = block // 2, block % 2
            for k in range(LAT // 128):
                out32[k, pl.ds(parity * 8 + s * 4 + q, 64, stride=16), :] = value[
                    block * 64 : block * 64 + 64, k * 128 : k * 128 + 128
                ]

    def rounded(e):
        rows = pl.ds(pl.multiple_of(e * 32, 32), 32)
        parts = [out32[k, rows, :] for k in range(LAT // 128)]
        return jnp.concatenate(parts, axis=1).astype(bf16)

    def head_copy(d, src, dst, device):
        return pltpu.make_async_remote_copy(
            src_ref=src,
            dst_ref=dst,
            send_sem=head_send.at[d],
            recv_sem=head_recv.at[d],
            device_id=device,
            device_id_type=MESH_IDS,
        )

    def head_block(d):
        target = lax.rem(ep + d, 32)
        return head_copy(d, out16.at[target], heads_ref.at[ep], (z, target))

    @pl.loop(1, 32)
    def _(d):
        target = lax.rem(ep + d, 32)
        out16[target] = rounded(target)
        head_block(d).start()

    heads_ref[ep] = rounded(ep)

    @pl.loop(1, 32)
    def _(d):
        source = heads_ref.at[lax.rem(ep + 32 - d, 32)]
        head_copy(d, source, source, (z, ep)).wait_recv()

    @pl.loop(1, 32)
    def _(d):
        head_block(d).wait_send()

    @pl.loop(0, CHUNKS)
    def _(j):
        for kind in range(3):
            outgoing(kind, j).wait_send()


def attend_call(prefill_pages, page_map, prompt_len, queries, new_latent):
    bf16, f32 = jnp.bfloat16, jnp.float32
    slots, width = prefill_pages.shape[3:]
    row = jnp.arange(32)
    request, fifth = row // 8, row % 8
    wanted = request[None, :] * 20 + 4 * fifth[None, :] + jnp.arange(4)[:, None]
    wanted = jnp.where(fifth[None, :] < 5, wanted, -1)
    slot_hit = (page_map.reshape(4, 1, 5, 1, 4) == wanted[:, :, None, None, None]).astype(bf16)
    same = jnp.eye(4, dtype=bf16)[:, None, None, :, None]
    perm = (slot_hit[:, None] * same).reshape(4, 128, 80)
    vmem, hbm = pl.BlockSpec(memory_space=pltpu.VMEM), pl.BlockSpec(memory_space=pl.ANY)
    return pl.pallas_call(
        attend_kernel,
        out_shape=jax.ShapeDtypeStruct((32, 32, LAT), bf16),
        in_specs=[pl.BlockSpec(memory_space=pltpu.SMEM), hbm, vmem, vmem, vmem],
        out_specs=vmem,
        scratch_shapes=[
            pltpu.VMEM((4, 128, WIDE), bf16),
            pltpu.VMEM((slots, 4, width), bf16),
            pltpu.VMEM((PAIR // 128, 320, 128), f32),
            pltpu.VMEM((4, 80, QUARTER), bf16),
            pltpu.VMEM((4, 80, QUARTER), bf16),
            pltpu.VMEM((PAIR // 128, 512, 128), f32),
            pltpu.VMEM((4, 256, WIDE), bf16),
            pltpu.VMEM((4, 256, WIDE), bf16),
            pltpu.VMEM((4, 128, PAIR), bf16),
            pltpu.VMEM((4, 256, LAT), f32),
            pltpu.VMEM((4, 256, WIDE), f32),
            pltpu.VMEM((4, 256, 128), f32),
            pltpu.VMEM((4, 256, 128), f32),
            pltpu.VMEM((LAT // 128, 1024, 128), f32),
            pltpu.VMEM((32, 32, LAT), bf16),
            pltpu.SemaphoreType.DMA((CHUNKS, 4)),
            pltpu.SemaphoreType.DMA((CHUNKS,)),
            pltpu.SemaphoreType.DMA((3, CHUNKS)),
            pltpu.SemaphoreType.DMA((3, CHUNKS)),
            pltpu.SemaphoreType.DMA((32,)),
            pltpu.SemaphoreType.DMA((32,)),
        ],
        compiler_params=pltpu.CompilerParams(
            collective_id=2, has_side_effects=True, vmem_limit_bytes=56 * 1024 * 1024
        ),
        cost_estimate=pl.CostEstimate(
            flops=4_000_000_000, bytes_accessed=8_000_000, transcendentals=1_500_000
        ),
        name="attend",
    )(prompt_len, jnp.swapaxes(prefill_pages[0, 0], 0, 1), perm, queries, new_latent)


def per_device(
    prefill_pages,
    page_map,
    prompt_len,
    queries,
    new_latent,
    resid,
    w_uv,
    w_out,
    norm_gain,
    router_w,
    routes,
    w_gate,
    w_up,
    w_down,
):
    head_rows = attend_call(prefill_pages, page_map, prompt_len, queries, new_latent)
    operands = layer_operands(resid, routes, w_out, norm_gain, router_w, w_gate, w_up, w_down)
    return layer_call(head_rows, w_uv, *operands).astype(jnp.bfloat16)


def solution(mesh):
    placed = (
        P("ctx", "ep", None, None, None),
        P("ctx", "ep", None, None),
        P(("ctx", "ep")),
        P(None, ("ctx", "ep"), None),
        P(None, ("ctx", "ep"), None),
        P(None, ("ctx", "ep"), None),
        P("ep", None, None),
        P("ep", None),
        P(),
        P(),
        P(None, ("ctx", "ep"), None),
        P("ep", None, "ctx"),
        P("ep", None, "ctx"),
        P("ep", "ctx", None),
    )
    return jax.shard_map(
        per_device,
        mesh=mesh,
        in_specs=placed,
        out_specs=P(None, ("ctx", "ep"), None),
        check_vma=False,
    )
```

```python
import jax
import jax.numpy as jnp
from jax import lax
from jax.experimental import pallas as pl
from jax.experimental.pallas import tpu as pltpu
from jax.sharding import PartitionSpec as P

LAT = 512
ROPE = 64
NOPE = 128
LATW = 576


norm_eps = 1e-06
route_scale = 2.5
masked_score = -1e30

HALF = 3584
GW = HALF + 128
MESH_IDS = pl.DeviceIdType.MESH
AG_PARTS = (
    (0, 512, 384),
    (896, 512, 384),
    (1792, 384, 384),
    (2560, 256, 128),
    (2944, 256, 128),
    (3328, 256, 128),
)
AG_SPLIT = 2560
GENERATIONS = ((0, 896), (896, 2688))
RS_PARTS = (
    (0, 128, 128),
    (256, 128, 128),
    (512, 256, 128),
    (896, 512, 384),
    (1792, 512, 384),
    (2688, 512, 384),
)
PLANE_PARTS = ((0, 256, 256), (512, 256, 128), (896, 768, 640), (2304, 640, 640))
COPIES = 256


class Links:
    def __init__(self, send_sem, recv_sem):
        self.send_sem, self.recv_sem, self.used = send_sem, recv_sem, 0
        self.z, ep = lax.axis_index("ctx"), lax.axis_index("ep")
        self.core = lax.rem(ep, 2)
        self.y, self.x = ep // 8, lax.rem(ep // 2, 4)
        self.ep = ep
        self.coords = (self.z, self.y, self.x)

    def shifted(self, axis, step):
        return lax.rem(self.coords[axis] + (step % 4), 4)

    def neighbour(self, axis, step):
        c = list(self.coords)
        c[axis] = self.shifted(axis, step)
        return (c[0], (c[1] * 4 + c[2]) * 2 + self.core)

    def partner(self):
        return (self.z, self.ep + 1 - 2 * self.core)

    def take(self, count):
        first = self.used
        self.used += count
        return first

    def send(self, src, dst, device, landing, k=None, start=True):
        if k is None:
            k = self.take(1)
        make = lambda s, d: pltpu.make_async_remote_copy(
            src_ref=s,
            dst_ref=d,
            send_sem=self.send_sem.at[k],
            recv_sem=self.recv_sem.at[k],
            device_id=device,
            device_id_type=MESH_IDS,
        )
        out = make(src, dst)
        if start:
            out.start()
        return out, make(landing, landing)


def wait_in(copies):
    for _, incoming in copies:
        incoming.wait_recv()


def wait_out(copies):
    for outgoing, _ in copies:
        outgoing.wait_send()


def pick(ref, chosen, start, width):
    index = tuple(chosen.get(a, slice(None)) for a in range(len(ref.shape) - 2))
    return ref.at[index + (slice(None), pl.ds(start, width))]


def gather_part(link, held, pushed, index, sent, pushes):
    start, wa, wb = AG_PARTS[index]
    order = [(index + j) % 3 for j in range(3)]

    def push(coord):
        src = pick(held, {order[2]: coord}, start, wa + wb)
        dst = pick(pushed, {order[2]: coord}, start, wa + wb)
        pushes.append(link.send(src, dst, link.partner(), dst))

    for stage in range(3):
        axis = order[stage]
        rest = {a: link.coords[a] for a in order[stage + 1 :]}

        def block(step, lo, w):
            coord = link.shifted(axis, step) if step else link.coords[axis]
            return pick(held, {**rest, axis: coord}, lo, w)

        mine = block(0, start, wa + wb)
        if stage == 0:
            near = [
                link.send(mine, mine, link.neighbour(axis, step), block(-step, start, wa + wb))
                for step in (2, 1, -1)
            ]
            sent += near
            yield
            wait_in(near)
            continue
        first = (
            link.send(mine, mine, link.neighbour(axis, 1), block(-1, start, wa + wb)),
            link.send(mine, mine, link.neighbour(axis, -1), block(1, start, wa + wb)),
        )
        if stage == 2:
            push(link.coords[axis])
        yield
        wait_in(first)
        up, down = block(-1, start, wa), block(1, start + wa, wb)
        second = (
            link.send(up, up, link.neighbour(axis, 1), block(2, start, wa)),
            link.send(down, down, link.neighbour(axis, -1), block(2, start + wa, wb)),
        )
        if stage == 2:
            push(link.shifted(axis, -1))
            push(link.shifted(axis, 1))
        sent += list(first) + list(second)
        yield
        wait_in(second)
        if stage == 2:
            push(link.shifted(axis, 2))


def scatter_part(link, parts, index, axes, sums, landings, last, sent):
    start, wa, wb = parts[index]
    count = len(axes)
    order = [axes[(index + j) % count] for j in range(count)]
    f32, bf16 = jnp.float32, jnp.bfloat16
    for stage in range(count):
        far_in, low_in, high_in = landings[stage]
        axis = order[stage]
        done = {a: link.coords[a] for a in order[:stage]}

        def at(coord, lo, w):
            return pick(sums, {k - axes[0]: v for k, v in {**done, axis: coord}.items()}, lo, w)

        def land(ref, lo, w):
            return ref.at[(slice(None),) * (count - stage) + (pl.ds(lo, w),)]

        far = link.shifted(axis, 2)
        if stage == count - 1:
            whole = (start, wa + wb)
            near = []
            for ref, step in ((far_in, 2), (low_in, 1), (high_in, -1)):
                place = land(ref, *whole)
                src = at(link.shifted(axis, step), *whole)
                near.append(link.send(src, place, link.neighbour(axis, step), place))
            sent += near
            yield
            wait_in(near)
            total = at(link.coords[axis], *whole)[...].astype(f32)
            for ref in (far_in, low_in, high_in):
                total = total + land(ref, *whole)[...].astype(f32)
            last(start, wa + wb, total)
            continue
        la, lb = land(far_in, start, wa), land(far_in, start + wa, wb)
        first = (
            link.send(at(far, start, wa), la, link.neighbour(axis, 1), la),
            link.send(at(far, start + wa, wb), lb, link.neighbour(axis, -1), lb),
        )
        yield
        wait_in(first)
        up, down = link.shifted(axis, 1), link.shifted(axis, -1)
        for coord, lo, w in ((up, start, wa), (down, start + wa, wb)):
            view, got = at(coord, lo, w), land(far_in, lo, w)
            view[...] = (view[...].astype(f32) + got[...].astype(f32)).astype(bf16)
        low, high = land(low_in, start, wa + wb), land(high_in, start, wa + wb)
        second = (
            link.send(at(up, start, wa + wb), low, link.neighbour(axis, 1), low),
            link.send(at(down, start, wa + wb), high, link.neighbour(axis, -1), high),
        )
        sent += list(first) + list(second)
        yield
        wait_in(second)
        view = at(link.coords[axis], start, wa + wb)
        total = view[...].astype(f32) + low[...].astype(f32) + high[...].astype(f32)
        view[...] = total.astype(bf16)


def resume(threads):
    for thread in threads:
        next(thread, None)


def layer_kernel(
    heads_ref,
    w_uv_ref,
    resid_ref,
    routes_ref,
    gain_ref,
    router_ref,
    w_out_hbm,
    w_gate_hbm,
    w_up_hbm,
    w_down_hbm,
    out_ref,
    big,
    wg,
    wu,
    wd,
    flat,
    part_send,
    part_land,
    part_sum,
    plane_a0,
    plane_a1,
    plane_b0,
    plane_b1,
    plane_c0,
    plane_c1,
    mask_out,
    resid_out,
    hid,
    picked,
    stat_out,
    stat_in,
    held,
    pushed,
    gate_acc,
    up_acc,
    units,
    far0,
    low0,
    high0,
    far1,
    low1,
    high1,
    far2,
    low2,
    high2,
    fin,
    fin_in,
    send_sem,
    recv_sem,
    load_sem,
):
    link = Links(send_sem, recv_sem)
    core = link.core
    other = 1 - core
    partner = link.partner()
    f32, bf16 = jnp.float32, jnp.bfloat16

    own_cols = pl.ds(pl.multiple_of(core * HALF, 128), HALF)
    other_cols = pl.ds(pl.multiple_of(other * HALF, 128), HALF)
    loads = []

    def load(src, dst):
        copy = pltpu.make_async_copy(src, dst, load_sem.at[len(loads)])
        copy.start()
        loads.append(copy)

    load(w_out_hbm.at[:, :, :, :, other_cols], big.at[pl.ds(2, 2)])
    load(w_out_hbm.at[:, :, :, :, own_cols], big.at[pl.ds(0, 2)])
    barrier = pltpu.get_barrier_semaphore()
    for axis in range(3):
        for step in (1, -1, 2):
            pl.semaphore_signal(
                barrier, inc=1, device_id=link.neighbour(axis, step), device_id_type=MESH_IDS
            )
    pl.semaphore_signal(barrier, inc=1, device_id=partner, device_id_type=MESH_IDS)

    for pair in range(2):
        rows = heads_ref[:, pl.ds(pair * 16, 16), :].reshape(512, LAT)
        for one in range(2):
            head = 2 * pair + one
            value = jnp.dot(rows, w_uv_ref[head], preferred_element_type=f32)
            value = value.reshape(32, 2, 8, 128)[:, one].reshape(256, 128)
            flat[:, pl.ds(head * 128, 128)] = value.astype(bf16)

    def project(slot, start):
        lanes = pl.ds(start, 896)
        weight = big[pl.ds(2 * slot, 2), :, :, :, lanes].reshape(512, 896)
        value = jnp.dot(flat[...], weight, preferred_element_type=f32)
        return value.reshape(4, 4, 16, 896)

    def project_away(start, width):
        @pl.loop(0, width // 896)
        def _(j):
            at = pl.multiple_of(start + j * 896, 128)
            part_send[:, :, :, pl.ds(at, 896)] = project(1, at).astype(bf16)

    def swap_sums(start, width):
        lanes = pl.ds(start, width)
        dst = part_land.at[:, :, :, lanes]
        return link.send(part_send.at[:, :, :, lanes], dst, partner, dst)

    loads[0].wait()
    project_away(*GENERATIONS[0])
    pl.semaphore_wait(barrier, 10)

    def token_rows(cols):
        return jnp.concatenate([resid_ref[s, :, cols].astype(f32) for s in range(2)], axis=0)

    resid_out[...] = token_rows(other_cols)
    names = jnp.concatenate([routes_ref[s] for s in range(2)], axis=0)
    expert = lax.broadcasted_iota(jnp.int32, (8, 128), 1)
    mask = jnp.zeros((8, 128), f32)
    for k in range(routes_ref.shape[2]):
        mask = jnp.where(expert == names[:, k : k + 1], 1.0, mask)
    mask_out[...] = mask
    sent = []
    swaps = [
        link.send(resid_out, hid.at[core], partner, hid.at[other]),
        link.send(mask_out, picked.at[core], partner, picked.at[other]),
    ]
    sent += swaps

    core_swap = [swap_sums(*GENERATIONS[0])]
    project_away(*GENERATIONS[1])
    core_swap.append(swap_sums(*GENERATIONS[1]))
    sent += core_swap
    loads[1].wait()
    for slot, cols in ((0, own_cols), (1, other_cols)):
        load(w_gate_hbm.at[cols], wg.at[slot])
        load(w_up_hbm.at[cols], wu.at[slot])
        load(w_down_hbm.at[:, cols], wd.at[slot])

    hid[core] = token_rows(own_cols)
    picked[core] = mask_out[...]
    wait_in(swaps)

    def add_hidden(start, width, total):
        lanes = pl.ds(start, width)
        hid[:, :, lanes] = hid[:, :, lanes] + total.reshape(2, 8, width)

    plane_land = ((plane_a0, plane_b0, plane_c0), (plane_a1, plane_b1, plane_c1))
    threads = []
    for turn, (start, width) in enumerate(GENERATIONS):
        wait_in(core_swap[turn : turn + 1])

        @pl.loop(0, width // 896)
        def _(j, start=start):
            at = pl.multiple_of(start + j * 896, 128)
            value = project(0, at) + part_land[:, :, :, pl.ds(at, 896)].astype(f32)
            part_sum[:, :, :, pl.ds(at, 896)] = value.astype(bf16)

        for index in (2 * turn, 2 * turn + 1):
            threads.append(
                scatter_part(
                    link, PLANE_PARTS, index, (1, 2), part_sum, plane_land, add_hidden, sent
                )
            )
            next(threads[-1])
    for _ in range(3):
        resume(threads)

    hidden = hid[...].reshape(16, HALF)
    gain = gain_ref[core]
    logits = lax.dot_general(
        (hidden * gain).astype(bf16),
        router_ref[:, own_cols],
        (((1,), (1,)), ((), ())),
        preferred_element_type=f32,
    )
    logits = jnp.concatenate([logits, jnp.zeros((16, 96), f32)], axis=1)
    squares = jnp.sum(hidden * hidden, axis=1, keepdims=True)
    lane = lax.broadcasted_iota(jnp.int32, (16, 128), 1)
    mine = jnp.where(lane < 64, logits, jnp.broadcast_to(squares, (16, 128)))
    stat_out[...] = mine
    stat = link.send(stat_out, stat_in, partner, stat_in)
    sent.append(stat)
    wait_in([stat])
    both = mine + stat_in[...]
    scale = lax.rsqrt(both[:, 64:65] / (2 * HALF) + norm_eps)
    affinity = jax.nn.sigmoid(both * scale) * picked[...].reshape(16, 128)
    weights = route_scale * affinity / jnp.sum(affinity, axis=1, keepdims=True)
    high = weights.astype(bf16)
    low = (weights - high.astype(f32)).astype(bf16).astype(f32)
    table = high.astype(f32) + pltpu.roll(low, 32, axis=1)
    normed = (hid[...].reshape(16, HALF) * scale * gain).astype(bf16)
    held[link.z, link.y, link.x, :, pl.ds(0, HALF)] = normed
    held[link.z, link.y, link.x, :, pl.ds(HALF, 128)] = table.astype(bf16)

    gathers, pushes = [], []
    threads = [gather_part(link, held, pushed, i, gathers, pushes) for i in range(6)]
    for _ in range(5):
        resume(threads)
    resume(threads[:3])
    for copy in loads[2:]:
        copy.wait()

    def own_first(i, carry):
        rows = held[pl.ds(4 * i, 4), :, :, :, pl.ds(0, AG_SPLIT)].reshape(1024, AG_SPLIT)
        cut = pl.ds(0, AG_SPLIT)
        gate_acc[i] = jnp.dot(rows, wg[0, cut], preferred_element_type=f32)
        up_acc[i] = jnp.dot(rows, wu[0, cut], preferred_element_type=f32)
        return carry

    lax.fori_loop(0, 1, own_first, 0)
    resume(threads[3:])

    def own_half(i, carry):
        cut = pl.ds(AG_SPLIT, HALF - AG_SPLIT)
        rows = held[pl.ds(4 * i, 4), :, :, :, cut].reshape(1024, HALF - AG_SPLIT)
        gate_acc[i] += jnp.dot(rows, wg[0, cut], preferred_element_type=f32)
        up_acc[i] += jnp.dot(rows, wu[0, cut], preferred_element_type=f32)
        return carry

    lax.fori_loop(0, 1, own_half, 0)
    wait_in(pushes)

    def other_half(i, carry):
        rows = pushed[pl.ds(4 * i, 4), :, :, :, pl.ds(0, HALF)].reshape(1024, HALF)
        gate_part = gate_acc[i] + jnp.dot(rows, wg[1], preferred_element_type=f32)
        up_part = up_acc[i] + jnp.dot(rows, wu[1], preferred_element_type=f32)
        table = held[pl.ds(4 * i, 4), :, :, :, pl.ds(HALF, 128)].reshape(1024, 128).astype(f32)
        lane = lax.broadcasted_iota(jnp.int32, (1024, 128), 1)
        here = (lane == link.ep) | (lane == link.ep + 32)
        factor = jnp.sum(jnp.where(here, table, 0.0), axis=1, keepdims=True)
        value = (jax.nn.silu(gate_part) * up_part * factor).astype(bf16)
        units[pl.ds(4 * i, 4)] = value.reshape(4, 256, 256)
        return carry

    lax.fori_loop(0, 1, other_half, 0)
    wait_out(gathers + pushes)

    def routed_chunk(slot, i, at):
        weight = wd[slot, :, pl.ds(at, 896)]
        value = jnp.dot(units[i], weight, preferred_element_type=f32)
        return value.reshape(4, 4, 16, 896)

    chunks = [range(start, start + width, 896) for start, width in GENERATIONS]
    back_first = link.take(8)

    def back(turn, i, start):
        lanes = pl.ds(*GENERATIONS[turn])
        dst = big.at[i, :, :, :, lanes]
        k = back_first + 4 * turn + i
        return link.send(pushed.at[i, :, :, :, lanes], dst, partner, dst, k, start)

    for turn in range(2):

        @pl.loop(0, 4)
        def _(i, turn=turn):
            for at in chunks[turn]:
                pushed[i, :, :, :, pl.ds(at, 896)] = routed_chunk(1, i, at).astype(bf16)
            back(turn, i, True)

    def add_routed(start, width, total):
        lanes = pl.ds(start, width)
        fin[:, :, lanes] = hid[:, :, lanes] + total.reshape(2, 8, width)

    torus_land = ((far0, low0, high0), (far1, low1, high1), (far2, low2, high2))
    threads = []
    for turn in range(2):

        @pl.loop(0, 4)
        def _(i, turn=turn):
            wait_in([back(turn, i, False)])
            for at in chunks[turn]:
                value = routed_chunk(0, i, at) + big[i, :, :, :, pl.ds(at, 896)].astype(f32)
                held[i, :, :, :, pl.ds(at, 896)] = value.astype(bf16)

        for index in range(3 * turn, 3 * turn + 3):
            threads.append(
                scatter_part(
                    link, RS_PARTS, index, (0, 1, 2), held, torus_land, add_routed, sent
                )
            )
            next(threads[-1])
    for _ in range(5):
        resume(threads)
    swap = link.send(fin.at[other], fin_in, partner, fin_in)
    sent.append(swap)
    for s in range(2):
        out_ref[s, :, own_cols] = fin[core, pl.ds(4 * s, 4)]
    wait_in([swap])
    for s in range(2):
        out_ref[s, :, other_cols] = fin_in[pl.ds(4 * s, 4)]
    wait_out(sent)
    for turn in range(2):

        @pl.loop(0, 4)
        def _(i, turn=turn):
            wait_out([back(turn, i, False)])


def layer_call(head_rows, w_uv, resid, routes, gain, router, w_out, w_gate, w_up, w_down):
    vmem, hbm = pl.BlockSpec(memory_space=pltpu.VMEM), pl.BlockSpec(memory_space=pl.ANY)
    bf16, f32 = jnp.bfloat16, jnp.float32

    def block(*lead, lanes=HALF, kind=bf16):
        return pltpu.VMEM(lead + (lanes,), kind)

    plane = [block(4, 16), block(16)] * 3
    torus = [block(4, 4, 16)] * 3 + [block(4, 16)] * 3 + [block(16)] * 3
    scratch = (
        [block(4, 4, 4, 16)]
        + [pltpu.VMEM((2, HALF, 256), bf16)] * 2
        + [pltpu.VMEM((2, 256, HALF), bf16), pltpu.VMEM((256, 512), bf16)]
        + [block(4, 4, 16)] * 3
        + plane
        + [pltpu.VMEM((8, 128), f32), block(8, kind=f32), block(2, 8, kind=f32), pltpu.VMEM((2, 8, 128), f32)]
        + [pltpu.VMEM((16, 128), f32)] * 2
        + [block(4, 4, 4, 16, lanes=GW)] * 2
        + [pltpu.VMEM((1, 1024, 256), f32)] * 2
        + [pltpu.VMEM((4, 256, 256), bf16)]
        + torus
        + [block(2, 8, kind=f32), block(8, kind=f32)]
        + [pltpu.SemaphoreType.DMA((COPIES,))] * 2
        + [pltpu.SemaphoreType.DMA((8,))]
    )
    return pl.pallas_call(
        layer_kernel,
        out_shape=jax.ShapeDtypeStruct((2, 4, 2 * HALF), f32),
        in_specs=[vmem] * 6 + [hbm] * 4,
        out_specs=vmem,
        scratch_shapes=scratch,
        compiler_params=pltpu.CompilerParams(
            collective_id=1, has_side_effects=True, vmem_limit_bytes=62 * 1024 * 1024
        ),
        cost_estimate=pl.CostEstimate(
            flops=20_000_000_000, bytes_accessed=22_000_000, transcendentals=300_000
        ),
        name="layer",
    )(head_rows, w_uv, resid, routes, gain, router, w_out, w_gate, w_up, w_down)


def layer_operands(resid, routes, w_out, norm_gain, router_w, w_gate, w_up, w_down):
    gain = norm_gain.astype(jnp.float32).reshape(2, 1, HALF)
    return (
        resid,
        routes,
        gain,
        router_w.T,
        w_out.reshape(2, 4, 4, 16, 2 * HALF),
        w_gate[0],
        w_up[0],
        w_down[0],
    )


CHUNKS = 8
PAIR = 2 * LATW
WIDE = 640
QUARTER = 9216
SPREAD = (2, 1, 3)
AHEAD = 4


def attend_kernel(
    length_ref,
    pages_hbm,
    perm_ref,
    query_hbm,
    fresh_ref,
    heads_ref,
    query_ref,
    query_sem,
    fresh_rows,
    raw,
    rows_raw,
    packed,
    pages,
    rows32,
    query_even,
    query_odd,
    keys,
    acc_even,
    acc_odd,
    row_max,
    row_sum,
    out32,
    out16,
    raw_sem,
    own_sem,
    link_send,
    link_recv,
    head_send,
    head_recv,
):
    f32, bf16 = jnp.float32, jnp.bfloat16
    z, ep = lax.axis_index("ctx"), lax.axis_index("ep")

    def lanes(j):
        return pl.ds(pl.multiple_of(j * PAIR, 128), PAIR)

    def ring(step):
        return lax.rem(z + step, 4)

    def copy(kind, j, src, dst, device):
        return pltpu.make_async_remote_copy(
            src_ref=src,
            dst_ref=dst,
            send_sem=link_send.at[kind, j],
            recv_sem=link_recv.at[kind, j],
            device_id=device,
            device_id_type=MESH_IDS,
        )

    def outgoing(kind, j):
        owner = ring(SPREAD[kind])
        return copy(
            kind, j, packed.at[owner, :, lanes(j)], pages.at[z, :, lanes(j)], (owner, ep)
        )

    def arrived(kind, j):
        producer = ring(4 - SPREAD[kind])
        place = pages.at[producer, :, lanes(j)]
        copy(kind, j, place, place, (producer, ep)).wait_recv()

    def own(j):
        return pltpu.make_async_copy(
            packed.at[z, :, lanes(j)], pages.at[z, :, lanes(j)], own_sem.at[j]
        )

    def fetch(j, quarter):
        span = pl.ds(pl.multiple_of(quarter * QUARTER + j * PAIR, 128), PAIR)
        return pltpu.make_async_copy(
            pages_hbm.at[:, :, span], raw.at[:, :, span], raw_sem.at[j, quarter]
        )

    @pl.loop(0, CHUNKS)
    def _(j):
        for quarter in range(4):
            fetch(j, quarter).start()

    barrier = pltpu.get_barrier_semaphore()
    for step in SPREAD:
        pl.semaphore_signal(barrier, inc=1, device_id=(ring(step), ep), device_id_type=MESH_IDS)

    @pl.loop(1, 32)
    def _(d):
        device = (z, lax.rem(ep + d, 32))
        pl.semaphore_signal(barrier, inc=1, device_id=device, device_id_type=MESH_IDS)


    def repack(j):
        for quarter in range(4):
            fetch(j, quarter).wait()
        for quarter in range(4):
            span = pl.ds(pl.multiple_of(quarter * QUARTER + j * PAIR, 128), PAIR)

            @pl.loop(0, 5)
            def _(group, quarter=quarter, span=span):
                for two in range(2):
                    slot = group * 4 + two * 2
                    both = jnp.concatenate(
                        [raw[slot, :, span].astype(f32), raw[slot + 1, :, span].astype(f32)], axis=0
                    )
                    place = pl.ds(pl.multiple_of((group * 4 + quarter) * 16 + two * 8, 8), 8)
                    for k in range(PAIR // 128):
                        rows_raw[k, place, :] = both[:, k * 128 : k * 128 + 128]

        for owner in range(4):
            for k in range(PAIR // 128):
                column = pl.ds(pl.multiple_of(j * PAIR + k * 128, 128), 128)
                packed[owner, :, column] = rows_raw[k, pl.ds(owner, 80, stride=4), :].astype(bf16)

    query_load = pltpu.make_async_copy(query_hbm, query_ref, query_sem)
    query_load.start()
    repack(0)
    pl.semaphore_wait(barrier, 34)

    @pl.loop(0, CHUNKS)
    def _(j):
        @pl.when(j < AHEAD)
        def _():
            for kind in range(3):
                outgoing(kind, j).start()

        own(j).start()

        @pl.when(j + 1 < CHUNKS)
        def _():
            repack(j + 1)

    query_load.wait()

    @pl.loop(0, 64)
    def _(pair):
        span = pl.ds(pl.multiple_of(pair * PAIR, 128), PAIR)
        both = [query_ref[s, :, span].astype(f32) for s in range(2)]
        both = jnp.concatenate(both, axis=0)
        for k in range(PAIR // 128):
            rows32[k, pl.ds(pl.multiple_of(pair * 8, 8), 8), :] = both[:, k * 128 : k * 128 + 128]

    lane = lax.broadcasted_iota(jnp.int32, (64, WIDE), 1)
    for q in range(4):
        for s in range(2):
            rows = jnp.concatenate(
                [rows32[k, pl.ds(s * 4 + q, 64, stride=8), :] for k in range(PAIR // 128)], axis=1
            )
            even = jnp.where(lane < LATW, rows[:, :WIDE], 0.0)
            odd = jnp.where(lane >= 64, rows[:, PAIR - WIDE :], 0.0)
            for parity, value, shift in ((0, even, 64), (1, odd, WIDE - 64)):
                place = pl.ds(s * 128 + parity * 64, 64)
                moved = pltpu.roll(value, shift, axis=1).astype(bf16)
                value = value.astype(bf16)
                query_even[q, place, :] = value if parity == 0 else moved
                query_odd[q, place, :] = moved if parity == 0 else value

    scale = (NOPE + ROPE) ** (-0.5)
    contract = (((1,), (1,)), ((), ()))

    drawn = [fresh_ref[j].astype(f32) for j in range(2)]
    for q in range(4):
        rows = jnp.concatenate([one[q : q + 1] for one in drawn] + [jnp.zeros((6, LATW), f32)], 0)
        rows = jnp.concatenate([rows, jnp.zeros((8, WIDE - LATW), f32)], axis=1)
        rows = jnp.concatenate([rows, jnp.zeros((120, WIDE), f32)], axis=0)
        fresh_rows[q] = rows.astype(bf16)

    @pl.loop(0, 4)
    def _(q):
        fresh = fresh_rows[q]
        score = (
            lax.dot_general(query_even[q], fresh, contract, preferred_element_type=f32) * scale
        )
        token = lax.broadcasted_iota(jnp.int32, (256, 128), 1)
        step = lax.broadcasted_iota(jnp.int32, (256, 128), 0) // 128
        score = jnp.where(token <= step, score, masked_score)
        top = jnp.max(score, axis=1, keepdims=True)
        weight = jnp.exp(score - top)
        row_max[q] = jnp.broadcast_to(top, (256, 128))
        row_sum[q] = jnp.broadcast_to(jnp.sum(weight, axis=1, keepdims=True), (256, 128))
        acc_even[q] = jnp.dot(weight.astype(bf16), fresh[:, :LAT], preferred_element_type=f32)
        acc_odd[q] = jnp.zeros((256, WIDE), f32)

    @pl.loop(0, CHUNKS)
    def _(j):
        @pl.when(j + AHEAD < CHUNKS)
        def _():
            for kind in range(3):
                outgoing(kind, j + AHEAD).start()

        own(j).wait()
        for kind in range(3):
            arrived(kind, j)

        found = [
            jnp.dot(perm_ref[c], pages[c, :, lanes(j)], preferred_element_type=f32)
            for c in range(4)
        ]
        for quarter in range(4):
            for q in range(4):
                at = quarter * 32 + q * 8
                rows = jnp.concatenate([one[at : at + 8] for one in found], axis=0)
                keys[q, pl.ds(quarter * 32, 32), :] = rows.astype(bf16)

        @pl.loop(0, 4)
        def _(q):
            key = keys[q]
            low, high = key[:, :WIDE], key[:, PAIR - WIDE :]
            score = jnp.concatenate(
                [
                    lax.dot_general(query_even[q], low, contract, preferred_element_type=f32),
                    lax.dot_general(query_odd[q], high, contract, preferred_element_type=f32),
                ],
                axis=1,
            )
            n = lax.broadcasted_iota(jnp.int32, (1, 256), 1)
            fifth = n % 8
            page = 4 * fifth + (n % 32) // 8
            position = page * 64 + 2 * (8 * ((n % 128) // 32) + j) + n // 128
            live = (fifth < 5) & (position < length_ref[q])
            score = jnp.where(live, score * scale, masked_score)
            before = row_max[q]
            top = jnp.maximum(before, jnp.max(score, axis=1, keepdims=True))
            shrink = jnp.exp(before - top)
            weight = jnp.exp(score - jnp.concatenate([top, top], axis=1))
            row_max[q] = top
            row_sum[q] = row_sum[q] * shrink + jnp.sum(weight, axis=1, keepdims=True)
            weight = weight.astype(bf16)
            acc_even[q] = acc_even[q] * shrink[:, :1] + jnp.dot(
                weight[:, :128], low[:, :LAT], preferred_element_type=f32
            )
            acc_odd[q] = acc_odd[q] * shrink[:, :1] + jnp.dot(
                weight[:, 128:], high, preferred_element_type=f32
            )

    for q in range(4):
        value = (acc_even[q] + acc_odd[q][:, 64 : 64 + LAT]) / row_sum[q][:, :1]
        for block in range(4):
            s, parity = block // 2, block % 2
            for k in range(LAT // 128):
                out32[k, pl.ds(parity * 8 + s * 4 + q, 64, stride=16), :] = value[
                    block * 64 : block * 64 + 64, k * 128 : k * 128 + 128
                ]

    def rounded(e):
        rows = pl.ds(pl.multiple_of(e * 32, 32), 32)
        parts = [out32[k, rows, :] for k in range(LAT // 128)]
        return jnp.concatenate(parts, axis=1).astype(bf16)

    def head_copy(d, src, dst, device):
        return pltpu.make_async_remote_copy(
            src_ref=src,
            dst_ref=dst,
            send_sem=head_send.at[d],
            recv_sem=head_recv.at[d],
            device_id=device,
            device_id_type=MESH_IDS,
        )

    def head_block(d):
        target = lax.rem(ep + d, 32)
        return head_copy(d, out16.at[target], heads_ref.at[ep], (z, target))

    @pl.loop(1, 32)
    def _(d):
        target = lax.rem(ep + d, 32)
        out16[target] = rounded(target)
        head_block(d).start()

    heads_ref[ep] = rounded(ep)

    @pl.loop(1, 32)
    def _(d):
        source = heads_ref.at[lax.rem(ep + 32 - d, 32)]
        head_copy(d, source, source, (z, ep)).wait_recv()

    @pl.loop(1, 32)
    def _(d):
        head_block(d).wait_send()

    @pl.loop(0, CHUNKS)
    def _(j):
        for kind in range(3):
            outgoing(kind, j).wait_send()


def attend_call(prefill_pages, page_map, prompt_len, queries, new_latent):
    bf16, f32 = jnp.bfloat16, jnp.float32
    slots, width = prefill_pages.shape[3:]
    row = jnp.arange(32)
    request, fifth = row // 8, row % 8
    wanted = request[None, :] * 20 + 4 * fifth[None, :] + jnp.arange(4)[:, None]
    wanted = jnp.where(fifth[None, :] < 5, wanted, -1)
    slot_hit = (page_map.reshape(4, 1, 5, 1, 4) == wanted[:, :, None, None, None]).astype(bf16)
    same = jnp.eye(4, dtype=bf16)[:, None, None, :, None]
    perm = (slot_hit[:, None] * same).reshape(4, 128, 80)
    vmem, hbm = pl.BlockSpec(memory_space=pltpu.VMEM), pl.BlockSpec(memory_space=pl.ANY)
    return pl.pallas_call(
        attend_kernel,
        out_shape=jax.ShapeDtypeStruct((32, 32, LAT), bf16),
        in_specs=[pl.BlockSpec(memory_space=pltpu.SMEM), hbm, vmem, hbm, vmem],
        out_specs=vmem,
        scratch_shapes=[
            pltpu.VMEM(queries.shape, bf16),
            pltpu.SemaphoreType.DMA,
            pltpu.VMEM((4, 128, WIDE), bf16),
            pltpu.VMEM((slots, 4, width), bf16),
            pltpu.VMEM((PAIR // 128, 320, 128), f32),
            pltpu.VMEM((4, 80, QUARTER), bf16),
            pltpu.VMEM((4, 80, QUARTER), bf16),
            pltpu.VMEM((PAIR // 128, 512, 128), f32),
            pltpu.VMEM((4, 256, WIDE), bf16),
            pltpu.VMEM((4, 256, WIDE), bf16),
            pltpu.VMEM((4, 128, PAIR), bf16),
            pltpu.VMEM((4, 256, LAT), f32),
            pltpu.VMEM((4, 256, WIDE), f32),
            pltpu.VMEM((4, 256, 128), f32),
            pltpu.VMEM((4, 256, 128), f32),
            pltpu.VMEM((LAT // 128, 1024, 128), f32),
            pltpu.VMEM((32, 32, LAT), bf16),
            pltpu.SemaphoreType.DMA((CHUNKS, 4)),
            pltpu.SemaphoreType.DMA((CHUNKS,)),
            pltpu.SemaphoreType.DMA((3, CHUNKS)),
            pltpu.SemaphoreType.DMA((3, CHUNKS)),
            pltpu.SemaphoreType.DMA((32,)),
            pltpu.SemaphoreType.DMA((32,)),
        ],
        compiler_params=pltpu.CompilerParams(
            collective_id=2, has_side_effects=True, vmem_limit_bytes=56 * 1024 * 1024
        ),
        cost_estimate=pl.CostEstimate(
            flops=4_000_000_000, bytes_accessed=8_000_000, transcendentals=1_500_000
        ),
        name="attend",
    )(prompt_len, jnp.swapaxes(prefill_pages[0, 0], 0, 1), perm, queries, new_latent)


def per_device(
    prefill_pages,
    page_map,
    prompt_len,
    queries,
    new_latent,
    resid,
    w_uv,
    w_out,
    norm_gain,
    router_w,
    routes,
    w_gate,
    w_up,
    w_down,
):
    head_rows = attend_call(prefill_pages, page_map, prompt_len, queries, new_latent)
    operands = layer_operands(resid, routes, w_out, norm_gain, router_w, w_gate, w_up, w_down)
    return layer_call(head_rows, w_uv, *operands).astype(jnp.bfloat16)


def solution(mesh):
    placed = (
        P("ctx", "ep", None, None, None),
        P("ctx", "ep", None, None),
        P(("ctx", "ep")),
        P(None, ("ctx", "ep"), None),
        P(None, ("ctx", "ep"), None),
        P(None, ("ctx", "ep"), None),
        P("ep", None, None),
        P("ep", None),
        P(),
        P(),
        P(None, ("ctx", "ep"), None),
        P("ep", None, "ctx"),
        P("ep", None, "ctx"),
        P("ep", "ctx", None),
    )
    return jax.shard_map(
        per_device,
        mesh=mesh,
        in_specs=placed,
        out_specs=P(None, ("ctx", "ep"), None),
        check_vma=False,
    )
```
